32 devices in a mesh: groups: 2 (over y), dp: 4 (over z), owner: 4 (over x, core).
Axes of the slice: x: 2, y: 2, z: 4, core: 2. Of those that a mesh axis runs over, the one named last changes fastest.
Arguments:
- activations: bfloat16 [6, 512, 2048], P('groups', 'dp'), parts along dimension 0, may hold values from -40 to 40
- out_grads: bfloat16 [6, 512, 2048], P('groups', 'dp'), parts along dimension 0, may hold values from -1.767767 to 1.767767
- basis_act: bfloat16 [6, 2048, 2048], P('groups', 'dp', 'owner'), parts along dimension 0, may hold values from -0.125 to 0.125
- basis_grad: bfloat16 [6, 2048, 2048], P('groups', 'dp', 'owner'), parts along dimension 0, may hold values from -0.125 to 0.125
- owner_of: int32 [3], replicated, may hold values from 0 to 3, as said below
- counts: int32 [8], P('groups'), parts along dimension 0, may hold values from 1 to 128, 384 in all
- state_act: float32 [8, 4096], P('owner', 'groups'), parts along dimension 1, may hold values from 0.5 to 5
- state_grad: float32 [8, 4096], P('owner', 'groups'), parts along dimension 1, may hold values from 0.0009765625 to 0.009765625
Outputs:
- precond: bfloat16 [6, 2048, 2048], P('groups', 'dp', 'owner'), parts along dimension 0
- new_state_act: float32 [8, 4096], P('owner', 'groups'), parts along dimension 1
- new_state_grad: float32 [8, 4096], P('owner', 'groups'), parts along dimension 1
The draws below stay inside these ranges and needn't reach their ends.
There are 2 independent parts, one for each index of `groups`. The reference program is written for one: setup_inputs(seed, part) draws one part's arguments, and reference() takes and returns one part's arrays. A program takes and returns all parts, laid end to end along the dimension named above; an argument that names none is the same for every part. Nothing has to cross between parts.
Inputs may be any that keep to these rules, and one draw needn't show every extreme that they name: `owner_of`: each owner index holds at most 2 of the 3 layers, and some owner index holds exactly 2. `counts`: at least one batch shard is full.
All inputs are finite; a program needn't handle non-finite values.
Results may differ from the reference program's by a relative error of at most 0.012.
Values may be sent and summed in bfloat16 or wider, within the bound.
No kernel may reach another device: no remote copies, remote signals or barrier semaphores. Data moves between devices by JAX's collectives and lax.ppermute only.
A program may use at most 64 MiB of HBM per device.

```python
import math
import jax
import jax.numpy as jnp
import numpy as np
from jax import lax

D = 2048
TOK_DEV = 128
LAYERS = 3
SLOTS = 2
TOKENS = 512
N_DP = 4
N_OWNER = 4


def shard_ramp(rows_total, rows_shard):
    shard_index = (jnp.arange(rows_total) // rows_shard).astype(jnp.float32)
    shard_total = rows_total // rows_shard
    return 3.0 ** (0.5 * shard_index / max(shard_total - 1, 1) - 0.25)


def scaled_rows(noise, key_rows, factor):
    row_scale = 10.0 ** (jax.random.uniform(key_rows, (LAYERS, TOKENS, 1), jnp.float32) - 0.5)
    return (factor * noise * row_scale * shard_ramp(TOKENS, TOK_DEV)[None, :, None]).astype(jnp.bfloat16)


def draw_activations(key, part):
    key = jax.random.fold_in(key, 11)
    key_noise, key_rows = jax.random.split(key, 2)
    shape_full = (LAYERS, TOKENS, D)
    noise = jnp.clip(jax.random.normal(key_noise, shape_full, jnp.float32), -6.0, 6.0)
    return scaled_rows(noise, key_rows, 1.0)


def draw_out_grads(key, part):
    key = jax.random.fold_in(key, 12)
    key_noise, key_rows = jax.random.split(key, 2)
    shape_full = (LAYERS, TOKENS, D)
    noise = jnp.clip(jax.random.normal(key_noise, shape_full, jnp.float32), -6.0, 6.0)
    return scaled_rows(noise, key_rows, TOKENS ** (-0.5))


def draw_owner_of(key, part):
    key = jax.random.fold_in(key, 13)
    key_owner, key_layer, key_offset = jax.random.split(key, 3)
    ends = jnp.array([N_OWNER - 1, 0], jnp.int32)
    if N_OWNER > 2:
        middle = 1 + jax.random.permutation(key_owner, N_OWNER - 2).astype(jnp.int32)
        owner_order = jnp.concatenate([ends, middle])
    else:
        owner_order = ends
    layer_order = jax.random.permutation(key_layer, LAYERS)
    offset_bit = jax.random.randint(key_offset, (), 0, 2)
    group_index = (jnp.arange(LAYERS) + offset_bit) // 2
    owners_placed = owner_order[group_index].astype(jnp.int32)
    return jnp.zeros((LAYERS,), jnp.int32).at[layer_order].set(owners_placed)


def level_of(rng, shape, cuts, low, top_value):
    def one(dim, shards_of):
        heights = jax.random.uniform(jax.random.fold_in(jax.random.fold_in(rng, 6), dim), (shards_of,), jnp.float32, low / len(cuts), top_value / len(cuts))
        return jnp.repeat(jnp.exp(heights), shape[dim] // shards_of).reshape((-1,) + (1,) * (len(shape) - dim - 1))

    level = one(*cuts[0])
    for cut in cuts[1:]:
        level = level * one(*cut)
    return level


def length_profile(amount, total, most, lean):
    weights = [(1 << 20) // math.isqrt(grade ** lean) + 1 for grade in range(2, amount + 1)]
    surplus, given = total - most - (amount - 1), [1] * (amount - 1)
    while surplus > 0:
        candidates = [i for i in range(amount - 1) if given[i] < most]
        mass, left = sum([weights[i] for i in candidates]), surplus
        for i in candidates:
            addition = min(most - given[i], max(1, left * weights[i] // mass), surplus)
            given[i] = given[i] + addition
            surplus = surplus - addition
    return np.array([most] + given)


def uneven_parts(key, number_of, total, most, skew):
    if number_of == 2:
        one = jax.random.randint(key, (), max(1, total - most), min(most, total - 1) + 1)
        return jnp.stack([one, total - one])
    lengths = jnp.asarray(length_profile(number_of, total, most, skew), jnp.int32)
    couples = (number_of - 1) // 2
    source_of, taker = lengths[1:1 + 2 * couples:2], lengths[2:2 + 2 * couples:2]
    room = jnp.minimum(source_of - 1, most - taker)
    moved = jax.random.randint(jax.random.fold_in(key, 1), (couples,), 0, 1 << 20) % (room + 1)
    lengths = lengths.at[1:1 + 2 * couples:2].set(source_of - moved).at[2:2 + 2 * couples:2].set(taker + moved)
    return lengths[jax.random.permutation(jax.random.fold_in(key, 2), number_of)]


def scatter_about(key, dims, spread, most, cuts=(), kind=jnp.bfloat16):
    entries = spread * jax.random.normal(key, dims, jnp.float32)
    if cuts:
        entries = entries * level_of(key, dims, cuts, -0.22, 0.18)
    return jnp.clip(entries, -most, most).astype(kind)


def setup_inputs(seed: int = 0, part: int = 0) -> dict:
    arg_keys = jax.random.split(jax.random.key(seed), 9)
    own_keys = jax.random.split(jax.random.fold_in(arg_keys[8], part), 9)
    activations = draw_activations(jax.random.fold_in(jax.random.fold_in(arg_keys[8], part), 71), part)
    out_grads = draw_out_grads(jax.random.fold_in(jax.random.fold_in(arg_keys[8], part), 71), part)
    basis_act = scatter_about(own_keys[2], (LAYERS, D, D), D ** -0.5, 0.125, ((1, 4), (2, 4)))
    basis_grad = scatter_about(own_keys[3], (LAYERS, D, D), D ** -0.5, 0.125, ((1, 4), (2, 4)))
    owner_of = draw_owner_of(jax.random.fold_in(arg_keys[8], 71), part)
    counts = uneven_parts(own_keys[5], N_DP, N_DP * TOK_DEV * 3 // 4, TOK_DEV, 2).astype(jnp.int32)
    state_act = jnp.clip(jnp.exp(math.log(5.0) - 2.3025851 * jax.random.uniform(own_keys[6], (N_OWNER * SLOTS, D), jnp.float32) ** level_of(own_keys[6], (N_OWNER * SLOTS, D), ((0, 4),), -0.2, 0.2)), 0.5, 5.0)
    state_grad = jnp.clip(jnp.exp(math.log(0.009765625) - 2.3025851 * jax.random.uniform(own_keys[7], (N_OWNER * SLOTS, D), jnp.float32) ** level_of(own_keys[7], (N_OWNER * SLOTS, D), ((0, 4),), -0.2, 0.2)), 0.0009765625, 0.009765625)
    return {"activations": activations, "out_grads": out_grads, "basis_act": basis_act, "basis_grad": basis_grad, "owner_of": owner_of, "counts": counts, "state_act": state_act, "state_grad": state_grad}


decay_rate = 0.25
damping_rate = 0.1


def shard_gram(proj_act, proj_grad, shard_count):
    shard_rows = proj_act.shape[0] // shard_count
    act_shards = proj_act.reshape(shard_count, shard_rows, proj_act.shape[1])
    grad_shards = proj_grad.reshape(shard_count, shard_rows, proj_grad.shape[1])

    def accumulate(running, shard_pair):
        partial_value = jnp.dot(shard_pair[1].T, shard_pair[0], preferred_element_type=jnp.float32)
        rounded = lax.optimization_barrier(partial_value.astype(jnp.bfloat16))
        return running + rounded.astype(jnp.float32), None

    start_value = jnp.zeros((proj_grad.shape[1], proj_act.shape[1]), jnp.float32)
    running, unused_out = lax.scan(accumulate, start_value, (act_shards, grad_shards))
    return running


def reference(activations, out_grads, basis_act, basis_grad, owner_of, counts, state_act, state_grad):
    tokens_all = activations.shape[1]
    shard_count = counts.shape[0]
    shard_rows = tokens_all // shard_count
    position = jnp.arange(tokens_all)
    shard_of = position // shard_rows
    valid_rows = ((position % shard_rows) < counts[shard_of]).astype(jnp.float32)[:, None]
    valid_total = jnp.sum(counts).astype(jnp.float32)
    new_act = state_act
    new_grad = state_grad
    results = []
    for layer_index in range(LAYERS):
        proj_act = (jnp.dot(activations[layer_index], basis_act[layer_index], preferred_element_type=jnp.float32) * valid_rows).astype(jnp.bfloat16)
        proj_grad = (jnp.dot(out_grads[layer_index], basis_grad[layer_index], preferred_element_type=jnp.float32) * valid_rows).astype(jnp.bfloat16)
        moment_act = jnp.sum(jnp.square(proj_act.astype(jnp.float32)), axis=0) / valid_total
        moment_grad = jnp.sum(jnp.square(proj_grad.astype(jnp.float32)), axis=0) / valid_total
        owner_now = owner_of[layer_index]
        slot_rank = jnp.sum((owner_of[:layer_index] == owner_now).astype(jnp.int32))
        slot_index = (owner_now * SLOTS + slot_rank).astype(jnp.int32)
        eigen_act = decay_rate * state_act[slot_index] + (1.0 - decay_rate) * moment_act
        eigen_grad = decay_rate * state_grad[slot_index] + (1.0 - decay_rate) * moment_grad
        new_act = new_act.at[slot_index].set(eigen_act)
        new_grad = new_grad.at[slot_index].set(eigen_grad)
        gram_tile = shard_gram(proj_act, proj_grad, shard_count) / valid_total
        damping = damping_rate * jnp.mean(eigen_grad) * jnp.mean(eigen_act)
        scaled = gram_tile / (eigen_grad[:, None] * eigen_act[None, :] + damping)
        results.append(scaled.astype(jnp.bfloat16))
    return jnp.stack(results), new_act, new_grad
```

```python
import jax
import jax.numpy as jnp
from jax import lax
from jax.sharding import PartitionSpec as P

decay_rate = 0.25
damping_rate = 0.1


def spread(array, axis, root):
    mine = lax.axis_index(axis) == root
    return lax.psum(jnp.where(mine, array, jnp.zeros_like(array)), axis)


def gather_plan(activations, out_grads, basis_act, basis_grad, owner_of, counts, state_act, state_grad):
    layers = activations.shape[0]
    tok_rows = activations.shape[1]
    tile_rows = basis_act.shape[1]
    tile_cols = basis_act.shape[2]
    slot_count = state_act.shape[0]
    dp_index = lax.axis_index("dp")
    own_index = lax.axis_index("owner")
    valid_rows = (jnp.arange(tok_rows) < counts[dp_index]).astype(jnp.float32)[:, None]
    valid_total = jnp.sum(counts).astype(jnp.float32)
    square_acts = []
    square_grads = []
    gram_tiles = []
    for layer_index in range(layers):
        panel_act = jnp.dot(
            activations[layer_index],
            lax.all_gather(basis_act[layer_index], "dp", axis=0, tiled=True),
            preferred_element_type=jnp.float32,
        )
        panel_grad = jnp.dot(
            out_grads[layer_index],
            lax.all_gather(basis_grad[layer_index], "dp", axis=0, tiled=True),
            preferred_element_type=jnp.float32,
        )
        panel_act = (panel_act * valid_rows).astype(jnp.bfloat16)
        panel_grad = (panel_grad * valid_rows).astype(jnp.bfloat16)
        full_act = lax.all_gather(panel_act, "owner", axis=1, tiled=True)
        full_grad = lax.all_gather(panel_grad, "owner", axis=1, tiled=True)
        square_act = jnp.sum(jnp.square(full_act.astype(jnp.float32)), axis=0)
        square_grad = jnp.sum(jnp.square(full_grad.astype(jnp.float32)), axis=0)
        gram_term = lax.dot_general(
            full_grad, panel_act, (((0,), (0,)), ((), ())), preferred_element_type=jnp.float32
        )
        gram_tiles.append(
            lax.psum_scatter(
                gram_term.astype(jnp.bfloat16), "dp", scatter_dimension=0, tiled=True
            ).astype(jnp.float32)
            / valid_total
        )
        square_act, square_grad = lax.psum((square_act, square_grad), "dp")
        square_acts.append(square_act)
        square_grads.append(square_grad)
    new_act = state_act
    new_grad = state_grad
    results = []
    for layer_index in range(layers):
        owner_now = owner_of[layer_index]
        slot_rank = jnp.sum((owner_of[:layer_index] == owner_now).astype(jnp.int32))
        selector = (jnp.arange(slot_count) == slot_rank).astype(jnp.float32)[:, None]
        local_act = decay_rate * jnp.sum(state_act * selector, axis=0) + (
            1.0 - decay_rate
        ) * (square_acts[layer_index] / valid_total)
        local_grad = decay_rate * jnp.sum(state_grad * selector, axis=0) + (
            1.0 - decay_rate
        ) * (square_grads[layer_index] / valid_total)
        eigen_act = spread(local_act, "owner", owner_now)
        eigen_grad = spread(local_grad, "owner", owner_now)
        replace_rows = ((jnp.arange(slot_count) == slot_rank) & (own_index == owner_now))[:, None]
        new_act = jnp.where(replace_rows, eigen_act[None, :], new_act)
        new_grad = jnp.where(replace_rows, eigen_grad[None, :], new_grad)
        damping = damping_rate * jnp.mean(eigen_grad) * jnp.mean(eigen_act)
        grad_eigen = lax.dynamic_slice_in_dim(eigen_grad, dp_index * tile_rows, tile_rows)
        act_eigen = lax.dynamic_slice_in_dim(eigen_act, own_index * tile_cols, tile_cols)
        scaled = gram_tiles[layer_index] / (grad_eigen[:, None] * act_eigen[None, :] + damping)
        results.append(scaled.astype(jnp.bfloat16))
    return (jnp.stack(results), new_act, new_grad)


def flip(array, axis, mask):
    return lax.ppermute(array, axis, [(i, i ^ mask) for i in range(lax.axis_size(axis))])


def hop(array, pairs):
    owners = lax.axis_size("owner")
    flat = [(a * owners + b, c * owners + e) for (a, b), (c, e) in pairs]
    return lax.ppermute(array, ("dp", "owner"), flat)


def line_plan(activations, out_grads, basis_act, basis_grad, owner_of, counts, state_act, state_grad):
    layers, tok_rows, width = activations.shape
    tile = basis_act.shape[1]
    n_dp = lax.axis_size("dp")
    n_own = lax.axis_size("owner")
    slot_count = state_act.shape[0]
    part_rows = tok_rows // n_own
    packed = 3 * n_dp * tok_rows // 4
    dp = lax.axis_index("dp")
    own = lax.axis_index("owner")
    valid_total = jnp.sum(counts).astype(jnp.float32)
    f32 = jnp.float32
    bf16 = jnp.bfloat16

    starts = jnp.cumsum(counts) - counts
    shard_ids = [jnp.full((tok_rows,), dp)]
    row_ids = [jnp.arange(tok_rows)]
    for peer in (own, own ^ 2, own ^ 1, own ^ 3):
        for mask in range(1, n_dp):
            shard_ids.append(jnp.full((part_rows,), dp ^ mask))
            row_ids.append(peer * part_rows + jnp.arange(part_rows))
    shard_ids = jnp.concatenate(shard_ids)
    row_ids = jnp.concatenate(row_ids)
    place = jnp.where(row_ids < counts[shard_ids], starts[shard_ids] + row_ids, -1)
    select = (jnp.arange(packed)[:, None] == place[None, :]).astype(bf16)

    state = jnp.concatenate([state_act, state_grad], axis=0)
    state = jnp.stack([state, flip(state, "owner", 1)])
    state = jnp.concatenate([state, flip(state, "owner", 2)])

    def rows_of(tokens):
        part = lax.dynamic_slice_in_dim(tokens, own * part_rows, part_rows, 1)
        got = [
            flip(lax.dynamic_slice_in_dim(part, (dp ^ mask) * tile, tile, 2), "dp", mask)
            for mask in range(1, n_dp)
        ]
        got = jnp.concatenate(got, axis=1)
        got = jnp.concatenate([got, flip(got, "owner", 2)], axis=1)
        mine = lax.dynamic_slice_in_dim(tokens, dp * tile, tile, 2)
        return jnp.concatenate([mine, got, flip(got, "owner", 1)], axis=1)

    def project(rows, basis):
        chosen = jnp.dot(select, rows, preferred_element_type=f32).astype(bf16)
        return jnp.dot(chosen, basis, preferred_element_type=f32).astype(bf16)

    def add(*terms):
        return sum(term.astype(f32) for term in terms).astype(bf16)

    rows_act = rows_of(activations)
    rows_grad = rows_of(out_grads)
    inner = (dp == 1) | (dp == 2)
    every = range(n_own)
    proj_act = []
    proj_grad = []
    for layer in range(layers):
        part = project(rows_act[layer], basis_act[layer])
        part = add(part, hop(part, [((a, b), (c, b)) for a, c in ((0, 1), (3, 2)) for b in every]))
        part = add(part, hop(part, [((a, b), (c, b)) for a, c in ((1, 2), (2, 1)) for b in every]))
        outer = hop(part, [((a, b), (c, b)) for a, c in ((1, 0), (2, 3)) for b in every])
        proj_act.append(jnp.where(inner, part, outer))
    for layer in range(layers):
        part = project(rows_grad[layer], basis_grad[layer])
        near = add(part, hop(part, [((0, b), (1, b)) for b in (1, 2, 3)] + [((3, b), (2, b)) for b in (0, 1, 2)]))
        across = hop(near, [((1, b), (2, b)) for b in (2, 3)] + [((2, b), (1, b)) for b in (0, 1)])
        near = add(near, across)
        near = add(near, hop(near, [((1, 0), (0, 0)), ((2, 3), (3, 3))]))
        chip = hop(near, [((a, a), (a, a ^ 2)) for a in range(n_dp)])
        half = jnp.where(own == dp, near, chip)
        core = hop(half, [((a, a ^ b), (a, a ^ b ^ 1)) for a in range(n_dp) for b in (0, 2)])
        proj_grad.append(jnp.where((own == dp) | (own == dp ^ 2), half, core))

    def squares(panels):
        return jnp.stack([jnp.sum(jnp.square(p.astype(f32)), axis=0) for p in panels]) / valid_total

    def gathered(vectors, axis, index):
        pair = jnp.stack([vectors, flip(vectors, axis, 1)])
        four = jnp.concatenate([pair, flip(pair, axis, 2)])
        order = jnp.arange(4) ^ index
        return jnp.concatenate([four[order[i]] for i in range(4)], axis=1)

    moment_act = gathered(squares(proj_act), "owner", own)
    moment_grad = gathered(squares(proj_grad), "dp", dp)

    new_act = state_act
    new_grad = state_grad
    results = []
    for layer in range(layers):
        owner_now = owner_of[layer]
        slot_rank = jnp.sum((owner_of[:layer] == owner_now).astype(jnp.int32))
        rows = state[owner_now ^ own]
        eigen_act = decay_rate * rows[slot_rank] + (1.0 - decay_rate) * moment_act[layer]
        eigen_grad = decay_rate * rows[slot_count + slot_rank] + (1.0 - decay_rate) * moment_grad[layer]
        replace_rows = ((jnp.arange(slot_count) == slot_rank) & (own == owner_now))[:, None]
        new_act = jnp.where(replace_rows, eigen_act[None, :], new_act)
        new_grad = jnp.where(replace_rows, eigen_grad[None, :], new_grad)
        damping = damping_rate * jnp.mean(eigen_grad) * jnp.mean(eigen_act)
        grad_eigen = lax.dynamic_slice_in_dim(eigen_grad, dp * tile, tile)
        act_eigen = lax.dynamic_slice_in_dim(eigen_act, own * tile, tile)
        gram = lax.dot_general(
            proj_grad[layer], proj_act[layer], (((0,), (0,)), ((), ())), preferred_element_type=f32
        )
        scaled = gram / valid_total / (grad_eigen[:, None] * act_eigen[None, :] + damping)
        results.append(scaled.astype(bf16))
    return (jnp.stack(results), new_act, new_grad)


def solution(mesh):
    placed = (
        P("groups", "dp", None),
        P("groups", "dp", None),
        P("groups", "dp", "owner"),
        P("groups", "dp", "owner"),
        P(),
        P("groups"),
        P("owner", "groups"),
        P("owner", "groups"),
    )
    square = mesh.shape["dp"] == 4 and mesh.shape["owner"] == 4
    return jax.shard_map(
        line_plan if square else gather_plan,
        mesh=mesh,
        in_specs=placed,
        out_specs=(P("groups", "dp", "owner"), P("owner", "groups"), P("owner", "groups")),
        check_vma=False,
    )
```

```python
import jax
import jax.numpy as jnp
from jax import lax
from jax.experimental import pallas as pl
from jax.experimental.pallas import tpu as pltpu
from jax.sharding import PartitionSpec as P

decay_rate = 0.25
damping_rate = 0.1


def spread(array, axis, root):
    mine = lax.axis_index(axis) == root
    return lax.psum(jnp.where(mine, array, jnp.zeros_like(array)), axis)


def gather_plan(activations, out_grads, basis_act, basis_grad, owner_of, counts, state_act, state_grad):
    layers = activations.shape[0]
    tok_rows = activations.shape[1]
    tile_rows = basis_act.shape[1]
    tile_cols = basis_act.shape[2]
    slot_count = state_act.shape[0]
    dp_index = lax.axis_index("dp")
    own_index = lax.axis_index("owner")
    valid_rows = (jnp.arange(tok_rows) < counts[dp_index]).astype(jnp.float32)[:, None]
    valid_total = jnp.sum(counts).astype(jnp.float32)
    square_acts = []
    square_grads = []
    gram_tiles = []
    for layer_index in range(layers):
        panel_act = jnp.dot(
            activations[layer_index],
            lax.all_gather(basis_act[layer_index], "dp", axis=0, tiled=True),
            preferred_element_type=jnp.float32,
        )
        panel_grad = jnp.dot(
            out_grads[layer_index],
            lax.all_gather(basis_grad[layer_index], "dp", axis=0, tiled=True),
            preferred_element_type=jnp.float32,
        )
        panel_act = (panel_act * valid_rows).astype(jnp.bfloat16)
        panel_grad = (panel_grad * valid_rows).astype(jnp.bfloat16)
        full_act = lax.all_gather(panel_act, "owner", axis=1, tiled=True)
        full_grad = lax.all_gather(panel_grad, "owner", axis=1, tiled=True)
        square_act = jnp.sum(jnp.square(full_act.astype(jnp.float32)), axis=0)
        square_grad = jnp.sum(jnp.square(full_grad.astype(jnp.float32)), axis=0)
        gram_term = lax.dot_general(
            full_grad, panel_act, (((0,), (0,)), ((), ())), preferred_element_type=jnp.float32
        )
        gram_tiles.append(
            lax.psum_scatter(
                gram_term.astype(jnp.bfloat16), "dp", scatter_dimension=0, tiled=True
            ).astype(jnp.float32)
            / valid_total
        )
        square_act, square_grad = lax.psum((square_act, square_grad), "dp")
        square_acts.append(square_act)
        square_grads.append(square_grad)
    new_act = state_act
    new_grad = state_grad
    results = []
    for layer_index in range(layers):
        owner_now = owner_of[layer_index]
        slot_rank = jnp.sum((owner_of[:layer_index] == owner_now).astype(jnp.int32))
        selector = (jnp.arange(slot_count) == slot_rank).astype(jnp.float32)[:, None]
        local_act = decay_rate * jnp.sum(state_act * selector, axis=0) + (
            1.0 - decay_rate
        ) * (square_acts[layer_index] / valid_total)
        local_grad = decay_rate * jnp.sum(state_grad * selector, axis=0) + (
            1.0 - decay_rate
        ) * (square_grads[layer_index] / valid_total)
        eigen_act = spread(local_act, "owner", owner_now)
        eigen_grad = spread(local_grad, "owner", owner_now)
        replace_rows = ((jnp.arange(slot_count) == slot_rank) & (own_index == owner_now))[:, None]
        new_act = jnp.where(replace_rows, eigen_act[None, :], new_act)
        new_grad = jnp.where(replace_rows, eigen_grad[None, :], new_grad)
        damping = damping_rate * jnp.mean(eigen_grad) * jnp.mean(eigen_act)
        grad_eigen = lax.dynamic_slice_in_dim(eigen_grad, dp_index * tile_rows, tile_rows)
        act_eigen = lax.dynamic_slice_in_dim(eigen_act, own_index * tile_cols, tile_cols)
        scaled = gram_tiles[layer_index] / (grad_eigen[:, None] * act_eigen[None, :] + damping)
        results.append(scaled.astype(jnp.bfloat16))
    return (jnp.stack(results), new_act, new_grad)


def flip(array, axis, mask):
    return lax.ppermute(array, axis, [(i, i ^ mask) for i in range(lax.axis_size(axis))])


def hop(array, pairs):
    owners = lax.axis_size("owner")
    flat = [(a * owners + b, c * owners + e) for (a, b), (c, e) in pairs]
    return lax.ppermute(array, ("dp", "owner"), flat)


def whole(*arrays):
    return [pl.BlockSpec(a.shape, lambda i, *s, n=a.ndim: (0,) * n) for a in arrays]


def project_rows(place, counts, tokens, pieces, basis):
    layers, tok_rows, _ = tokens.shape
    tile, cols = basis.shape[1:]
    n_dp = len(pieces) + 1
    n_own = len(pieces[0])
    part_rows = tok_rows // n_own
    packed = 3 * n_dp * tok_rows // 4
    flat = [p for group in pieces for p in group]

    def kernel(place_ref, counts_ref, tokens_ref, basis_ref, *refs):
        piece_refs, out_refs = refs[: len(flat)], refs[len(flat) :]
        dp, own = place_ref[0], place_ref[1]
        row = lax.broadcasted_iota(jnp.int32, (packed, tok_rows), 0)
        col = lax.broadcasted_iota(jnp.int32, (packed, tok_rows), 1)
        turn = (col // part_rows) % n_own
        shared = (own ^ (((turn & 1) << 1) | (turn >> 1))) * part_rows + col % part_rows
        picks = []
        for mask in range(n_dp):
            shard = dp ^ mask
            start = jnp.int32(0)
            for other in range(n_dp):
                start += jnp.where(other < shard, counts_ref[other], 0)
            index = col if mask == 0 else shared
            picks.append(((row == start + index) & (index < counts_ref[shard])).astype(jnp.bfloat16))
        select = jnp.concatenate(picks, axis=1)
        for layer in range(layers):
            rows = jnp.concatenate([tokens_ref[layer]] + [p[layer] for p in piece_refs], axis=0)
            chosen = jnp.dot(select, rows, preferred_element_type=jnp.float32).astype(jnp.bfloat16)
            out_refs[layer][...] = jnp.dot(
                chosen, basis_ref[layer], preferred_element_type=jnp.float32
            ).astype(jnp.bfloat16)

    return pl.pallas_call(
        kernel,
        out_shape=[jax.ShapeDtypeStruct((packed, cols), jnp.bfloat16)] * layers,
        grid_spec=pltpu.PrefetchScalarGridSpec(
            num_scalar_prefetch=2,
            grid=(1,),
            in_specs=[pl.BlockSpec((layers, tok_rows, tile), lambda i, place, n: (0, 0, place[0]))]
            + whole(basis, *flat),
            out_specs=[pl.BlockSpec((packed, cols), lambda i, *s: (0, 0))] * layers,
        ),
        compiler_params=pltpu.CompilerParams(vmem_limit_bytes=32 * 1024 * 1024),
        cost_estimate=pl.CostEstimate(
            flops=layers * 2 * packed * tile * (n_dp * tok_rows + cols),
            bytes_accessed=2 * layers * tile * (n_dp * tok_rows + 2 * cols),
            transcendentals=0,
        ),
    )(place, counts, tokens, basis, *flat)


def settle(flags, near, far):
    def kernel(flags_ref, near_ref, *refs):
        far_refs, panel_ref, square_ref = refs[:-2], refs[-2], refs[-1]
        value = near_ref[...]
        for index, far_ref in enumerate(far_refs):
            value = jnp.where(flags_ref[0] == index + 1, far_ref[...], value)
        panel_ref[...] = value
        wide = value.astype(jnp.float32)
        square_ref[...] = jnp.sum(wide * wide, axis=0, keepdims=True)

    return pl.pallas_call(
        kernel,
        out_shape=[
            jax.ShapeDtypeStruct(near.shape, near.dtype),
            jax.ShapeDtypeStruct((1, near.shape[1]), jnp.float32),
        ],
        grid_spec=pltpu.PrefetchScalarGridSpec(
            num_scalar_prefetch=1,
            grid=(1,),
            in_specs=whole(near, *far),
            out_specs=[
                pl.BlockSpec(near.shape, lambda i, *s: (0, 0)),
                pl.BlockSpec((1, near.shape[1]), lambda i, *s: (0, 0)),
            ],
        ),
        compiler_params=pltpu.CompilerParams(vmem_limit_bytes=16 * 1024 * 1024),
        cost_estimate=pl.CostEstimate(
            flops=3 * near.size, bytes_accessed=4 * near.size, transcendentals=0
        ),
    )(flags, near, *far)


def finish(place, counts, owner_of, states, acts, grads, square_acts, square_grads):
    layers = len(acts)
    n_own, n_dp = len(square_acts), len(square_grads)
    tile = acts[0].shape[1]
    slot_count = states[0].shape[0] // 2
    width = states[0].shape[1]
    operands = [*states, *acts, *grads, *square_acts, *square_grads]

    def kernel(place_ref, counts_ref, owner_ref, *refs):
        refs = list(refs)
        take = lambda n: [refs.pop(0) for _ in range(n)]
        state_refs, act_refs, grad_refs = take(n_own), take(layers), take(layers)
        square_act_refs, square_grad_refs = take(n_own), take(n_dp)
        out_ref, new_act_ref, new_grad_ref, act_full, grad_full = refs
        dp, own = place_ref[0], place_ref[1]
        total = counts_ref[0]
        for index in range(1, counts_ref.shape[0]):
            total += counts_ref[index]
        total = total.astype(jnp.float32)
        for mask in range(n_own):
            at = pl.ds(pl.multiple_of((own ^ mask) * tile, tile), tile)
            act_full[:, at] = square_act_refs[mask][...] / total
        for mask in range(n_dp):
            at = pl.ds(pl.multiple_of((dp ^ mask) * tile, tile), tile)
            grad_full[:, at] = square_grad_refs[mask][...] / total
        new_act_ref[...] = state_refs[0][:slot_count]
        new_grad_ref[...] = state_refs[0][slot_count:]
        for layer in range(layers):
            owner_now = owner_ref[layer]
            rank = jnp.int32(0)
            for earlier in range(layer):
                rank += jnp.where(owner_ref[earlier] == owner_now, 1, 0)
            old_act = jnp.zeros((1, width), jnp.float32)
            old_grad = jnp.zeros((1, width), jnp.float32)
            for mask in range(n_own):
                for slot in range(slot_count):
                    here = (owner_now == own ^ mask) & (rank == slot)
                    old_act = jnp.where(here, state_refs[mask][slot : slot + 1], old_act)
                    old_grad = jnp.where(
                        here, state_refs[mask][slot_count + slot : slot_count + slot + 1], old_grad
                    )
            act_full[layer : layer + 1] = eigen_act = (
                decay_rate * old_act + (1.0 - decay_rate) * act_full[layer : layer + 1]
            )
            grad_full[layer : layer + 1] = eigen_grad = (
                decay_rate * old_grad + (1.0 - decay_rate) * grad_full[layer : layer + 1]
            )
            for slot in range(slot_count):

                @pl.when((owner_now == own) & (rank == slot))
                def _(slot=slot, eigen_act=eigen_act, eigen_grad=eigen_grad):
                    new_act_ref[slot : slot + 1] = eigen_act
                    new_grad_ref[slot : slot + 1] = eigen_grad

            damping = damping_rate * (jnp.sum(eigen_grad) / width) * (jnp.sum(eigen_act) / width)
            rows = grad_full[layer : layer + 1, pl.ds(pl.multiple_of(dp * tile, tile), tile)]
            cols = act_full[layer : layer + 1, pl.ds(pl.multiple_of(own * tile, tile), tile)]
            rows = jnp.transpose(jnp.broadcast_to(rows, (128, tile)))
            rows = jnp.concatenate([rows] * (tile // 128), axis=1)
            gram = lax.dot_general(
                grad_refs[layer][...],
                act_refs[layer][...],
                (((0,), (0,)), ((), ())),
                preferred_element_type=jnp.float32,
            )
            out_ref[layer] = (gram / total / (rows * cols + damping)).astype(jnp.bfloat16)

    out_shape = [
        jax.ShapeDtypeStruct((layers, tile, tile), jnp.bfloat16),
        jax.ShapeDtypeStruct((slot_count, width), jnp.float32),
        jax.ShapeDtypeStruct((slot_count, width), jnp.float32),
    ]
    return pl.pallas_call(
        kernel,
        out_shape=out_shape,
        grid_spec=pltpu.PrefetchScalarGridSpec(
            num_scalar_prefetch=3,
            grid=(1,),
            in_specs=whole(*operands),
            out_specs=whole(*out_shape),
            scratch_shapes=[pltpu.VMEM((layers, width), jnp.float32)] * 2,
        ),
        compiler_params=pltpu.CompilerParams(vmem_limit_bytes=32 * 1024 * 1024),
    )(place, counts, owner_of, *operands)


def line_plan(activations, out_grads, basis_act, basis_grad, owner_of, counts, state_act, state_grad):
    layers, tok_rows, width = activations.shape
    tile = basis_act.shape[1]
    n_dp = lax.axis_size("dp")
    n_own = lax.axis_size("owner")
    part_rows = tok_rows // n_own
    dp = lax.axis_index("dp")
    own = lax.axis_index("owner")
    place = jnp.stack([dp, own]).astype(jnp.int32)
    f32 = jnp.float32

    def pieces_of(tokens):
        part = lax.dynamic_slice_in_dim(tokens, own * part_rows, part_rows, 1)
        groups = []
        for mask in range(1, n_dp):
            got = flip(lax.dynamic_slice_in_dim(part, (dp ^ mask) * tile, tile, 2), "dp", mask)
            chip = flip(got, "owner", 2)
            groups.append([got, chip, flip(got, "owner", 1), flip(chip, "owner", 1)])
        return groups

    def add(*terms):
        return sum(term.astype(f32) for term in terms).astype(jnp.bfloat16)

    pieces_act = pieces_of(activations)
    pieces_grad = pieces_of(out_grads)

    states = [jnp.concatenate([state_act, state_grad], axis=0)]
    states += [flip(states[0], "owner", mask) for mask in range(1, n_own)]

    parts_act = project_rows(place, counts, activations, pieces_act, basis_act)
    parts_grad = project_rows(place, counts, out_grads, pieces_grad, basis_grad)
    outer = (dp == 0) | (dp == n_dp - 1)
    take_outer = jnp.where(outer, 1, 0).astype(jnp.int32)[None]
    home = jnp.where(own == dp, 0, jnp.where(own == dp ^ 2, 1, 2)).astype(jnp.int32)[None]
    every = range(n_own)
    acts, grads, square_acts, square_grads = [], [], [], []
    for layer in range(layers):
        part = parts_act[layer]
        part = add(part, hop(part, [((a, b), (c, b)) for a, c in ((0, 1), (3, 2)) for b in every]))
        part = add(part, hop(part, [((a, b), (c, b)) for a, c in ((1, 2), (2, 1)) for b in every]))
        back = hop(part, [((a, b), (c, b)) for a, c in ((1, 0), (2, 3)) for b in every])
        panel, square = settle(take_outer, part, [back])
        acts.append(panel)
        square_acts.append(square)
        part = parts_grad[layer]
        part = add(part, hop(part, [((0, b), (1, b)) for b in (1, 2, 3)] + [((3, b), (2, b)) for b in (0, 1, 2)]))
        part = add(part, hop(part, [((1, b), (2, b)) for b in (2, 3)] + [((2, b), (1, b)) for b in (0, 1)]))
        part = add(part, hop(part, [((1, 0), (0, 0)), ((2, 3), (3, 3))]))
        chip = hop(part, [((a, a), (a, a ^ 2)) for a in range(n_dp)])
        half = jnp.where(own == dp, part, chip)
        core = hop(half, [((a, a ^ b), (a, a ^ b ^ 1)) for a in range(n_dp) for b in (0, 2)])
        panel, square = settle(home, part, [chip, core])
        grads.append(panel)
        square_grads.append(square)
    square_act = jnp.concatenate(square_acts, axis=0)
    square_grad = jnp.concatenate(square_grads, axis=0)
    square_acts = [square_act] + [flip(square_act, "owner", mask) for mask in range(1, n_own)]
    square_grads = [square_grad] + [flip(square_grad, "dp", mask) for mask in range(1, n_dp)]
    return tuple(finish(place, counts, owner_of, states, acts, grads, square_acts, square_grads))


def solution(mesh):
    placed = (
        P("groups", "dp", None),
        P("groups", "dp", None),
        P("groups", "dp", "owner"),
        P("groups", "dp", "owner"),
        P(),
        P("groups"),
        P("owner", "groups"),
        P("owner", "groups"),
    )
    square = mesh.shape["dp"] == 4 and mesh.shape["owner"] == 4
    return jax.shard_map(
        line_plan if square else gather_plan,
        mesh=mesh,
        in_specs=placed,
        out_specs=(P("groups", "dp", "owner"), P("owner", "groups"), P("owner", "groups")),
        check_vma=False,
    )
```

```python
import jax
import jax.numpy as jnp
from jax import lax
from jax.experimental import pallas as pl
from jax.experimental.pallas import tpu as pltpu
from jax.sharding import PartitionSpec as P

decay_rate = 0.25
damping_rate = 0.1


def spread(array, axis, root):
    mine = lax.axis_index(axis) == root
    return lax.psum(jnp.where(mine, array, jnp.zeros_like(array)), axis)


def gather_plan(activations, out_grads, basis_act, basis_grad, owner_of, counts, state_act, state_grad):
    layers = activations.shape[0]
    tok_rows = activations.shape[1]
    tile_rows = basis_act.shape[1]
    tile_cols = basis_act.shape[2]
    slot_count = state_act.shape[0]
    dp_index = lax.axis_index("dp")
    own_index = lax.axis_index("owner")
    valid_rows = (jnp.arange(tok_rows) < counts[dp_index]).astype(jnp.float32)[:, None]
    valid_total = jnp.sum(counts).astype(jnp.float32)
    square_acts = []
    square_grads = []
    gram_tiles = []
    for layer_index in range(layers):
        panel_act = jnp.dot(
            activations[layer_index],
            lax.all_gather(basis_act[layer_index], "dp", axis=0, tiled=True),
            preferred_element_type=jnp.float32,
        )
        panel_grad = jnp.dot(
            out_grads[layer_index],
            lax.all_gather(basis_grad[layer_index], "dp", axis=0, tiled=True),
            preferred_element_type=jnp.float32,
        )
        panel_act = (panel_act * valid_rows).astype(jnp.bfloat16)
        panel_grad = (panel_grad * valid_rows).astype(jnp.bfloat16)
        full_act = lax.all_gather(panel_act, "owner", axis=1, tiled=True)
        full_grad = lax.all_gather(panel_grad, "owner", axis=1, tiled=True)
        square_act = jnp.sum(jnp.square(full_act.astype(jnp.float32)), axis=0)
        square_grad = jnp.sum(jnp.square(full_grad.astype(jnp.float32)), axis=0)
        gram_term = lax.dot_general(
            full_grad, panel_act, (((0,), (0,)), ((), ())), preferred_element_type=jnp.float32
        )
        gram_tiles.append(
            lax.psum_scatter(
                gram_term.astype(jnp.bfloat16), "dp", scatter_dimension=0, tiled=True
            ).astype(jnp.float32)
            / valid_total
        )
        square_act, square_grad = lax.psum((square_act, square_grad), "dp")
        square_acts.append(square_act)
        square_grads.append(square_grad)
    new_act = state_act
    new_grad = state_grad
    results = []
    for layer_index in range(layers):
        owner_now = owner_of[layer_index]
        slot_rank = jnp.sum((owner_of[:layer_index] == owner_now).astype(jnp.int32))
        selector = (jnp.arange(slot_count) == slot_rank).astype(jnp.float32)[:, None]
        local_act = decay_rate * jnp.sum(state_act * selector, axis=0) + (
            1.0 - decay_rate
        ) * (square_acts[layer_index] / valid_total)
        local_grad = decay_rate * jnp.sum(state_grad * selector, axis=0) + (
            1.0 - decay_rate
        ) * (square_grads[layer_index] / valid_total)
        eigen_act = spread(local_act, "owner", owner_now)
        eigen_grad = spread(local_grad, "owner", owner_now)
        replace_rows = ((jnp.arange(slot_count) == slot_rank) & (own_index == owner_now))[:, None]
        new_act = jnp.where(replace_rows, eigen_act[None, :], new_act)
        new_grad = jnp.where(replace_rows, eigen_grad[None, :], new_grad)
        damping = damping_rate * jnp.mean(eigen_grad) * jnp.mean(eigen_act)
        grad_eigen = lax.dynamic_slice_in_dim(eigen_grad, dp_index * tile_rows, tile_rows)
        act_eigen = lax.dynamic_slice_in_dim(eigen_act, own_index * tile_cols, tile_cols)
        scaled = gram_tiles[layer_index] / (grad_eigen[:, None] * act_eigen[None, :] + damping)
        results.append(scaled.astype(jnp.bfloat16))
    return (jnp.stack(results), new_act, new_grad)


def flip(array, axis, mask):
    return lax.ppermute(array, axis, [(i, i ^ mask) for i in range(lax.axis_size(axis))])


def hop(array, pairs):
    owners = lax.axis_size("owner")
    flat = [(a * owners + b, c * owners + e) for (a, b), (c, e) in pairs]
    return lax.ppermute(array, ("dp", "owner"), flat)


def whole(*arrays):
    return [pl.BlockSpec(a.shape, lambda i, *s, n=a.ndim: (0,) * n) for a in arrays]


def project_rows(place, counts, tokens, pieces, basis, groups):
    layers, tok_rows, _ = tokens.shape
    tile, cols = basis.shape[1:]
    n_dp = len(pieces) + 1
    n_own = len(pieces[0])
    part_rows = tok_rows // n_own
    packed = 3 * n_dp * tok_rows // 4
    half = packed // 2
    flat = [p for group in pieces for p in group]
    shapes = [(len(group), half, cols) for group in groups for _ in range(2)]

    def kernel(place_ref, counts_ref, tokens_ref, basis_ref, *refs):
        piece_refs, out_refs = refs[: len(flat)], refs[len(flat) :]
        dp, own = place_ref[0], place_ref[1]
        row = lax.broadcasted_iota(jnp.int32, (packed, tok_rows), 0)
        row = jnp.where(dp % 2 == 0, row, jnp.where(row < half, row + half, row - half))
        col = lax.broadcasted_iota(jnp.int32, (packed, tok_rows), 1)
        turn = (col // part_rows) % n_own
        shared = (own ^ (((turn & 1) << 1) | (turn >> 1))) * part_rows + col % part_rows
        picks = []
        for mask in range(n_dp):
            shard = dp ^ mask
            start = jnp.int32(0)
            for other in range(n_dp):
                start += jnp.where(other < shard, counts_ref[other], 0)
            index = col if mask == 0 else shared
            picks.append(((row == start + index) & (index < counts_ref[shard])).astype(jnp.bfloat16))
        select = jnp.concatenate(picks, axis=1)
        for number, group in enumerate(groups):
            for at, layer in enumerate(group):
                rows = jnp.concatenate([tokens_ref[layer]] + [p[layer] for p in piece_refs], axis=0)
                chosen = jnp.dot(select, rows, preferred_element_type=jnp.float32).astype(jnp.bfloat16)
                result = jnp.dot(
                    chosen, basis_ref[layer], preferred_element_type=jnp.float32
                ).astype(jnp.bfloat16)
                out_refs[2 * number][at] = result[:half]
                out_refs[2 * number + 1][at] = result[half:]

    return pl.pallas_call(
        kernel,
        out_shape=[jax.ShapeDtypeStruct(shape, jnp.bfloat16) for shape in shapes],
        grid_spec=pltpu.PrefetchScalarGridSpec(
            num_scalar_prefetch=2,
            grid=(1,),
            in_specs=[pl.BlockSpec((layers, tok_rows, tile), lambda i, place, n: (0, 0, place[0]))]
            + whole(basis, *flat),
            out_specs=[pl.BlockSpec(shape, lambda i, *s: (0, 0, 0)) for shape in shapes],
        ),
        compiler_params=pltpu.CompilerParams(vmem_limit_bytes=32 * 1024 * 1024),
        cost_estimate=pl.CostEstimate(
            flops=layers * 2 * packed * tile * (n_dp * tok_rows + cols),
            bytes_accessed=2 * layers * tile * (n_dp * tok_rows + 2 * cols),
            transcendentals=0,
        ),
    )(place, counts, tokens, basis, *flat)


def column_squares(ref, other_ref, layer):
    near = ref[layer].astype(jnp.float32)
    far = other_ref[layer].astype(jnp.float32)
    return jnp.sum(near * near, axis=0, keepdims=True) + jnp.sum(far * far, axis=0, keepdims=True)


def settle_acts(state_act, state_grad, panels):
    slot_count, width = state_act.shape
    cols = panels[0].shape[2]
    layers = sum(panel.shape[0] for panel in panels[::2])

    def kernel(state_act_ref, state_grad_ref, *refs):
        packet_ref = refs[-1]
        packet_ref[...] = jnp.zeros_like(packet_ref)
        packet_ref[:slot_count] = state_act_ref[...]
        packet_ref[slot_count : 2 * slot_count] = state_grad_ref[...]
        layer = 2 * slot_count
        for near_ref, far_ref in zip(refs[:-1:2], refs[1:-1:2], strict=True):
            for at in range(near_ref.shape[0]):
                packet_ref[layer : layer + 1, :cols] = column_squares(near_ref, far_ref, at)
                layer += 1

    return pl.pallas_call(
        kernel,
        out_shape=jax.ShapeDtypeStruct((2 * slot_count + layers, width), jnp.float32),
        compiler_params=pltpu.CompilerParams(vmem_limit_bytes=32 * 1024 * 1024),
    )(state_act, state_grad, *panels)


def settle_grads(place, home, arrivals):
    layers, half, cols = arrivals[0][0].shape
    flat = [array for pair in arrivals for array in pair]

    def kernel(home_ref, *refs):
        in_refs, (near_ref, far_ref, square_ref) = refs[:-3], refs[-3:]
        for index in range(len(arrivals)):

            @pl.when(home_ref[0] == index)
            def _(index=index):
                near_ref[...] = in_refs[2 * index][...]
                far_ref[...] = in_refs[2 * index + 1][...]

        for layer in range(layers):
            square_ref[layer : layer + 1] = column_squares(near_ref, far_ref, layer)

    out_shape = [jax.ShapeDtypeStruct((layers, half, cols), jnp.bfloat16)] * 2 + [
        jax.ShapeDtypeStruct((layers, cols), jnp.float32)
    ]
    return pl.pallas_call(
        kernel,
        out_shape=out_shape,
        grid_spec=pltpu.PrefetchScalarGridSpec(
            num_scalar_prefetch=1, grid=(1,), in_specs=whole(*flat), out_specs=whole(*out_shape)
        ),
        compiler_params=pltpu.CompilerParams(vmem_limit_bytes=32 * 1024 * 1024),
    )(home, *flat)


def finish(place, counts, owner_of, packets, squares, acts, grads, slot_count):
    layers = owner_of.shape[0]
    n_own, n_dp = len(packets), len(squares)
    tile = acts[0].shape[2]
    width = packets[0].shape[1]
    where_act = [(2 * number, at) for number, a in enumerate(acts[::2]) for at in range(a.shape[0])]
    operands = [*packets, *squares, *acts, *grads]

    def kernel(place_ref, counts_ref, owner_ref, *refs):
        packet_refs, refs = refs[:n_own], refs[n_own:]
        square_refs, refs = refs[:n_dp], refs[n_dp:]
        act_refs, refs = refs[: len(acts)], refs[len(acts) :]
        grad_refs, refs = refs[:2], refs[2:]
        out_ref, new_act_ref, new_grad_ref, act_full, grad_full = refs
        dp, own = place_ref[0], place_ref[1]
        total = counts_ref[0]
        for index in range(1, counts_ref.shape[0]):
            total += counts_ref[index]
        total = total.astype(jnp.float32)
        for mask in range(n_own):
            at = pl.ds(pl.multiple_of((own ^ mask) * tile, tile), tile)
            act_full[:, at] = packet_refs[mask][2 * slot_count :, :tile] / total
        for mask in range(n_dp):
            at = pl.ds(pl.multiple_of((dp ^ mask) * tile, tile), tile)
            grad_full[:, at] = square_refs[mask][...] / total
        new_act_ref[...] = packet_refs[0][:slot_count]
        new_grad_ref[...] = packet_refs[0][slot_count : 2 * slot_count]
        for layer in range(layers):
            owner_now = owner_ref[layer]
            rank = jnp.int32(0)
            for earlier in range(layer):
                rank += jnp.where(owner_ref[earlier] == owner_now, 1, 0)
            old_act = jnp.zeros((1, width), jnp.float32)
            old_grad = jnp.zeros((1, width), jnp.float32)
            for mask in range(n_own):
                for slot in range(slot_count):
                    here = (owner_now == own ^ mask) & (rank == slot)
                    down = slot_count + slot
                    old_act = jnp.where(here, packet_refs[mask][slot : slot + 1], old_act)
                    old_grad = jnp.where(here, packet_refs[mask][down : down + 1], old_grad)
            eigen_act = decay_rate * old_act + (1.0 - decay_rate) * act_full[layer : layer + 1]
            eigen_grad = decay_rate * old_grad + (1.0 - decay_rate) * grad_full[layer : layer + 1]
            act_full[layer : layer + 1] = eigen_act
            grad_full[layer : layer + 1] = eigen_grad
            for slot in range(slot_count):

                @pl.when((owner_now == own) & (rank == slot))
                def _(slot=slot, eigen_act=eigen_act, eigen_grad=eigen_grad):
                    new_act_ref[slot : slot + 1] = eigen_act
                    new_grad_ref[slot : slot + 1] = eigen_grad

            damping = damping_rate * (jnp.sum(eigen_grad) / width) * (jnp.sum(eigen_act) / width)
            rows = grad_full[layer : layer + 1, pl.ds(pl.multiple_of(dp * tile, tile), tile)]
            cols = act_full[layer : layer + 1, pl.ds(pl.multiple_of(own * tile, tile), tile)]
            rows = jnp.transpose(jnp.broadcast_to(rows, (128, tile)))
            rows = jnp.concatenate([rows] * (tile // 128), axis=1)
            number, at = where_act[layer]
            gram = sum(
                lax.dot_general(
                    grad_refs[side][layer],
                    act_refs[number + side][at],
                    (((0,), (0,)), ((), ())),
                    preferred_element_type=jnp.float32,
                )
                for side in range(2)
            )
            out_ref[layer] = (gram / total / (rows * cols + damping)).astype(jnp.bfloat16)

    out_shape = [
        jax.ShapeDtypeStruct((layers, tile, tile), jnp.bfloat16),
        jax.ShapeDtypeStruct((slot_count, width), jnp.float32),
        jax.ShapeDtypeStruct((slot_count, width), jnp.float32),
    ]
    return pl.pallas_call(
        kernel,
        out_shape=out_shape,
        grid_spec=pltpu.PrefetchScalarGridSpec(
            num_scalar_prefetch=3,
            grid=(1,),
            in_specs=whole(*operands),
            out_specs=whole(*out_shape),
            scratch_shapes=[pltpu.VMEM((layers, width), jnp.float32)] * 2,
        ),
        compiler_params=pltpu.CompilerParams(vmem_limit_bytes=32 * 1024 * 1024),
    )(place, counts, owner_of, *operands)


def line_plan(activations, out_grads, basis_act, basis_grad, owner_of, counts, state_act, state_grad):
    layers, tok_rows, width = activations.shape
    tile = basis_act.shape[1]
    n_dp = lax.axis_size("dp")
    n_own = lax.axis_size("owner")
    part_rows = tok_rows // n_own
    dp = lax.axis_index("dp")
    own = lax.axis_index("owner")
    place = jnp.stack([dp, own]).astype(jnp.int32)

    def pieces_of(tokens):
        part = lax.dynamic_slice_in_dim(tokens, own * part_rows, part_rows, 1)
        groups = []
        for mask in range(1, n_dp):
            got = flip(lax.dynamic_slice_in_dim(part, (dp ^ mask) * tile, tile, 2), "dp", mask)
            chip = flip(got, "owner", 2)
            groups.append([got, chip, flip(got, "owner", 1), flip(chip, "owner", 1)])
        return groups

    def add(first, second):
        return (first.astype(jnp.float32) + second.astype(jnp.float32)).astype(jnp.bfloat16)

    swapped = lax.ppermute(basis_grad, "owner", [(o, -o % n_own) for o in range(n_own)])
    held = [-o % n_own for o in range(n_own)]

    pieces_act = pieces_of(activations)
    pieces_grad = pieces_of(out_grads)
    early = [[*range(layers - 1)], [layers - 1]]
    parts_act = project_rows(place, counts, activations, pieces_act, basis_act, early)
    keep, send = project_rows(place, counts, out_grads, pieces_grad, swapped, [[*range(layers)]])

    def total_of(keep, send):
        part = add(keep, flip(send, "dp", 1))
        part = add(part, flip(part, "dp", 2))
        return [part, flip(part, "dp", 1)]

    first = total_of(*parts_act[:2])

    part = add(keep, flip(send, "dp", 1))
    pairs = [((a, o), (a ^ 2, o)) for a in range(n_dp) for o in range(n_own) if (a ^ held[o]) & 2]
    near = add(part, hop(part, pairs))
    far = hop(near, [((held[o] ^ 1, o), (held[o], o)) for o in range(n_own)])
    arrivals = [(near, far)]
    arrivals.append([hop(a, [((held[o], o), (held[o], o ^ 2)) for o in range(n_own)]) for a in (near, far)])
    source = -dp % n_own
    pairs = [((held[o], o ^ b), (held[o], o ^ b ^ 1)) for o in range(n_own) for b in (0, 2)]
    arrivals.append([hop(jnp.where(own == source, a, b), pairs) for a, b in zip(*arrivals, strict=True)])
    home = jnp.where(own == source, 0, jnp.where(own == source ^ 2, 1, 2)).astype(jnp.int32)[None]
    *grads, squares = settle_grads(place, home, arrivals)
    squares = [squares] + [flip(squares, "dp", mask) for mask in range(1, n_dp)]

    acts = first + total_of(*parts_act[2:])
    packet = settle_acts(state_act, state_grad, acts)
    packets = [packet] + [flip(packet, "owner", mask) for mask in range(1, n_own)]
    return tuple(finish(place, counts, owner_of, packets, squares, acts, grads, state_act.shape[0]))


def solution(mesh):
    placed = (
        P("groups", "dp", None),
        P("groups", "dp", None),
        P("groups", "dp", "owner"),
        P("groups", "dp", "owner"),
        P(),
        P("groups"),
        P("owner", "groups"),
        P("owner", "groups"),
    )
    square = mesh.shape["dp"] == 4 and mesh.shape["owner"] == 4
    return jax.shard_map(
        line_plan if square else gather_plan,
        mesh=mesh,
        in_specs=placed,
        out_specs=(P("groups", "dp", "owner"), P("owner", "groups"), P("owner", "groups")),
        check_vma=False,
    )
```

```python
import jax
import jax.numpy as jnp
from jax import lax
from jax.experimental import pallas as pl
from jax.experimental.pallas import tpu as pltpu
from jax.sharding import PartitionSpec as P

decay_rate = 0.25
damping_rate = 0.1
vmem_spec = pl.BlockSpec(memory_space=pltpu.VMEM)
scalar_spec = pl.BlockSpec(memory_space=pltpu.SMEM)
light = pl.CostEstimate(flops=0, bytes_accessed=0, transcendentals=0)


def spread(array, axis, root):
    mine = lax.axis_index(axis) == root
    return lax.psum(jnp.where(mine, array, jnp.zeros_like(array)), axis)


def gather_plan(activations, out_grads, basis_act, basis_grad, owner_of, counts, state_act, state_grad):
    layers = activations.shape[0]
    tok_rows = activations.shape[1]
    tile_rows = basis_act.shape[1]
    tile_cols = basis_act.shape[2]
    slot_count = state_act.shape[0]
    dp_index = lax.axis_index("dp")
    own_index = lax.axis_index("owner")
    valid_rows = (jnp.arange(tok_rows) < counts[dp_index]).astype(jnp.float32)[:, None]
    valid_total = jnp.sum(counts).astype(jnp.float32)
    square_acts = []
    square_grads = []
    gram_tiles = []
    for layer_index in range(layers):
        panel_act = jnp.dot(
            activations[layer_index],
            lax.all_gather(basis_act[layer_index], "dp", axis=0, tiled=True),
            preferred_element_type=jnp.float32,
        )
        panel_grad = jnp.dot(
            out_grads[layer_index],
            lax.all_gather(basis_grad[layer_index], "dp", axis=0, tiled=True),
            preferred_element_type=jnp.float32,
        )
        panel_act = (panel_act * valid_rows).astype(jnp.bfloat16)
        panel_grad = (panel_grad * valid_rows).astype(jnp.bfloat16)
        full_act = lax.all_gather(panel_act, "owner", axis=1, tiled=True)
        full_grad = lax.all_gather(panel_grad, "owner", axis=1, tiled=True)
        square_act = jnp.sum(jnp.square(full_act.astype(jnp.float32)), axis=0)
        square_grad = jnp.sum(jnp.square(full_grad.astype(jnp.float32)), axis=0)
        gram_term = lax.dot_general(
            full_grad, panel_act, (((0,), (0,)), ((), ())), preferred_element_type=jnp.float32
        )
        gram_tiles.append(
            lax.psum_scatter(
                gram_term.astype(jnp.bfloat16), "dp", scatter_dimension=0, tiled=True
            ).astype(jnp.float32)
            / valid_total
        )
        square_act, square_grad = lax.psum((square_act, square_grad), "dp")
        square_acts.append(square_act)
        square_grads.append(square_grad)
    new_act = state_act
    new_grad = state_grad
    results = []
    for layer_index in range(layers):
        owner_now = owner_of[layer_index]
        slot_rank = jnp.sum((owner_of[:layer_index] == owner_now).astype(jnp.int32))
        selector = (jnp.arange(slot_count) == slot_rank).astype(jnp.float32)[:, None]
        local_act = decay_rate * jnp.sum(state_act * selector, axis=0) + (
            1.0 - decay_rate
        ) * (square_acts[layer_index] / valid_total)
        local_grad = decay_rate * jnp.sum(state_grad * selector, axis=0) + (
            1.0 - decay_rate
        ) * (square_grads[layer_index] / valid_total)
        eigen_act = spread(local_act, "owner", owner_now)
        eigen_grad = spread(local_grad, "owner", owner_now)
        replace_rows = ((jnp.arange(slot_count) == slot_rank) & (own_index == owner_now))[:, None]
        new_act = jnp.where(replace_rows, eigen_act[None, :], new_act)
        new_grad = jnp.where(replace_rows, eigen_grad[None, :], new_grad)
        damping = damping_rate * jnp.mean(eigen_grad) * jnp.mean(eigen_act)
        grad_eigen = lax.dynamic_slice_in_dim(eigen_grad, dp_index * tile_rows, tile_rows)
        act_eigen = lax.dynamic_slice_in_dim(eigen_act, own_index * tile_cols, tile_cols)
        scaled = gram_tiles[layer_index] / (grad_eigen[:, None] * act_eigen[None, :] + damping)
        results.append(scaled.astype(jnp.bfloat16))
    return (jnp.stack(results), new_act, new_grad)


def flip(array, axis, mask):
    return lax.ppermute(array, axis, [(i, i ^ mask) for i in range(lax.axis_size(axis))])


def hop(array, pairs):
    owners = lax.axis_size("owner")
    flat = [(a * owners + b, c * owners + e) for (a, b), (c, e) in pairs]
    return lax.ppermute(array, ("dp", "owner"), flat)


def project_rows(scalars, tokens, pieces, basis):
    layers, tok_rows, _ = tokens.shape
    tile, cols = basis.shape[1:]
    n_dp = len(pieces) + 1
    n_own = len(pieces[0])
    part_rows = tok_rows // n_own
    packed = 3 * n_dp * tok_rows // 4
    half = packed // 2
    flat = [p for group in pieces for p in group]
    shapes = [(layers, half, cols)] * 2

    def kernel(scalar_ref, tokens_hbm, basis_hbm, *refs):
        piece_refs, refs = refs[: len(flat)], refs[len(flat) :]
        out_refs, (tokens_ref, basis_ref, sems) = refs[: len(shapes)], refs[len(shapes) :]
        dp, own = scalar_ref[0], scalar_ref[1]
        at = pl.ds(pl.multiple_of(dp * tile, tile), tile)
        copies = []
        for layer in range(layers):
            copies.append(
                [
                    pltpu.make_async_copy(
                        tokens_hbm.at[layer, :, at], tokens_ref.at[layer], sems.at[2 * layer]
                    ),
                    pltpu.make_async_copy(basis_hbm.at[layer], basis_ref.at[layer], sems.at[2 * layer + 1]),
                ]
            )
            for copy in copies[-1]:
                copy.start()
        row = lax.broadcasted_iota(jnp.int32, (packed, tok_rows), 0)
        row = jnp.where(dp % 2 == 0, row, jnp.where(row < half, row + half, row - half))
        col = lax.broadcasted_iota(jnp.int32, (packed, tok_rows), 1)
        turn = (col // part_rows) % n_own
        shared = (own ^ (((turn & 1) << 1) | (turn >> 1))) * part_rows + col % part_rows
        picks = []
        for mask in range(n_dp):
            shard = dp ^ mask
            start = jnp.int32(0)
            for other in range(n_dp):
                start += jnp.where(other < shard, scalar_ref[2 + other], 0)
            index = col if mask == 0 else shared
            chosen = (row == start + index) & (index < scalar_ref[2 + shard])
            picks.append(chosen.astype(jnp.bfloat16))
        select = jnp.concatenate(picks, axis=1)
        for layer in range(layers):
            copies[layer][0].wait()
            rows = jnp.concatenate([tokens_ref[layer]] + [p[layer] for p in piece_refs], axis=0)
            chosen = jnp.dot(select, rows, preferred_element_type=jnp.float32).astype(jnp.bfloat16)
            copies[layer][1].wait()
            result = jnp.dot(chosen, basis_ref[layer], preferred_element_type=jnp.float32).astype(
                jnp.bfloat16
            )
            out_refs[0][layer] = result[:half]
            out_refs[1][layer] = result[half:]

    return pl.pallas_call(
        kernel,
        out_shape=[jax.ShapeDtypeStruct(shape, jnp.bfloat16) for shape in shapes],
        in_specs=[scalar_spec] + [pl.BlockSpec(memory_space=pltpu.HBM)] * 2 + [vmem_spec] * len(flat),
        out_specs=[vmem_spec] * len(shapes),
        scratch_shapes=[
            pltpu.VMEM((layers, tok_rows, tile), jnp.bfloat16),
            pltpu.VMEM((layers, tile, cols), jnp.bfloat16),
            pltpu.SemaphoreType.DMA((2 * layers,)),
        ],
        compiler_params=pltpu.CompilerParams(vmem_limit_bytes=16 * 1024 * 1024),
        cost_estimate=light,
    )(scalars, *[pltpu.with_memory_space_constraint(array, pltpu.HBM) for array in (tokens, basis)], *flat)


def add(first, second):
    def kernel(first_ref, second_ref, out_ref):
        total = first_ref[...].astype(jnp.float32) + second_ref[...].astype(jnp.float32)
        out_ref[...] = total.astype(out_ref.dtype)

    return pl.pallas_call(
        kernel,
        out_shape=jax.ShapeDtypeStruct(first.shape, first.dtype),
        in_specs=[vmem_spec] * 2,
        out_specs=vmem_spec,
        compiler_params=pltpu.CompilerParams(vmem_limit_bytes=8 * 1024 * 1024),
        cost_estimate=light,
    )(first, second)


def cut_rows(arrays, tile, n_own, n_dp):
    layers, tok_rows, _ = arrays[0].shape
    part_rows = tok_rows // n_own
    peers = n_dp - 1

    def kernel(*refs):
        in_refs, out_refs, sems = refs[: len(arrays)], refs[len(arrays) : -1], refs[-1]
        dp, own = lax.axis_index("dp"), lax.axis_index("owner")
        rows = pl.ds(pl.multiple_of(own * part_rows, part_rows), part_rows)
        copies = []
        for number, out_ref in enumerate(out_refs):
            block = dp ^ (number % peers + 1)
            cols = pl.ds(pl.multiple_of(block * tile, tile), tile)
            copies.append(
                pltpu.make_async_copy(in_refs[number // peers].at[:, rows, cols], out_ref, sems.at[number])
            )
            copies[-1].start()
        for copy in copies:
            copy.wait()

    count = len(arrays) * peers
    return pl.pallas_call(
        kernel,
        out_shape=[jax.ShapeDtypeStruct((layers, part_rows, tile), arrays[0].dtype)] * count,
        in_specs=[pl.BlockSpec(memory_space=pltpu.HBM)] * len(arrays),
        out_specs=[vmem_spec] * count,
        scratch_shapes=[pltpu.SemaphoreType.DMA((count,))],
        compiler_params=pltpu.CompilerParams(vmem_limit_bytes=8 * 1024 * 1024),
        cost_estimate=light,
    )(*[pltpu.with_memory_space_constraint(array, pltpu.HBM) for array in arrays])


def pick(home, choices):
    flat = [array for arrays in choices for array in arrays]
    count = len(choices[0])

    def kernel(home_ref, *refs):
        for number, out_ref in enumerate(refs[len(flat) :]):
            for index in range(count):

                @pl.when(home_ref[0] == index)
                def _(number=number, index=index, out_ref=out_ref):
                    out_ref[...] = refs[number * count + index][...]

    return pl.pallas_call(
        kernel,
        out_shape=[jax.ShapeDtypeStruct(arrays[0].shape, arrays[0].dtype) for arrays in choices],
        in_specs=[scalar_spec] + [vmem_spec] * len(flat),
        out_specs=[vmem_spec] * len(choices),
        compiler_params=pltpu.CompilerParams(vmem_limit_bytes=8 * 1024 * 1024),
        cost_estimate=light,
    )(home, *flat)


def column_squares(ref, other_ref, layer):
    near = ref[layer].astype(jnp.float32)
    far = other_ref[layer].astype(jnp.float32)
    return jnp.sum(near * near, axis=0, keepdims=True) + jnp.sum(far * far, axis=0, keepdims=True)


def settle_acts(state_act, state_grad, panels):
    slot_count, width = state_act.shape
    cols = panels[0].shape[2]
    layers = panels[0].shape[0]

    def kernel(state_act_ref, state_grad_ref, *refs):
        packet_ref = refs[-1]
        packet_ref[...] = jnp.zeros_like(packet_ref)
        packet_ref[:slot_count] = state_act_ref[...]
        packet_ref[slot_count : 2 * slot_count] = state_grad_ref[...]
        for layer in range(layers):
            row = 2 * slot_count + layer
            packet_ref[row : row + 1, :cols] = column_squares(refs[0], refs[1], layer)

    return pl.pallas_call(
        kernel,
        out_shape=jax.ShapeDtypeStruct((2 * slot_count + layers, width), jnp.float32),
        in_specs=[vmem_spec] * (2 + len(panels)),
        out_specs=vmem_spec,
        compiler_params=pltpu.CompilerParams(vmem_limit_bytes=8 * 1024 * 1024),
        cost_estimate=light,
    )(state_act, state_grad, *panels)


def settle_grads(home, arrivals):
    layers, half, cols = arrivals[0][0].shape
    flat = [array for pair in arrivals for array in pair]

    def kernel(home_ref, *refs):
        in_refs, (near_ref, far_ref, square_ref) = refs[:-3], refs[-3:]
        for index in range(len(arrivals)):

            @pl.when(home_ref[0] == index)
            def _(index=index):
                near_ref[...] = in_refs[2 * index][...]
                far_ref[...] = in_refs[2 * index + 1][...]

        for layer in range(layers):
            square_ref[layer : layer + 1] = column_squares(near_ref, far_ref, layer)

    out_shape = [jax.ShapeDtypeStruct((layers, half, cols), jnp.bfloat16)] * 2 + [
        jax.ShapeDtypeStruct((layers, cols), jnp.float32)
    ]
    return pl.pallas_call(
        kernel,
        out_shape=out_shape,
        in_specs=[scalar_spec] + [vmem_spec] * len(flat),
        out_specs=[vmem_spec] * len(out_shape),
        compiler_params=pltpu.CompilerParams(vmem_limit_bytes=8 * 1024 * 1024),
        cost_estimate=light,
    )(home, *flat)


def finish(scalars, packets, squares, acts, grads, slot_count):
    n_own, n_dp = len(packets), len(squares)
    layers, _, tile = acts[0].shape
    width = packets[0].shape[1]
    operands = [*packets, *squares, *acts, *grads]

    def kernel(scalar_ref, *refs):
        packet_refs, refs = refs[:n_own], refs[n_own:]
        square_refs, refs = refs[:n_dp], refs[n_dp:]
        act_refs, refs = refs[: len(acts)], refs[len(acts) :]
        grad_refs, refs = refs[:2], refs[2:]
        out_ref, new_act_ref, new_grad_ref, act_full, grad_full = refs
        dp, own = scalar_ref[0], scalar_ref[1]
        total = scalar_ref[2]
        for index in range(1, n_dp):
            total += scalar_ref[2 + index]
        total = total.astype(jnp.float32)
        owners = [scalar_ref[2 + n_dp + layer] for layer in range(layers)]
        for mask in range(n_own):
            at = pl.ds(pl.multiple_of((own ^ mask) * tile, tile), tile)
            act_full[:, at] = packet_refs[mask][2 * slot_count :, :tile] / total
        for mask in range(n_dp):
            at = pl.ds(pl.multiple_of((dp ^ mask) * tile, tile), tile)
            grad_full[:, at] = square_refs[mask][...] / total
        new_act_ref[...] = packet_refs[0][:slot_count]
        new_grad_ref[...] = packet_refs[0][slot_count : 2 * slot_count]
        for layer in range(layers):
            owner_now = owners[layer]
            rank = jnp.int32(0)
            for earlier in range(layer):
                rank += jnp.where(owners[earlier] == owner_now, 1, 0)
            old_act = jnp.zeros((1, width), jnp.float32)
            old_grad = jnp.zeros((1, width), jnp.float32)
            for mask in range(n_own):
                for slot in range(slot_count):
                    here = (owner_now == own ^ mask) & (rank == slot)
                    down = slot_count + slot
                    old_act = jnp.where(here, packet_refs[mask][slot : slot + 1], old_act)
                    old_grad = jnp.where(here, packet_refs[mask][down : down + 1], old_grad)
            eigen_act = decay_rate * old_act + (1.0 - decay_rate) * act_full[layer : layer + 1]
            eigen_grad = decay_rate * old_grad + (1.0 - decay_rate) * grad_full[layer : layer + 1]
            act_full[layer : layer + 1] = eigen_act
            grad_full[layer : layer + 1] = eigen_grad
            for slot in range(slot_count):

                @pl.when((owner_now == own) & (rank == slot))
                def _(slot=slot, eigen_act=eigen_act, eigen_grad=eigen_grad):
                    new_act_ref[slot : slot + 1] = eigen_act
                    new_grad_ref[slot : slot + 1] = eigen_grad

            damping = damping_rate * (jnp.sum(eigen_grad) / width) * (jnp.sum(eigen_act) / width)
            rows = grad_full[layer : layer + 1, pl.ds(pl.multiple_of(dp * tile, tile), tile)]
            cols = act_full[layer : layer + 1, pl.ds(pl.multiple_of(own * tile, tile), tile)]
            rows = jnp.transpose(jnp.broadcast_to(rows, (128, tile)))
            rows = jnp.concatenate([rows] * (tile // 128), axis=1)
            gram = sum(
                lax.dot_general(
                    grad_refs[side][layer],
                    act_refs[side][layer],
                    (((0,), (0,)), ((), ())),
                    preferred_element_type=jnp.float32,
                )
                for side in range(2)
            )
            out_ref[layer] = (gram / total / (rows * cols + damping)).astype(jnp.bfloat16)

    out_shape = [
        jax.ShapeDtypeStruct((layers, tile, tile), jnp.bfloat16),
        jax.ShapeDtypeStruct((slot_count, width), jnp.float32),
        jax.ShapeDtypeStruct((slot_count, width), jnp.float32),
    ]
    return pl.pallas_call(
        kernel,
        out_shape=out_shape,
        in_specs=[scalar_spec] + [vmem_spec] * len(operands),
        out_specs=[vmem_spec] * len(out_shape),
        scratch_shapes=[pltpu.VMEM((layers, width), jnp.float32)] * 2,
        compiler_params=pltpu.CompilerParams(vmem_limit_bytes=16 * 1024 * 1024),
        cost_estimate=light,
    )(scalars, *operands)


def line_plan(activations, out_grads, basis_act, basis_grad, owner_of, counts, state_act, state_grad):
    layers, tok_rows, width = activations.shape
    tile = basis_act.shape[1]
    n_dp = lax.axis_size("dp")
    n_own = lax.axis_size("owner")
    dp = lax.axis_index("dp")
    own = lax.axis_index("owner")
    scalars = jnp.concatenate([jnp.stack([dp, own]), counts, owner_of]).astype(jnp.int32)

    def after(array, *others):
        return lax.optimization_barrier((array, *others))[0]

    def step(arrays, *others):
        return lax.optimization_barrier((*arrays, *others))[: len(arrays)]

    def sent(cuts):
        return [flip(cut, "dp", mask) for mask, cut in enumerate(cuts, 1)]

    def pieces_of(gots, chips):
        return [
            [got, chip, flip(got, "owner", 1), flip(chip, "owner", 1)]
            for got, chip in zip(gots, chips, strict=True)
        ]

    cuts = cut_rows((out_grads, activations), tile, n_own, n_dp)
    got_grad = sent(cuts[: n_dp - 1])
    chips_grad = [flip(got, "owner", 2) for got in got_grad]
    got_act = sent(after(cut, *got_grad) for cut in cuts[n_dp - 1 :])
    pieces_grad = pieces_of(got_grad, chips_grad)
    pieces_grad[0][0] = after(pieces_grad[0][0], *got_act)
    keep, send = project_rows(scalars, out_grads, pieces_grad, basis_grad)

    owners = range(n_own)
    to_home = [((o ^ 1, o), (o, o)) for o in owners]
    swaps = [((a, o), (a ^ 1, o)) for a in range(n_dp) for o in owners if (a ^ o) & 2]
    near = hop(send, to_home + swaps)
    far = hop(keep, to_home)
    chips_act = [flip(after(got, keep), "owner", 2) for got in got_act]
    keep, send, near, far, *chips_act = step([keep, send, near, far, *chips_act])
    part = add(keep, near)
    rest = add(send, far)
    pieces_act = pieces_of(got_act, chips_act)
    pieces_act[0][0] = after(pieces_act[0][0], part, rest)
    keep_act, send_act = project_rows(scalars, activations, pieces_act, basis_act)
    near = hop(part, [((o ^ 2, o), (o, o)) for o in owners])
    far = hop(part, [((o ^ 3, o), (o, o)) for o in owners])
    near_act = flip(send_act, "dp", 1)

    part, rest, near, far, keep_act, near_act = step([part, rest, near, far, keep_act, near_act])
    part_act = add(keep_act, near_act)
    cross_act = flip(part_act, "dp", 2)
    part = add(part, near)
    rest = add(rest, far)
    to_chip = [((o, o), (o, o ^ 2)) for o in owners]
    part_chip = hop(part, to_chip)
    rest_chip = hop(rest, to_chip)

    part_act, cross_act, part, rest, part_chip, rest_chip = step(
        [part_act, cross_act, part, rest, part_chip, rest_chip]
    )
    full_act = add(part_act, cross_act)
    back_act = flip(full_act, "dp", 1)
    to_core = [((o, o ^ b), (o, o ^ b ^ 1)) for o in owners for b in (0, 2)]
    home = jnp.where(own == dp, 0, jnp.where(own == dp ^ 2, 1, 2)).astype(jnp.int32)[None]
    part_half, rest_half = pick(home, [(part, part_chip), (rest, rest_chip)])
    part_core = hop(part_half, to_core)
    rest_core = hop(rest_half, to_core)
    *grads, squares = settle_grads(home // 2, [(part_half, rest_half), (part_core, rest_core)])
    squares = [squares] + [flip(squares, "dp", mask) for mask in range(1, n_dp)]

    full_act, back_act, *squares = step([full_act, back_act, *squares])
    acts = [full_act, back_act]
    packet = settle_acts(state_act, state_grad, acts)
    packets = [packet] + [flip(packet, "owner", mask) for mask in range(1, n_own)]
    return tuple(finish(scalars, packets, squares, acts, grads, state_act.shape[0]))


def solution(mesh):
    placed = (
        P("groups", "dp", None),
        P("groups", "dp", None),
        P("groups", "dp", "owner"),
        P("groups", "dp", "owner"),
        P(),
        P("groups"),
        P("owner", "groups"),
        P("owner", "groups"),
    )
    square = mesh.shape["dp"] == 4 and mesh.shape["owner"] == 4
    return jax.shard_map(
        line_plan if square else gather_plan,
        mesh=mesh,
        in_specs=placed,
        out_specs=(P("groups", "dp", "owner"), P("owner", "groups"), P("owner", "groups")),
        check_vma=False,
    )
```

```python
import jax
import jax.numpy as jnp
from jax import lax
from jax.experimental import pallas as pl
from jax.experimental.pallas import tpu as pltpu
from jax.sharding import PartitionSpec as P

decay_rate = 0.25
damping_rate = 0.1
vmem_spec = pl.BlockSpec(memory_space=pltpu.VMEM)
scalar_spec = pl.BlockSpec(memory_space=pltpu.SMEM)
light = pl.CostEstimate(flops=0, bytes_accessed=0, transcendentals=0)


def spread(array, axis, root):
    mine = lax.axis_index(axis) == root
    return lax.psum(jnp.where(mine, array, jnp.zeros_like(array)), axis)


def gather_plan(activations, out_grads, basis_act, basis_grad, owner_of, counts, state_act, state_grad):
    layers = activations.shape[0]
    tok_rows = activations.shape[1]
    tile_rows = basis_act.shape[1]
    tile_cols = basis_act.shape[2]
    slot_count = state_act.shape[0]
    dp_index = lax.axis_index("dp")
    own_index = lax.axis_index("owner")
    valid_rows = (jnp.arange(tok_rows) < counts[dp_index]).astype(jnp.float32)[:, None]
    valid_total = jnp.sum(counts).astype(jnp.float32)
    square_acts = []
    square_grads = []
    gram_tiles = []
    for layer_index in range(layers):
        panel_act = jnp.dot(
            activations[layer_index],
            lax.all_gather(basis_act[layer_index], "dp", axis=0, tiled=True),
            preferred_element_type=jnp.float32,
        )
        panel_grad = jnp.dot(
            out_grads[layer_index],
            lax.all_gather(basis_grad[layer_index], "dp", axis=0, tiled=True),
            preferred_element_type=jnp.float32,
        )
        panel_act = (panel_act * valid_rows).astype(jnp.bfloat16)
        panel_grad = (panel_grad * valid_rows).astype(jnp.bfloat16)
        full_act = lax.all_gather(panel_act, "owner", axis=1, tiled=True)
        full_grad = lax.all_gather(panel_grad, "owner", axis=1, tiled=True)
        square_act = jnp.sum(jnp.square(full_act.astype(jnp.float32)), axis=0)
        square_grad = jnp.sum(jnp.square(full_grad.astype(jnp.float32)), axis=0)
        gram_term = lax.dot_general(
            full_grad, panel_act, (((0,), (0,)), ((), ())), preferred_element_type=jnp.float32
        )
        gram_tiles.append(
            lax.psum_scatter(
                gram_term.astype(jnp.bfloat16), "dp", scatter_dimension=0, tiled=True
            ).astype(jnp.float32)
            / valid_total
        )
        square_act, square_grad = lax.psum((square_act, square_grad), "dp")
        square_acts.append(square_act)
        square_grads.append(square_grad)
    new_act = state_act
    new_grad = state_grad
    results = []
    for layer_index in range(layers):
        owner_now = owner_of[layer_index]
        slot_rank = jnp.sum((owner_of[:layer_index] == owner_now).astype(jnp.int32))
        selector = (jnp.arange(slot_count) == slot_rank).astype(jnp.float32)[:, None]
        local_act = decay_rate * jnp.sum(state_act * selector, axis=0) + (
            1.0 - decay_rate
        ) * (square_acts[layer_index] / valid_total)
        local_grad = decay_rate * jnp.sum(state_grad * selector, axis=0) + (
            1.0 - decay_rate
        ) * (square_grads[layer_index] / valid_total)
        eigen_act = spread(local_act, "owner", owner_now)
        eigen_grad = spread(local_grad, "owner", owner_now)
        replace_rows = ((jnp.arange(slot_count) == slot_rank) & (own_index == owner_now))[:, None]
        new_act = jnp.where(replace_rows, eigen_act[None, :], new_act)
        new_grad = jnp.where(replace_rows, eigen_grad[None, :], new_grad)
        damping = damping_rate * jnp.mean(eigen_grad) * jnp.mean(eigen_act)
        grad_eigen = lax.dynamic_slice_in_dim(eigen_grad, dp_index * tile_rows, tile_rows)
        act_eigen = lax.dynamic_slice_in_dim(eigen_act, own_index * tile_cols, tile_cols)
        scaled = gram_tiles[layer_index] / (grad_eigen[:, None] * act_eigen[None, :] + damping)
        results.append(scaled.astype(jnp.bfloat16))
    return (jnp.stack(results), new_act, new_grad)


def flip(array, axis, mask):
    return lax.ppermute(array, axis, [(i, i ^ mask) for i in range(lax.axis_size(axis))])


def hop(array, pairs):
    owners = lax.axis_size("owner")
    flat = [(a * owners + b, c * owners + e) for (a, b), (c, e) in pairs]
    return lax.ppermute(array, ("dp", "owner"), flat)


def project_rows(scalars, tokens, pieces, basis, n_own, n_dp):
    layers, tok_rows, _ = tokens.shape
    tile, cols = basis.shape[1:]
    part_rows = tok_rows // n_own
    packed = 3 * n_dp * tok_rows // 4
    half = packed // 2
    shapes = [(layers, half, cols)] * 2

    def kernel(scalar_ref, tokens_hbm, basis_hbm, *refs):
        piece_refs, refs = refs[: len(pieces)], refs[len(pieces) :]
        out_refs, (tokens_ref, basis_ref, sems) = refs[: len(shapes)], refs[len(shapes) :]
        dp, own = scalar_ref[0], scalar_ref[1]
        at = pl.ds(pl.multiple_of(dp * tile, tile), tile)
        copies = []
        for layer in range(layers):
            copies.append(
                [
                    pltpu.make_async_copy(
                        tokens_hbm.at[layer, :, at], tokens_ref.at[layer], sems.at[2 * layer]
                    ),
                    pltpu.make_async_copy(basis_hbm.at[layer], basis_ref.at[layer], sems.at[2 * layer + 1]),
                ]
            )
            for copy in copies[-1]:
                copy.start()
        col = lax.broadcasted_iota(jnp.int32, (1, n_dp * tok_rows), 1)
        turn = (col - tok_rows) // part_rows
        peer = turn // (n_dp - 1)
        peer = own ^ (((peer & 1) << 1) | (peer >> 1))
        mine = col < tok_rows
        mask = jnp.where(mine, 0, turn % (n_dp - 1) + 1)
        index = jnp.where(mine, col, peer * part_rows + col % part_rows)
        place = jnp.full_like(col, -1)
        for number in range(n_dp):
            shard = dp ^ number
            start = jnp.int32(0)
            for other in range(n_dp):
                start += jnp.where(other < shard, scalar_ref[2 + other], 0)
            here = (mask == number) & (index < scalar_ref[2 + shard])
            place = jnp.where(here, start + index, place)
        row = lax.broadcasted_iota(jnp.int32, (packed, n_dp * tok_rows), 0)
        row = row + jnp.where(dp % 2 == 0, 0, jnp.where(row < half, half, -half))
        select = (row == place).astype(jnp.bfloat16)
        for layer in range(layers):
            copies[layer][0].wait()
            rows = jnp.concatenate([tokens_ref[layer]] + [p[layer] for p in piece_refs], axis=0)
            chosen = jnp.dot(select, rows, preferred_element_type=jnp.float32).astype(jnp.bfloat16)
            copies[layer][1].wait()
            result = jnp.dot(chosen, basis_ref[layer], preferred_element_type=jnp.float32).astype(
                jnp.bfloat16
            )
            out_refs[0][layer] = result[:half]
            out_refs[1][layer] = result[half:]

    return pl.pallas_call(
        kernel,
        out_shape=[jax.ShapeDtypeStruct(shape, jnp.bfloat16) for shape in shapes],
        in_specs=[scalar_spec] + [pl.BlockSpec(memory_space=pltpu.HBM)] * 2 + [vmem_spec] * len(pieces),
        out_specs=[vmem_spec] * len(shapes),
        scratch_shapes=[
            pltpu.VMEM((layers, tok_rows, tile), jnp.bfloat16),
            pltpu.VMEM((layers, tile, cols), jnp.bfloat16),
            pltpu.SemaphoreType.DMA((2 * layers,)),
        ],
        compiler_params=pltpu.CompilerParams(vmem_limit_bytes=16 * 1024 * 1024),
        cost_estimate=light,
    )(scalars, *[pltpu.with_memory_space_constraint(array, pltpu.HBM) for array in (tokens, basis)], *pieces)


def add(*pairs):
    layers = pairs[0][0].shape[0]

    def kernel(*refs):
        for number in range(len(pairs)):
            total = refs[2 * number][...].astype(jnp.float32) + refs[2 * number + 1][...].astype(jnp.float32)
            refs[-1][number * layers : (number + 1) * layers] = total.astype(refs[-1].dtype)

    first = pairs[0][0]
    return pl.pallas_call(
        kernel,
        out_shape=jax.ShapeDtypeStruct((layers * len(pairs), *first.shape[1:]), first.dtype),
        in_specs=[vmem_spec] * (2 * len(pairs)),
        out_specs=vmem_spec,
        compiler_params=pltpu.CompilerParams(vmem_limit_bytes=8 * 1024 * 1024),
        cost_estimate=light,
    )(*[array for pair in pairs for array in pair])


def join(arrays):
    layers, rows, cols = arrays[0].shape

    def kernel(*refs):
        for number, ref in enumerate(refs[:-1]):
            refs[-1][:, number * rows : (number + 1) * rows] = ref[...]

    return pl.pallas_call(
        kernel,
        out_shape=jax.ShapeDtypeStruct((layers, len(arrays) * rows, cols), arrays[0].dtype),
        in_specs=[vmem_spec] * len(arrays),
        out_specs=vmem_spec,
        compiler_params=pltpu.CompilerParams(vmem_limit_bytes=8 * 1024 * 1024),
        cost_estimate=light,
    )(*arrays)


def cut_rows(arrays, tile, n_own, n_dp):
    layers, tok_rows, _ = arrays[0].shape
    part_rows = tok_rows // n_own
    peers = n_dp - 1

    def kernel(*refs):
        in_refs, out_refs, sems = refs[: len(arrays)], refs[len(arrays) : -1], refs[-1]
        dp, own = lax.axis_index("dp"), lax.axis_index("owner")
        rows = pl.ds(pl.multiple_of(own * part_rows, part_rows), part_rows)
        copies = []
        for number, out_ref in enumerate(out_refs):
            block = dp ^ (number % peers + 1)
            cols = pl.ds(pl.multiple_of(block * tile, tile), tile)
            copies.append(
                pltpu.make_async_copy(in_refs[number // peers].at[:, rows, cols], out_ref, sems.at[number])
            )
            copies[-1].start()
        for copy in copies:
            copy.wait()

    count = len(arrays) * peers
    return pl.pallas_call(
        kernel,
        out_shape=[jax.ShapeDtypeStruct((layers, part_rows, tile), arrays[0].dtype)] * count,
        in_specs=[pl.BlockSpec(memory_space=pltpu.HBM)] * len(arrays),
        out_specs=[vmem_spec] * count,
        scratch_shapes=[pltpu.SemaphoreType.DMA((count,))],
        compiler_params=pltpu.CompilerParams(vmem_limit_bytes=8 * 1024 * 1024),
        cost_estimate=light,
    )(*[pltpu.with_memory_space_constraint(array, pltpu.HBM) for array in arrays])


def pick(home, choices):
    def kernel(home_ref, *refs):
        for index in range(len(choices)):

            @pl.when(home_ref[0] == index)
            def _(index=index):
                refs[-1][...] = refs[index][...]

    return pl.pallas_call(
        kernel,
        out_shape=jax.ShapeDtypeStruct(choices[0].shape, choices[0].dtype),
        in_specs=[scalar_spec] + [vmem_spec] * len(choices),
        out_specs=vmem_spec,
        compiler_params=pltpu.CompilerParams(vmem_limit_bytes=8 * 1024 * 1024),
        cost_estimate=light,
    )(home, *choices)


def squares_of(panel, layers):
    parts, _, cols = panel.shape

    def kernel(panel_ref, out_ref):
        for layer in range(layers):
            total = jnp.zeros((1, cols), jnp.float32)
            for part in range(layer, parts, layers):
                wide = panel_ref[part].astype(jnp.float32)
                total += jnp.sum(wide * wide, axis=0, keepdims=True)
            out_ref[layer : layer + 1] = total

    return pl.pallas_call(
        kernel,
        out_shape=jax.ShapeDtypeStruct((layers, cols), jnp.float32),
        in_specs=[vmem_spec],
        out_specs=vmem_spec,
        compiler_params=pltpu.CompilerParams(vmem_limit_bytes=8 * 1024 * 1024),
        cost_estimate=light,
    )(panel)


def packet_of(home, state_act, state_grad, act_halves, grads):
    slot_count, width = state_act.shape
    layers, cols = grads[0].shape
    arrays = [state_act, state_grad, *act_halves, *grads]

    def kernel(home_ref, *refs):
        packet_ref, refs = refs[-1], refs[:-1]
        packet_ref[:slot_count] = refs[0][...]
        packet_ref[slot_count : 2 * slot_count] = refs[1][...]
        packet_ref[2 * slot_count :] = jnp.zeros_like(packet_ref[2 * slot_count :])
        packet_ref[2 * slot_count : 2 * slot_count + layers, :cols] = refs[2][...] + refs[3][...]
        total = jnp.where(home_ref[0] == 0, refs[4][...], 0.0)
        for ref in refs[5:]:
            total += ref[...]
        packet_ref[2 * slot_count + layers :, :cols] = total

    return pl.pallas_call(
        kernel,
        out_shape=jax.ShapeDtypeStruct((2 * (slot_count + layers), width), jnp.float32),
        in_specs=[scalar_spec] + [vmem_spec] * len(arrays),
        out_specs=vmem_spec,
        compiler_params=pltpu.CompilerParams(vmem_limit_bytes=8 * 1024 * 1024),
        cost_estimate=light,
    )(home, *arrays)


def gram_of(grads, act):
    layers, _, cols = act.shape

    def kernel(grad_ref, act_ref, out_ref):
        for layer in range(layers):
            out_ref[layer] = product_of(grad_ref[layer], act_ref[layer])

    return pl.pallas_call(
        kernel,
        out_shape=jax.ShapeDtypeStruct((layers, grads.shape[2], cols), jnp.float32),
        in_specs=[vmem_spec] * 2,
        out_specs=vmem_spec,
        compiler_params=pltpu.CompilerParams(vmem_limit_bytes=16 * 1024 * 1024),
        cost_estimate=light,
    )(grads, act)


def product_of(grad, act):
    return lax.dot_general(grad, act, (((0,), (0,)), ((), ())), preferred_element_type=jnp.float32)


def finish(grads, act, grams, factors):
    layers, tile, cols = grams.shape

    def kernel(grad_ref, act_ref, gram_ref, factor_ref, out_ref):
        for layer in range(layers):
            gram = gram_ref[layer] + product_of(grad_ref[layers + layer], act_ref[layer])
            out_ref[layer] = (gram * factor_ref[layer]).astype(jnp.bfloat16)

    return pl.pallas_call(
        kernel,
        out_shape=jax.ShapeDtypeStruct((layers, tile, cols), jnp.bfloat16),
        in_specs=[vmem_spec] * 4,
        out_specs=vmem_spec,
        compiler_params=pltpu.CompilerParams(vmem_limit_bytes=24 * 1024 * 1024),
        cost_estimate=light,
    )(grads, act, grams, factors)


def eigenvalues(scalars, packets, layers, slot_count, n_dp, tile):
    n_own = len(packets)
    width = packets[0].shape[1]

    def kernel(scalar_ref, *refs):
        packet_refs, refs = refs[:n_own], refs[n_own:]
        out_ref, new_act_ref, new_grad_ref, act_full, grad_full = refs
        dp, own = scalar_ref[0], scalar_ref[1]
        total = scalar_ref[2]
        for index in range(1, n_dp):
            total += scalar_ref[2 + index]
        total = total.astype(jnp.float32)
        owners = [scalar_ref[2 + n_dp + layer] for layer in range(layers)]
        for mask in range(n_own):
            at = pl.ds(pl.multiple_of((own ^ mask) * tile, tile), tile)
            lower = 2 * slot_count + layers
            act_full[:, at] = packet_refs[mask][2 * slot_count : lower, :tile] / total
            grad_full[:, at] = packet_refs[mask][lower:, :tile] / total
        new_act_ref[...] = packet_refs[0][:slot_count]
        new_grad_ref[...] = packet_refs[0][slot_count : 2 * slot_count]
        for layer in range(layers):
            owner_now = owners[layer]
            rank = jnp.int32(0)
            for earlier in range(layer):
                rank += jnp.where(owners[earlier] == owner_now, 1, 0)
            old_act = jnp.zeros((1, width), jnp.float32)
            old_grad = jnp.zeros((1, width), jnp.float32)
            for mask in range(n_own):
                for slot in range(slot_count):
                    here = (owner_now == own ^ mask) & (rank == slot)
                    down = slot_count + slot
                    old_act = jnp.where(here, packet_refs[mask][slot : slot + 1], old_act)
                    old_grad = jnp.where(here, packet_refs[mask][down : down + 1], old_grad)
            eigen_act = decay_rate * old_act + (1.0 - decay_rate) * act_full[layer : layer + 1]
            eigen_grad = decay_rate * old_grad + (1.0 - decay_rate) * grad_full[layer : layer + 1]
            act_full[layer : layer + 1] = eigen_act
            grad_full[layer : layer + 1] = eigen_grad
            for slot in range(slot_count):

                @pl.when((owner_now == own) & (rank == slot))
                def _(slot=slot, eigen_act=eigen_act, eigen_grad=eigen_grad):
                    new_act_ref[slot : slot + 1] = eigen_act
                    new_grad_ref[slot : slot + 1] = eigen_grad

            damping = damping_rate * (jnp.sum(eigen_grad) / width) * (jnp.sum(eigen_act) / width)
            rows = grad_full[layer : layer + 1, pl.ds(pl.multiple_of(dp * tile, tile), tile)]
            cols = act_full[layer : layer + 1, pl.ds(pl.multiple_of(own * tile, tile), tile)]
            rows = jnp.transpose(jnp.broadcast_to(rows, (128, tile)))
            rows = jnp.concatenate([rows] * (tile // 128), axis=1)
            out_ref[layer] = 1.0 / (total * (rows * cols + damping))

    out_shape = [
        jax.ShapeDtypeStruct((layers, tile, tile), jnp.float32),
        jax.ShapeDtypeStruct((slot_count, width), jnp.float32),
        jax.ShapeDtypeStruct((slot_count, width), jnp.float32),
    ]
    return pl.pallas_call(
        kernel,
        out_shape=out_shape,
        in_specs=[scalar_spec] + [vmem_spec] * n_own,
        out_specs=[vmem_spec] * len(out_shape),
        scratch_shapes=[pltpu.VMEM((layers, width), jnp.float32)] * 2,
        compiler_params=pltpu.CompilerParams(vmem_limit_bytes=16 * 1024 * 1024),
        cost_estimate=light,
    )(scalars, *packets)


def line_plan(activations, out_grads, basis_act, basis_grad, owner_of, counts, state_act, state_grad):
    layers, tok_rows, width = activations.shape
    tile = basis_act.shape[1]
    n_dp = lax.axis_size("dp")
    n_own = lax.axis_size("owner")
    dp = lax.axis_index("dp")
    own = lax.axis_index("owner")
    scalars = jnp.concatenate([jnp.stack([dp, own]), counts, owner_of]).astype(jnp.int32)

    def after(array, *others):
        return lax.optimization_barrier((array, *others))[0]

    def step(arrays, *others):
        return lax.optimization_barrier((*arrays, *others))[: len(arrays)]

    cuts = cut_rows((out_grads, activations), tile, n_own, n_dp)
    cuts = [flip(cut, "dp", number % (n_dp - 1) + 1) for number, cut in enumerate(cuts)]
    got_grad, got_act = cuts[: n_dp - 1], cuts[n_dp - 1 :]
    pieces = got_grad[:-1] + [after(got_grad[-1], got_act[0])]
    pieces += [flip(piece, "owner", 2) for piece in pieces]
    pieces += [flip(piece, "owner", 1) for piece in pieces]
    keep, send = project_rows(scalars, out_grads, pieces, basis_grad, n_own, n_dp)

    owners = range(n_own)
    to_home = [((o ^ 1, o), (o, o)) for o in owners]
    swaps = [((a, o), (a ^ 1, o)) for a in range(n_dp) for o in owners if (a ^ o) & 2]
    near = hop(after(send, *got_act), to_home + swaps)
    far = hop(after(keep, *got_act), to_home)
    pieces = [join(got_act)]
    pieces += [flip(pieces[0], "owner", 2)]
    pieces += [flip(piece, "owner", 1) for piece in pieces]
    keep_act, send_act = project_rows(scalars, activations, pieces, basis_act, n_own, n_dp)

    keep, send, near, far, keep_act, send_act = step([keep, send, near, far, keep_act, send_act])
    part = add((keep, near))
    rest = add((send, far))
    near = hop(part, [((o ^ 2, o), (o, o)) for o in owners])
    far = hop(part, [((o ^ 3, o), (o, o)) for o in owners])
    near_act = flip(send_act, "dp", 1)

    part, rest, near, far, keep_act, near_act = step([part, rest, near, far, keep_act, near_act])
    part_act = add((keep_act, near_act))
    cross_act = flip(part_act, "dp", 2)
    full = add((after(part, part_act), near), (rest, far))
    chip = hop(full, [((o, o), (o, o ^ 2)) for o in owners])
    squares = [squares_of(full, layers)]
    squares += [hop(squares[0], [((o, o), (o ^ mask, o)) for o in owners]) for mask in range(1, n_dp)]

    part_act, cross_act, full, chip, *squares = step([part_act, cross_act, full, chip, *squares])
    full_act = add((part_act, cross_act))
    halves = [squares_of(full_act, layers)]
    halves += [flip(halves[0], "dp", 1)]
    home = jnp.where(own == dp, 0, jnp.where(own == dp ^ 2, 1, 2)).astype(jnp.int32)[None]
    packet = packet_of(home, state_act, state_grad, halves, squares)
    back_act = flip(after(full_act, packet), "dp", 1)
    full = pick(home, [after(full, packet), chip])
    core = hop(full, [((o, o ^ b), (o, o ^ b ^ 1)) for o in owners for b in (0, 2)])
    packets = [packet] + [flip(packet, "owner", mask) for mask in range(1, n_own)]
    factors, new_act, new_grad = eigenvalues(scalars, packets, layers, state_act.shape[0], n_dp, tile)
    grads = pick(home // 2, [full, core])
    grams = gram_of(grads, full_act)

    grads, grams, factors, back_act = step([grads, grams, factors, back_act])
    return finish(grads, back_act, grams, factors), new_act, new_grad


def solution(mesh):
    placed = (
        P("groups", "dp", None),
        P("groups", "dp", None),
        P("groups", "dp", "owner"),
        P("groups", "dp", "owner"),
        P(),
        P("groups"),
        P("owner", "groups"),
        P("owner", "groups"),
    )
    square = mesh.shape["dp"] == 4 and mesh.shape["owner"] == 4
    return jax.shard_map(
        line_plan if square else gather_plan,
        mesh=mesh,
        in_specs=placed,
        out_specs=(P("groups", "dp", "owner"), P("owner", "groups"), P("owner", "groups")),
        check_vma=False,
    )
```

```python
import jax
import jax.numpy as jnp
from jax import lax
from jax.experimental import pallas as pl
from jax.experimental.pallas import tpu as pltpu
from jax.sharding import PartitionSpec as P

decay_rate = 0.25
damping_rate = 0.1
vmem_spec = pl.BlockSpec(memory_space=pltpu.VMEM)
scalar_spec = pl.BlockSpec(memory_space=pltpu.SMEM)
light = pl.CostEstimate(flops=0, bytes_accessed=0, transcendentals=0)


def spread(array, axis, root):
    mine = lax.axis_index(axis) == root
    return lax.psum(jnp.where(mine, array, jnp.zeros_like(array)), axis)


def gather_plan(activations, out_grads, basis_act, basis_grad, owner_of, counts, state_act, state_grad):
    layers = activations.shape[0]
    tok_rows = activations.shape[1]
    tile_rows = basis_act.shape[1]
    tile_cols = basis_act.shape[2]
    slot_count = state_act.shape[0]
    dp_index = lax.axis_index("dp")
    own_index = lax.axis_index("owner")
    valid_rows = (jnp.arange(tok_rows) < counts[dp_index]).astype(jnp.float32)[:, None]
    valid_total = jnp.sum(counts).astype(jnp.float32)
    square_acts = []
    square_grads = []
    gram_tiles = []
    for layer_index in range(layers):
        panel_act = jnp.dot(
            activations[layer_index],
            lax.all_gather(basis_act[layer_index], "dp", axis=0, tiled=True),
            preferred_element_type=jnp.float32,
        )
        panel_grad = jnp.dot(
            out_grads[layer_index],
            lax.all_gather(basis_grad[layer_index], "dp", axis=0, tiled=True),
            preferred_element_type=jnp.float32,
        )
        panel_act = (panel_act * valid_rows).astype(jnp.bfloat16)
        panel_grad = (panel_grad * valid_rows).astype(jnp.bfloat16)
        full_act = lax.all_gather(panel_act, "owner", axis=1, tiled=True)
        full_grad = lax.all_gather(panel_grad, "owner", axis=1, tiled=True)
        square_act = jnp.sum(jnp.square(full_act.astype(jnp.float32)), axis=0)
        square_grad = jnp.sum(jnp.square(full_grad.astype(jnp.float32)), axis=0)
        gram_term = lax.dot_general(
            full_grad, panel_act, (((0,), (0,)), ((), ())), preferred_element_type=jnp.float32
        )
        gram_tiles.append(
            lax.psum_scatter(
                gram_term.astype(jnp.bfloat16), "dp", scatter_dimension=0, tiled=True
            ).astype(jnp.float32)
            / valid_total
        )
        square_act, square_grad = lax.psum((square_act, square_grad), "dp")
        square_acts.append(square_act)
        square_grads.append(square_grad)
    new_act = state_act
    new_grad = state_grad
    results = []
    for layer_index in range(layers):
        owner_now = owner_of[layer_index]
        slot_rank = jnp.sum((owner_of[:layer_index] == owner_now).astype(jnp.int32))
        selector = (jnp.arange(slot_count) == slot_rank).astype(jnp.float32)[:, None]
        local_act = decay_rate * jnp.sum(state_act * selector, axis=0) + (
            1.0 - decay_rate
        ) * (square_acts[layer_index] / valid_total)
        local_grad = decay_rate * jnp.sum(state_grad * selector, axis=0) + (
            1.0 - decay_rate
        ) * (square_grads[layer_index] / valid_total)
        eigen_act = spread(local_act, "owner", owner_now)
        eigen_grad = spread(local_grad, "owner", owner_now)
        replace_rows = ((jnp.arange(slot_count) == slot_rank) & (own_index == owner_now))[:, None]
        new_act = jnp.where(replace_rows, eigen_act[None, :], new_act)
        new_grad = jnp.where(replace_rows, eigen_grad[None, :], new_grad)
        damping = damping_rate * jnp.mean(eigen_grad) * jnp.mean(eigen_act)
        grad_eigen = lax.dynamic_slice_in_dim(eigen_grad, dp_index * tile_rows, tile_rows)
        act_eigen = lax.dynamic_slice_in_dim(eigen_act, own_index * tile_cols, tile_cols)
        scaled = gram_tiles[layer_index] / (grad_eigen[:, None] * act_eigen[None, :] + damping)
        results.append(scaled.astype(jnp.bfloat16))
    return (jnp.stack(results), new_act, new_grad)


def flip(array, axis, mask):
    return lax.ppermute(array, axis, [(i, i ^ mask) for i in range(lax.axis_size(axis))])


def hop(array, pairs):
    owners = lax.axis_size("owner")
    flat = [(a * owners + b, c * owners + e) for (a, b), (c, e) in pairs]
    return lax.ppermute(array, ("dp", "owner"), flat)


def project_rows(scalars, tokens, pieces, basis, n_own, n_dp):
    layers, tok_rows, _ = tokens.shape
    tile, cols = basis.shape[1:]
    part_rows = tok_rows // n_own
    packed = 3 * n_dp * tok_rows // 4
    half = packed // 2
    shapes = [(layers, half, cols)] * 2

    def kernel(scalar_ref, tokens_hbm, basis_hbm, *refs):
        piece_refs, refs = refs[: len(pieces)], refs[len(pieces) :]
        out_refs, (tokens_ref, basis_ref, sems) = refs[: len(shapes)], refs[len(shapes) :]
        dp, own = scalar_ref[0], scalar_ref[1]
        at = pl.ds(pl.multiple_of(dp * tile, tile), tile)
        copies = []
        for layer in range(layers):
            copies.append(
                [
                    pltpu.make_async_copy(
                        tokens_hbm.at[layer, :, at], tokens_ref.at[layer], sems.at[2 * layer]
                    ),
                    pltpu.make_async_copy(basis_hbm.at[layer], basis_ref.at[layer], sems.at[2 * layer + 1]),
                ]
            )
            for copy in copies[-1]:
                copy.start()
        col = lax.broadcasted_iota(jnp.int32, (1, n_dp * tok_rows), 1)
        turn = (col - tok_rows) // part_rows
        peer = turn // (n_dp - 1)
        peer = own ^ (((peer & 1) << 1) | (peer >> 1))
        mine = col < tok_rows
        mask = jnp.where(mine, 0, turn % (n_dp - 1) + 1)
        index = jnp.where(mine, col, peer * part_rows + col % part_rows)
        place = jnp.full_like(col, -1)
        for number in range(n_dp):
            shard = dp ^ number
            start = jnp.int32(0)
            for other in range(n_dp):
                start += jnp.where(other < shard, scalar_ref[2 + other], 0)
            here = (mask == number) & (index < scalar_ref[2 + shard])
            place = jnp.where(here, start + index, place)
        row = lax.broadcasted_iota(jnp.int32, (packed, n_dp * tok_rows), 0)
        row = row + jnp.where(dp % 2 == 0, 0, jnp.where(row < half, half, -half))
        select = (row == place).astype(jnp.bfloat16)
        for layer in range(layers):
            copies[layer][0].wait()
            rows = jnp.concatenate([tokens_ref[layer]] + [p[layer] for p in piece_refs], axis=0)
            chosen = jnp.dot(select, rows, preferred_element_type=jnp.float32).astype(jnp.bfloat16)
            copies[layer][1].wait()
            result = jnp.dot(chosen, basis_ref[layer], preferred_element_type=jnp.float32).astype(
                jnp.bfloat16
            )
            out_refs[0][layer] = result[:half]
            out_refs[1][layer] = result[half:]

    return pl.pallas_call(
        kernel,
        out_shape=[jax.ShapeDtypeStruct(shape, jnp.bfloat16) for shape in shapes],
        in_specs=[scalar_spec] + [pl.BlockSpec(memory_space=pltpu.HBM)] * 2 + [vmem_spec] * len(pieces),
        out_specs=[vmem_spec] * len(shapes),
        scratch_shapes=[
            pltpu.VMEM((layers, tok_rows, tile), jnp.bfloat16),
            pltpu.VMEM((layers, tile, cols), jnp.bfloat16),
            pltpu.SemaphoreType.DMA((2 * layers,)),
        ],
        compiler_params=pltpu.CompilerParams(vmem_limit_bytes=16 * 1024 * 1024),
        cost_estimate=light,
    )(scalars, *[pltpu.with_memory_space_constraint(array, pltpu.HBM) for array in (tokens, basis)], *pieces)


def add(*pairs):
    layers = pairs[0][0].shape[0]

    def kernel(*refs):
        for number in range(len(pairs)):
            total = refs[2 * number][...].astype(jnp.float32) + refs[2 * number + 1][...].astype(jnp.float32)
            refs[-1][number * layers : (number + 1) * layers] = total.astype(refs[-1].dtype)

    first = pairs[0][0]
    return pl.pallas_call(
        kernel,
        out_shape=jax.ShapeDtypeStruct((layers * len(pairs), *first.shape[1:]), first.dtype),
        in_specs=[vmem_spec] * (2 * len(pairs)),
        out_specs=vmem_spec,
        compiler_params=pltpu.CompilerParams(vmem_limit_bytes=8 * 1024 * 1024),
        cost_estimate=light,
    )(*[array for pair in pairs for array in pair])


def add_by_layer(*pairs):
    layers, height, cols = pairs[0][0].shape

    def kernel(*refs):
        in_refs, out_refs = refs[: 2 * len(pairs)], refs[2 * len(pairs) :]
        for layer in range(layers):
            for number in range(len(pairs)):
                near, far = [ref[layer].astype(jnp.float32) for ref in in_refs[2 * number : 2 * number + 2]]
                out_refs[layer][number] = (near + far).astype(out_refs[layer].dtype)

    return pl.pallas_call(
        kernel,
        out_shape=[jax.ShapeDtypeStruct((len(pairs), height, cols), pairs[0][0].dtype)] * layers,
        in_specs=[vmem_spec] * (2 * len(pairs)),
        out_specs=[vmem_spec] * layers,
        compiler_params=pltpu.CompilerParams(vmem_limit_bytes=8 * 1024 * 1024),
        cost_estimate=light,
    )(*[array for pair in pairs for array in pair])


def join(arrays):
    layers, rows, cols = arrays[0].shape

    def kernel(*refs):
        for number, ref in enumerate(refs[:-1]):
            refs[-1][:, number * rows : (number + 1) * rows] = ref[...]

    return pl.pallas_call(
        kernel,
        out_shape=jax.ShapeDtypeStruct((layers, len(arrays) * rows, cols), arrays[0].dtype),
        in_specs=[vmem_spec] * len(arrays),
        out_specs=vmem_spec,
        compiler_params=pltpu.CompilerParams(vmem_limit_bytes=8 * 1024 * 1024),
        cost_estimate=light,
    )(*arrays)


def cut_rows(arrays, tile, n_own, n_dp):
    layers, tok_rows, _ = arrays[0].shape
    part_rows = tok_rows // n_own
    peers = n_dp - 1

    def kernel(*refs):
        in_refs, out_refs, sems = refs[: len(arrays)], refs[len(arrays) : -1], refs[-1]
        dp, own = lax.axis_index("dp"), lax.axis_index("owner")
        rows = pl.ds(pl.multiple_of(own * part_rows, part_rows), part_rows)
        copies = []
        for number, out_ref in enumerate(out_refs):
            block = dp ^ (number % peers + 1)
            cols = pl.ds(pl.multiple_of(block * tile, tile), tile)
            copies.append(
                pltpu.make_async_copy(in_refs[number // peers].at[:, rows, cols], out_ref, sems.at[number])
            )
            copies[-1].start()
        for copy in copies:
            copy.wait()

    count = len(arrays) * peers
    return pl.pallas_call(
        kernel,
        out_shape=[jax.ShapeDtypeStruct((layers, part_rows, tile), arrays[0].dtype)] * count,
        in_specs=[pl.BlockSpec(memory_space=pltpu.HBM)] * len(arrays),
        out_specs=[vmem_spec] * count,
        scratch_shapes=[pltpu.SemaphoreType.DMA((count,))],
        compiler_params=pltpu.CompilerParams(vmem_limit_bytes=8 * 1024 * 1024),
        cost_estimate=light,
    )(*[pltpu.with_memory_space_constraint(array, pltpu.HBM) for array in arrays])


def pick(home, choices):
    flat = [array for arrays in choices for array in arrays]
    count = len(choices[0])

    def kernel(home_ref, *refs):
        for index in range(count):

            @pl.when(home_ref[0] == index)
            def _(index=index):
                for number, out_ref in enumerate(refs[len(flat) :]):
                    out_ref[...] = refs[number * count + index][...]

    return pl.pallas_call(
        kernel,
        out_shape=[jax.ShapeDtypeStruct(arrays[0].shape, arrays[0].dtype) for arrays in choices],
        in_specs=[scalar_spec] + [vmem_spec] * len(flat),
        out_specs=[vmem_spec] * len(choices),
        compiler_params=pltpu.CompilerParams(vmem_limit_bytes=12 * 1024 * 1024),
        cost_estimate=light,
    )(home, *flat)


def squares_of(panels, by_layer):
    layers = len(panels) if by_layer else panels[0].shape[0]
    cols = panels[0].shape[2]

    def kernel(*refs):
        for layer in range(layers):
            parts = [refs[layer][at] for at in range(panels[0].shape[0])] if by_layer else [refs[0][layer]]
            wide = [part.astype(jnp.float32) for part in parts]
            total = sum(part * part for part in wide)
            refs[-1][layer : layer + 1] = jnp.sum(total, axis=0, keepdims=True)

    return pl.pallas_call(
        kernel,
        out_shape=jax.ShapeDtypeStruct((layers, cols), jnp.float32),
        in_specs=[vmem_spec] * len(panels),
        out_specs=vmem_spec,
        compiler_params=pltpu.CompilerParams(vmem_limit_bytes=8 * 1024 * 1024),
        cost_estimate=light,
    )(*panels)


def packet_of(home, act_halves, grads):
    layers, cols = grads[0].shape
    arrays = [*act_halves, *grads]

    def kernel(home_ref, *refs):
        refs[-1][:layers] = refs[0][...] + refs[1][...]
        total = jnp.where(home_ref[0] == 0, refs[2][...], 0.0)
        for ref in refs[3:-1]:
            total += ref[...]
        refs[-1][layers:] = total

    return pl.pallas_call(
        kernel,
        out_shape=jax.ShapeDtypeStruct((2 * layers, cols), jnp.float32),
        in_specs=[scalar_spec] + [vmem_spec] * len(arrays),
        out_specs=vmem_spec,
        compiler_params=pltpu.CompilerParams(vmem_limit_bytes=8 * 1024 * 1024),
        cost_estimate=light,
    )(home, *arrays)


def gram_of(grads, act):
    layers, _, cols = act.shape

    def kernel(*refs):
        for layer in range(layers):
            refs[-1][layer] = product_of(refs[layer][0], refs[-2][layer])

    return pl.pallas_call(
        kernel,
        out_shape=jax.ShapeDtypeStruct((layers, grads[0].shape[2], cols), jnp.float32),
        in_specs=[vmem_spec] * (layers + 1),
        out_specs=vmem_spec,
        compiler_params=pltpu.CompilerParams(vmem_limit_bytes=16 * 1024 * 1024),
        cost_estimate=light,
    )(*grads, act)


def product_of(grad, act):
    return lax.dot_general(grad, act, (((0,), (0,)), ((), ())), preferred_element_type=jnp.float32)


def finish(grads, act, grams, factors):
    layers, tile, cols = grams.shape

    def kernel(*refs):
        grad_refs, (act_ref, gram_ref, factor_ref, out_ref) = refs[:layers], refs[layers:]
        for layer in range(layers):
            gram = gram_ref[layer] + product_of(grad_refs[layer][1], act_ref[layer])
            out_ref[layer] = (gram * factor_ref[layer]).astype(jnp.bfloat16)

    return pl.pallas_call(
        kernel,
        out_shape=jax.ShapeDtypeStruct((layers, tile, cols), jnp.bfloat16),
        in_specs=[vmem_spec] * (layers + 3),
        out_specs=vmem_spec,
        compiler_params=pltpu.CompilerParams(vmem_limit_bytes=24 * 1024 * 1024),
        cost_estimate=light,
    )(*grads, act, grams, factors)


def eigenvalues(scalars, states, packets, n_dp):
    n_own = len(packets)
    layers, tile = packets[0].shape[0] // 2, packets[0].shape[1]
    slot_count, width = states[0].shape[0] // 2, states[0].shape[1]

    def kernel(scalar_ref, *refs):
        state_refs, packet_refs, refs = refs[:n_own], refs[n_own : 2 * n_own], refs[2 * n_own :]
        out_ref, new_act_ref, new_grad_ref, act_full, grad_full = refs
        dp, own = scalar_ref[0], scalar_ref[1]
        total = scalar_ref[2]
        for index in range(1, n_dp):
            total += scalar_ref[2 + index]
        total = total.astype(jnp.float32)
        owners = [scalar_ref[2 + n_dp + layer] for layer in range(layers)]
        for mask in range(n_own):
            at = pl.ds(pl.multiple_of((own ^ mask) * tile, tile), tile)
            act_full[:, at] = packet_refs[mask][:layers] / total
            grad_full[:, at] = packet_refs[mask][layers:] / total
        new_act_ref[...] = state_refs[0][:slot_count]
        new_grad_ref[...] = state_refs[0][slot_count:]
        for layer in range(layers):
            owner_now = owners[layer]
            rank = jnp.int32(0)
            for earlier in range(layer):
                rank += jnp.where(owners[earlier] == owner_now, 1, 0)
            old_act = jnp.zeros((1, width), jnp.float32)
            old_grad = jnp.zeros((1, width), jnp.float32)
            for mask in range(n_own):
                for slot in range(slot_count):
                    here = (owner_now == own ^ mask) & (rank == slot)
                    down = slot_count + slot
                    old_act = jnp.where(here, state_refs[mask][slot : slot + 1], old_act)
                    old_grad = jnp.where(here, state_refs[mask][down : down + 1], old_grad)
            eigen_act = decay_rate * old_act + (1.0 - decay_rate) * act_full[layer : layer + 1]
            eigen_grad = decay_rate * old_grad + (1.0 - decay_rate) * grad_full[layer : layer + 1]
            act_full[layer : layer + 1] = eigen_act
            grad_full[layer : layer + 1] = eigen_grad
            for slot in range(slot_count):

                @pl.when((owner_now == own) & (rank == slot))
                def _(slot=slot, eigen_act=eigen_act, eigen_grad=eigen_grad):
                    new_act_ref[slot : slot + 1] = eigen_act
                    new_grad_ref[slot : slot + 1] = eigen_grad

            damping = damping_rate * (jnp.sum(eigen_grad) / width) * (jnp.sum(eigen_act) / width)
            rows = grad_full[layer : layer + 1, pl.ds(pl.multiple_of(dp * tile, tile), tile)]
            cols = act_full[layer : layer + 1, pl.ds(pl.multiple_of(own * tile, tile), tile)]
            rows = jnp.transpose(jnp.broadcast_to(rows, (128, tile)))
            rows = jnp.concatenate([rows] * (tile // 128), axis=1)
            out_ref[layer] = 1.0 / (total * (rows * cols + damping))

    out_shape = [
        jax.ShapeDtypeStruct((layers, tile, tile), jnp.float32),
        jax.ShapeDtypeStruct((slot_count, width), jnp.float32),
        jax.ShapeDtypeStruct((slot_count, width), jnp.float32),
    ]
    return pl.pallas_call(
        kernel,
        out_shape=out_shape,
        in_specs=[scalar_spec] + [vmem_spec] * (2 * n_own),
        out_specs=[vmem_spec] * len(out_shape),
        scratch_shapes=[pltpu.VMEM((layers, width), jnp.float32)] * 2,
        compiler_params=pltpu.CompilerParams(vmem_limit_bytes=16 * 1024 * 1024),
        cost_estimate=light,
    )(scalars, *states, *packets)


def line_plan(activations, out_grads, basis_act, basis_grad, owner_of, counts, state_act, state_grad):
    layers, tok_rows, width = activations.shape
    tile = basis_act.shape[1]
    n_dp = lax.axis_size("dp")
    n_own = lax.axis_size("owner")
    dp = lax.axis_index("dp")
    own = lax.axis_index("owner")
    scalars = jnp.concatenate([jnp.stack([dp, own]), counts, owner_of]).astype(jnp.int32)

    def after(array, *others):
        return lax.optimization_barrier((array, *others))[0]

    def step(arrays, *others):
        return lax.optimization_barrier((*arrays, *others))[: len(arrays)]

    cuts = cut_rows((out_grads, activations), tile, n_own, n_dp)
    cuts = [flip(cut, "dp", number % (n_dp - 1) + 1) for number, cut in enumerate(cuts)]
    got_grad, got_act = cuts[: n_dp - 1], cuts[n_dp - 1 :]
    pieces = got_grad[:-1] + [after(got_grad[-1], got_act[0])]
    pieces += [flip(piece, "owner", 2) for piece in pieces]
    pieces += [flip(piece, "owner", 1) for piece in pieces]
    keep, send = project_rows(scalars, out_grads, pieces, basis_grad, n_own, n_dp)

    owners = range(n_own)
    to_home = [((o ^ 1, o), (o, o)) for o in owners]
    swaps = [((a, o), (a ^ 1, o)) for a in range(n_dp) for o in owners if (a ^ o) & 2]
    near = hop(after(send, *got_act), to_home + swaps)
    far = hop(after(keep, *got_act), to_home)
    pieces = [join(got_act)]
    pieces += [flip(pieces[0], "owner", 2)]
    pieces += [flip(piece, "owner", 1) for piece in pieces]
    keep_act, send_act = project_rows(scalars, activations, pieces, basis_act, n_own, n_dp)

    state = after(jnp.concatenate([state_act, state_grad], axis=0), keep)
    states = [state] + [flip(state, "owner", mask) for mask in range(1, n_own)]

    keep, send, near, far, keep_act, send_act, *states = step([keep, send, near, far, keep_act, send_act, *states])
    part = add((keep, near))
    rest = add((send, far))
    near = hop(part, [((o ^ 2, o), (o, o)) for o in owners])
    far = hop(part, [((o ^ 3, o), (o, o)) for o in owners])
    near_act = flip(send_act, "dp", 1)

    part, rest, near, far, keep_act, near_act = step([part, rest, near, far, keep_act, near_act])
    part_act = add((keep_act, near_act))
    cross_act = flip(part_act, "dp", 2)
    full = add_by_layer((part, near), (rest, far))
    chip = [hop(array, [((o, o), (o, o ^ 2)) for o in owners]) for array in full]
    squares = [squares_of(full, True)]
    squares += [hop(squares[0], [((o, o), (o ^ mask, o)) for o in owners]) for mask in range(1, n_dp)]

    done = step([part_act, cross_act, *full, *chip, *squares])
    (part_act, cross_act), full, chip, squares = done[:2], done[2:][:layers], done[2 + layers :][:layers], done[2 + 2 * layers :]
    full_act = add((part_act, cross_act))
    halves = [squares_of([full_act], False)]
    halves += [flip(halves[0], "dp", 1)]
    home = jnp.where(own == dp, 0, jnp.where(own == dp ^ 2, 1, 2)).astype(jnp.int32)[None]
    packet = packet_of(home, halves, squares)
    back_act = flip(after(full_act, packet), "dp", 1)
    packets = [packet] + [flip(packet, "owner", mask) for mask in range(1, n_own)]
    full = pick(after(home, *packets), [*zip(full, chip, strict=True)])
    core = [hop(array, [((o, o ^ b), (o, o ^ b ^ 1)) for o in owners for b in (0, 2)]) for array in full]
    factors, new_act, new_grad = eigenvalues(scalars, states, packets, n_dp)
    grads = pick(home // 2, [*zip(full, core, strict=True)])
    grams = gram_of(grads, full_act)

    grams, factors, back_act, *grads = step([grams, factors, back_act, *grads])
    return finish(grads, back_act, grams, factors), new_act, new_grad


def solution(mesh):
    placed = (
        P("groups", "dp", None),
        P("groups", "dp", None),
        P("groups", "dp", "owner"),
        P("groups", "dp", "owner"),
        P(),
        P("groups"),
        P("owner", "groups"),
        P("owner", "groups"),
    )
    square = mesh.shape["dp"] == 4 and mesh.shape["owner"] == 4
    return jax.shard_map(
        line_plan if square else gather_plan,
        mesh=mesh,
        in_specs=placed,
        out_specs=(P("groups", "dp", "owner"), P("owner", "groups"), P("owner", "groups")),
        check_vma=False,
    )
```

```python
import jax
import jax.numpy as jnp
from jax import lax
from jax.experimental import pallas as pl
from jax.experimental.pallas import tpu as pltpu
from jax.sharding import PartitionSpec as P

decay_rate = 0.25
damping_rate = 0.1
vmem_spec = pl.BlockSpec(memory_space=pltpu.VMEM)
scalar_spec = pl.BlockSpec(memory_space=pltpu.SMEM)
light = pl.CostEstimate(flops=0, bytes_accessed=0, transcendentals=0)


def spread(array, axis, root):
    mine = lax.axis_index(axis) == root
    return lax.psum(jnp.where(mine, array, jnp.zeros_like(array)), axis)


def gather_plan(activations, out_grads, basis_act, basis_grad, owner_of, counts, state_act, state_grad):
    layers = activations.shape[0]
    tok_rows = activations.shape[1]
    tile_rows = basis_act.shape[1]
    tile_cols = basis_act.shape[2]
    slot_count = state_act.shape[0]
    dp_index = lax.axis_index("dp")
    own_index = lax.axis_index("owner")
    valid_rows = (jnp.arange(tok_rows) < counts[dp_index]).astype(jnp.float32)[:, None]
    valid_total = jnp.sum(counts).astype(jnp.float32)
    square_acts = []
    square_grads = []
    gram_tiles = []
    for layer_index in range(layers):
        panel_act = jnp.dot(
            activations[layer_index],
            lax.all_gather(basis_act[layer_index], "dp", axis=0, tiled=True),
            preferred_element_type=jnp.float32,
        )
        panel_grad = jnp.dot(
            out_grads[layer_index],
            lax.all_gather(basis_grad[layer_index], "dp", axis=0, tiled=True),
            preferred_element_type=jnp.float32,
        )
        panel_act = (panel_act * valid_rows).astype(jnp.bfloat16)
        panel_grad = (panel_grad * valid_rows).astype(jnp.bfloat16)
        full_act = lax.all_gather(panel_act, "owner", axis=1, tiled=True)
        full_grad = lax.all_gather(panel_grad, "owner", axis=1, tiled=True)
        square_act = jnp.sum(jnp.square(full_act.astype(jnp.float32)), axis=0)
        square_grad = jnp.sum(jnp.square(full_grad.astype(jnp.float32)), axis=0)
        gram_term = lax.dot_general(
            full_grad, panel_act, (((0,), (0,)), ((), ())), preferred_element_type=jnp.float32
        )
        gram_tiles.append(
            lax.psum_scatter(
                gram_term.astype(jnp.bfloat16), "dp", scatter_dimension=0, tiled=True
            ).astype(jnp.float32)
            / valid_total
        )
        square_act, square_grad = lax.psum((square_act, square_grad), "dp")
        square_acts.append(square_act)
        square_grads.append(square_grad)
    new_act = state_act
    new_grad = state_grad
    results = []
    for layer_index in range(layers):
        owner_now = owner_of[layer_index]
        slot_rank = jnp.sum((owner_of[:layer_index] == owner_now).astype(jnp.int32))
        selector = (jnp.arange(slot_count) == slot_rank).astype(jnp.float32)[:, None]
        local_act = decay_rate * jnp.sum(state_act * selector, axis=0) + (
            1.0 - decay_rate
        ) * (square_acts[layer_index] / valid_total)
        local_grad = decay_rate * jnp.sum(state_grad * selector, axis=0) + (
            1.0 - decay_rate
        ) * (square_grads[layer_index] / valid_total)
        eigen_act = spread(local_act, "owner", owner_now)
        eigen_grad = spread(local_grad, "owner", owner_now)
        replace_rows = ((jnp.arange(slot_count) == slot_rank) & (own_index == owner_now))[:, None]
        new_act = jnp.where(replace_rows, eigen_act[None, :], new_act)
        new_grad = jnp.where(replace_rows, eigen_grad[None, :], new_grad)
        damping = damping_rate * jnp.mean(eigen_grad) * jnp.mean(eigen_act)
        grad_eigen = lax.dynamic_slice_in_dim(eigen_grad, dp_index * tile_rows, tile_rows)
        act_eigen = lax.dynamic_slice_in_dim(eigen_act, own_index * tile_cols, tile_cols)
        scaled = gram_tiles[layer_index] / (grad_eigen[:, None] * act_eigen[None, :] + damping)
        results.append(scaled.astype(jnp.bfloat16))
    return (jnp.stack(results), new_act, new_grad)


def flip(array, axis, mask):
    return lax.ppermute(array, axis, [(i, i ^ mask) for i in range(lax.axis_size(axis))])


def hop(array, pairs):
    owners = lax.axis_size("owner")
    flat = [(a * owners + b, c * owners + e) for (a, b), (c, e) in pairs]
    return lax.ppermute(array, ("dp", "owner"), flat)


def project_rows(scalars, tokens, pieces, basis, n_own, n_dp):
    layers, tok_rows, _ = tokens.shape
    tile, cols = basis.shape[1:]
    part_rows = tok_rows // n_own
    packed = 3 * n_dp * tok_rows // 4
    half = packed // 2
    shapes = [(layers, half, cols)] * 2

    def kernel(scalar_ref, tokens_hbm, basis_hbm, *refs):
        piece_refs, refs = refs[: len(pieces)], refs[len(pieces) :]
        out_refs, (tokens_ref, basis_ref, sems) = refs[: len(shapes)], refs[len(shapes) :]
        dp, own = scalar_ref[0], scalar_ref[1]
        at = pl.ds(pl.multiple_of(dp * tile, tile), tile)
        copies = []
        for layer in range(layers):
            copies.append(
                [
                    pltpu.make_async_copy(
                        tokens_hbm.at[layer, :, at], tokens_ref.at[layer], sems.at[2 * layer]
                    ),
                    pltpu.make_async_copy(basis_hbm.at[layer], basis_ref.at[layer], sems.at[2 * layer + 1]),
                ]
            )
            for copy in copies[-1]:
                copy.start()
        col = lax.broadcasted_iota(jnp.int32, (1, n_dp * tok_rows), 1)
        turn = (col - tok_rows) // part_rows
        peer = turn // (n_dp - 1)
        peer = own ^ (((peer & 1) << 1) | (peer >> 1))
        mine = col < tok_rows
        mask = jnp.where(mine, 0, turn % (n_dp - 1) + 1)
        index = jnp.where(mine, col, peer * part_rows + col % part_rows)
        place = jnp.full_like(col, -1)
        for number in range(n_dp):
            shard = dp ^ number
            start = jnp.int32(0)
            for other in range(n_dp):
                start += jnp.where(other < shard, scalar_ref[2 + other], 0)
            here = (mask == number) & (index < scalar_ref[2 + shard])
            place = jnp.where(here, start + index, place)
        row = lax.broadcasted_iota(jnp.int32, (packed, n_dp * tok_rows), 0)
        row = row + jnp.where(dp % 2 == 0, 0, jnp.where(row < half, half, -half))
        select = (row == place).astype(jnp.bfloat16)
        for layer in range(layers):
            copies[layer][0].wait()
            rows = jnp.concatenate([tokens_ref[layer]] + [p[layer] for p in piece_refs], axis=0)
            chosen = jnp.dot(select, rows, preferred_element_type=jnp.float32).astype(jnp.bfloat16)
            copies[layer][1].wait()
            result = jnp.dot(chosen, basis_ref[layer], preferred_element_type=jnp.float32).astype(
                jnp.bfloat16
            )
            out_refs[0][layer] = result[:half]
            out_refs[1][layer] = result[half:]

    return pl.pallas_call(
        kernel,
        out_shape=[jax.ShapeDtypeStruct(shape, jnp.bfloat16) for shape in shapes],
        in_specs=[scalar_spec] + [pl.BlockSpec(memory_space=pltpu.HBM), pl.BlockSpec(memory_space=pl.ANY)] + [vmem_spec] * len(pieces),
        out_specs=[vmem_spec] * len(shapes),
        scratch_shapes=[
            pltpu.VMEM((layers, tok_rows, tile), jnp.bfloat16),
            pltpu.VMEM((layers, tile, cols), jnp.bfloat16),
            pltpu.SemaphoreType.DMA((2 * layers,)),
        ],
        compiler_params=pltpu.CompilerParams(vmem_limit_bytes=16 * 1024 * 1024),
        cost_estimate=light,
    )(scalars, pltpu.with_memory_space_constraint(tokens, pltpu.HBM), basis, *pieces)


def add(*pairs):
    layers = pairs[0][0].shape[0]

    def kernel(*refs):
        for number in range(len(pairs)):
            total = refs[2 * number][...].astype(jnp.float32) + refs[2 * number + 1][...].astype(jnp.float32)
            refs[-1][number * layers : (number + 1) * layers] = total.astype(refs[-1].dtype)

    first = pairs[0][0]
    return pl.pallas_call(
        kernel,
        out_shape=jax.ShapeDtypeStruct((layers * len(pairs), *first.shape[1:]), first.dtype),
        in_specs=[vmem_spec] * (2 * len(pairs)),
        out_specs=vmem_spec,
        compiler_params=pltpu.CompilerParams(vmem_limit_bytes=8 * 1024 * 1024),
        cost_estimate=light,
    )(*[array for pair in pairs for array in pair])


def add_rows(pairs, cut=None):
    layers, height, cols = pairs[0][0].shape
    spans = [(0, cut), (cut, height)] if cut else [(n * height, (n + 1) * height) for n in range(len(pairs))]

    def kernel(*refs):
        out_refs = refs[2 * len(pairs) :]
        for number, (start, stop) in enumerate(spans):
            if cut:
                total = refs[0][:, start:stop].astype(jnp.float32) + refs[1][:, start:stop].astype(jnp.float32)
                out_refs[number][...] = total.astype(out_refs[number].dtype)
            else:
                total = refs[2 * number][...].astype(jnp.float32) + refs[2 * number + 1][...].astype(jnp.float32)
                out_refs[0][:, start:stop] = total.astype(out_refs[0].dtype)

    heights = [stop - start for start, stop in spans] if cut else [spans[-1][1]]
    return pl.pallas_call(
        kernel,
        out_shape=[jax.ShapeDtypeStruct((layers, rows, cols), pairs[0][0].dtype) for rows in heights],
        in_specs=[vmem_spec] * (2 * len(pairs)),
        out_specs=[vmem_spec] * len(heights),
        compiler_params=pltpu.CompilerParams(vmem_limit_bytes=8 * 1024 * 1024),
        cost_estimate=light,
    )(*[array for pair in pairs for array in pair])


def by_layer(near, far):
    layers, height, cols = near.shape

    def kernel(near_ref, far_ref, *out_refs):
        for layer, out_ref in enumerate(out_refs):
            out_ref[0] = near_ref[layer]
            out_ref[1] = far_ref[layer]

    return pl.pallas_call(
        kernel,
        out_shape=[jax.ShapeDtypeStruct((2, height, cols), near.dtype)] * layers,
        in_specs=[vmem_spec] * 2,
        out_specs=[vmem_spec] * layers,
        compiler_params=pltpu.CompilerParams(vmem_limit_bytes=8 * 1024 * 1024),
        cost_estimate=light,
    )(near, far)


def join(arrays):
    layers, rows, cols = arrays[0].shape

    def kernel(*refs):
        for number, ref in enumerate(refs[:-1]):
            refs[-1][:, number * rows : (number + 1) * rows] = ref[...]

    return pl.pallas_call(
        kernel,
        out_shape=jax.ShapeDtypeStruct((layers, len(arrays) * rows, cols), arrays[0].dtype),
        in_specs=[vmem_spec] * len(arrays),
        out_specs=vmem_spec,
        compiler_params=pltpu.CompilerParams(vmem_limit_bytes=8 * 1024 * 1024),
        cost_estimate=light,
    )(*arrays)


def cut_rows(arrays, tile, n_own, n_dp):
    layers, tok_rows, _ = arrays[0].shape
    part_rows = tok_rows // n_own
    peers = n_dp - 1

    def kernel(*refs):
        in_refs, out_refs, sems = refs[: len(arrays)], refs[len(arrays) : -1], refs[-1]
        dp, own = lax.axis_index("dp"), lax.axis_index("owner")
        rows = pl.ds(pl.multiple_of(own * part_rows, part_rows), part_rows)
        copies = []
        for number, out_ref in enumerate(out_refs):
            block = dp ^ (number % peers + 1)
            cols = pl.ds(pl.multiple_of(block * tile, tile), tile)
            copies.append(
                pltpu.make_async_copy(in_refs[number // peers].at[:, rows, cols], out_ref, sems.at[number])
            )
            copies[-1].start()
        for copy in copies:
            copy.wait()

    count = len(arrays) * peers
    return pl.pallas_call(
        kernel,
        out_shape=[jax.ShapeDtypeStruct((layers, part_rows, tile), arrays[0].dtype)] * count,
        in_specs=[pl.BlockSpec(memory_space=pltpu.HBM)] * len(arrays),
        out_specs=[vmem_spec] * count,
        scratch_shapes=[pltpu.SemaphoreType.DMA((count,))],
        compiler_params=pltpu.CompilerParams(vmem_limit_bytes=8 * 1024 * 1024),
        cost_estimate=light,
    )(*[pltpu.with_memory_space_constraint(array, pltpu.HBM) for array in arrays])


def pick(home, choices):
    flat = [array for arrays in choices for array in arrays]
    count = len(choices[0])

    def kernel(home_ref, *refs):
        for index in range(count):

            @pl.when(home_ref[0] == index)
            def _(index=index):
                for number, out_ref in enumerate(refs[len(flat) :]):
                    out_ref[...] = refs[number * count + index][...]

    return pl.pallas_call(
        kernel,
        out_shape=[jax.ShapeDtypeStruct(arrays[0].shape, arrays[0].dtype) for arrays in choices],
        in_specs=[scalar_spec] + [vmem_spec] * len(flat),
        out_specs=[vmem_spec] * len(choices),
        compiler_params=pltpu.CompilerParams(vmem_limit_bytes=12 * 1024 * 1024),
        cost_estimate=light,
    )(home, *flat)


def squares_of(aside, panel):
    layers, _, cols = panel.shape

    def kernel(aside_ref, panel_ref, out_ref):
        for layer in range(layers):
            wide = panel_ref[layer].astype(jnp.float32)
            total = jnp.sum(wide * wide, axis=0, keepdims=True)
            out_ref[layer : layer + 1] = jnp.where(aside_ref[0] == 0, total, 0.0)

    return pl.pallas_call(
        kernel,
        out_shape=jax.ShapeDtypeStruct((layers, cols), jnp.float32),
        in_specs=[scalar_spec, vmem_spec],
        out_specs=vmem_spec,
        compiler_params=pltpu.CompilerParams(vmem_limit_bytes=8 * 1024 * 1024),
        cost_estimate=light,
    )(aside, panel)


def total_of(arrays):
    def kernel(*refs):
        refs[-1][...] = (refs[0][...] + refs[1][...]) + (refs[2][...] + refs[3][...])

    return pl.pallas_call(
        kernel,
        out_shape=jax.ShapeDtypeStruct(arrays[0].shape, arrays[0].dtype),
        in_specs=[vmem_spec] * len(arrays),
        out_specs=vmem_spec,
        compiler_params=pltpu.CompilerParams(vmem_limit_bytes=4 * 1024 * 1024),
        cost_estimate=light,
    )(*arrays)


def packet_of(acts, grad):
    layers, cols = grad.shape

    def kernel(near_ref, far_ref, grad_ref, out_ref):
        out_ref[:layers] = near_ref[...] + far_ref[...]
        out_ref[layers:] = grad_ref[...]

    return pl.pallas_call(
        kernel,
        out_shape=jax.ShapeDtypeStruct((2 * layers, cols), jnp.float32),
        in_specs=[vmem_spec] * 3,
        out_specs=vmem_spec,
        compiler_params=pltpu.CompilerParams(vmem_limit_bytes=4 * 1024 * 1024),
        cost_estimate=light,
    )(*acts, grad)


def gram_of(grads, act):
    layers, _, cols = act.shape

    def kernel(*refs):
        for layer in range(layers):
            refs[-1][layer] = product_of(refs[layer][0], refs[-2][layer])

    return pl.pallas_call(
        kernel,
        out_shape=jax.ShapeDtypeStruct((layers, grads[0].shape[2], cols), jnp.float32),
        in_specs=[vmem_spec] * (layers + 1),
        out_specs=vmem_spec,
        compiler_params=pltpu.CompilerParams(vmem_limit_bytes=16 * 1024 * 1024),
        cost_estimate=light,
    )(*grads, act)


def product_of(grad, act):
    return lax.dot_general(grad, act, (((0,), (0,)), ((), ())), preferred_element_type=jnp.float32)


def finish(grads, act, grams, factors):
    layers, tile, cols = grams.shape

    def kernel(*refs):
        grad_refs, (act_ref, gram_ref, factor_ref, out_ref) = refs[:layers], refs[layers:]
        for layer in range(layers):
            gram = gram_ref[layer] + product_of(grad_refs[layer][1], act_ref[layer])
            out_ref[layer] = (gram * factor_ref[layer]).astype(jnp.bfloat16)

    return pl.pallas_call(
        kernel,
        out_shape=jax.ShapeDtypeStruct((layers, tile, cols), jnp.bfloat16),
        in_specs=[vmem_spec] * (layers + 3),
        out_specs=vmem_spec,
        compiler_params=pltpu.CompilerParams(vmem_limit_bytes=24 * 1024 * 1024),
        cost_estimate=light,
    )(*grads, act, grams, factors)


def eigenvalues(scalars, states, packets, n_dp):
    n_own = len(packets)
    layers, tile = packets[0].shape[0] // 2, packets[0].shape[1]
    slot_count, width = states[0].shape[0] // 2, states[0].shape[1]

    def kernel(scalar_ref, *refs):
        state_refs, packet_refs, refs = refs[:n_own], refs[n_own : 2 * n_own], refs[2 * n_own :]
        out_ref, new_act_ref, new_grad_ref, act_full, grad_full = refs
        dp, own = scalar_ref[0], scalar_ref[1]
        total = scalar_ref[2]
        for index in range(1, n_dp):
            total += scalar_ref[2 + index]
        total = total.astype(jnp.float32)
        owners = [scalar_ref[2 + n_dp + layer] for layer in range(layers)]
        for mask in range(n_own):
            at = pl.ds(pl.multiple_of((own ^ mask) * tile, tile), tile)
            act_full[:, at] = packet_refs[mask][:layers] / total
            at = pl.ds(pl.multiple_of((n_own - (own ^ mask)) % n_own * tile, tile), tile)
            grad_full[:, at] = packet_refs[mask][layers:] / total
        new_act_ref[...] = state_refs[0][:slot_count]
        new_grad_ref[...] = state_refs[0][slot_count:]
        for layer in range(layers):
            owner_now = owners[layer]
            rank = jnp.int32(0)
            for earlier in range(layer):
                rank += jnp.where(owners[earlier] == owner_now, 1, 0)
            old_act = jnp.zeros((1, width), jnp.float32)
            old_grad = jnp.zeros((1, width), jnp.float32)
            for mask in range(n_own):
                for slot in range(slot_count):
                    here = (owner_now == own ^ mask) & (rank == slot)
                    down = slot_count + slot
                    old_act = jnp.where(here, state_refs[mask][slot : slot + 1], old_act)
                    old_grad = jnp.where(here, state_refs[mask][down : down + 1], old_grad)
            eigen_act = decay_rate * old_act + (1.0 - decay_rate) * act_full[layer : layer + 1]
            eigen_grad = decay_rate * old_grad + (1.0 - decay_rate) * grad_full[layer : layer + 1]
            act_full[layer : layer + 1] = eigen_act
            grad_full[layer : layer + 1] = eigen_grad
            for slot in range(slot_count):

                @pl.when((owner_now == own) & (rank == slot))
                def _(slot=slot, eigen_act=eigen_act, eigen_grad=eigen_grad):
                    new_act_ref[slot : slot + 1] = eigen_act
                    new_grad_ref[slot : slot + 1] = eigen_grad

            damping = damping_rate * (jnp.sum(eigen_grad) / width) * (jnp.sum(eigen_act) / width)
            rows = grad_full[layer : layer + 1, pl.ds(pl.multiple_of(dp * tile, tile), tile)]
            cols = act_full[layer : layer + 1, pl.ds(pl.multiple_of(own * tile, tile), tile)]
            rows = jnp.transpose(jnp.broadcast_to(rows, (128, tile)))
            rows = jnp.concatenate([rows] * (tile // 128), axis=1)
            out_ref[layer] = 1.0 / (total * (rows * cols + damping))

    out_shape = [
        jax.ShapeDtypeStruct((layers, tile, tile), jnp.float32),
        jax.ShapeDtypeStruct((slot_count, width), jnp.float32),
        jax.ShapeDtypeStruct((slot_count, width), jnp.float32),
    ]
    return pl.pallas_call(
        kernel,
        out_shape=out_shape,
        in_specs=[scalar_spec] + [vmem_spec] * (2 * n_own),
        out_specs=[vmem_spec] * len(out_shape),
        scratch_shapes=[pltpu.VMEM((layers, width), jnp.float32)] * 2,
        compiler_params=pltpu.CompilerParams(vmem_limit_bytes=16 * 1024 * 1024),
        cost_estimate=light,
    )(scalars, *states, *packets)


def line_plan(activations, out_grads, basis_act, basis_grad, owner_of, counts, state_act, state_grad):
    layers, tok_rows, width = activations.shape
    tile = basis_act.shape[1]
    n_dp = lax.axis_size("dp")
    n_own = lax.axis_size("owner")
    dp = lax.axis_index("dp")
    own = lax.axis_index("owner")
    scalars = jnp.concatenate([jnp.stack([dp, own]), counts, owner_of]).astype(jnp.int32)

    def after(array, *others):
        return lax.optimization_barrier((array, *others))[0]

    def step(arrays, *others):
        return lax.optimization_barrier((*arrays, *others))[: len(arrays)]

    owners = range(n_own)
    held = [-o % n_own for o in owners]
    cuts = cut_rows((out_grads, activations), tile, n_own, n_dp)
    cuts = [flip(cut, "dp", number % (n_dp - 1) + 1) for number, cut in enumerate(cuts)]
    got_grad, got_act = cuts[: n_dp - 1], cuts[n_dp - 1 :]
    pieces = got_grad[:-1] + [after(got_grad[-1], got_act[0])]
    pieces += [flip(piece, "owner", 2) for piece in pieces]
    pieces += [flip(piece, "owner", 1) for piece in pieces]
    stay = pltpu.with_memory_space_constraint(basis_grad, pltpu.HBM)
    keep, send = project_rows(scalars, out_grads, pieces, stay, n_own, n_dp)

    near = flip(after(send, *got_act), "dp", 1)
    pieces = [join(got_act)]
    pieces += [flip(pieces[0], "owner", 2)]
    pieces += [flip(piece, "owner", 1) for piece in pieces]
    stay = pltpu.with_memory_space_constraint(basis_act, pltpu.HBM)
    keep_act, send_act = project_rows(scalars, activations, pieces, stay, n_own, n_dp)

    state = after(jnp.concatenate([state_act, state_grad], axis=0), keep)
    states = [state] + [flip(state, "owner", mask) for mask in range(1, n_own)]

    keep, near, keep_act, send_act, *states = step([keep, near, keep_act, send_act, *states])
    parts = add_rows([(keep, near)], keep.shape[1] // 2)
    parts = [lax.ppermute(array, "owner", [*enumerate(held)]) for array in parts]
    to_pair = [((a, o), (a ^ 2, o)) for a in range(n_dp) for o in owners if (a ^ held[o]) & 2]
    crosses = [hop(array, to_pair) for array in parts]
    near_act = flip(send_act, "dp", 1)

    (near,) = add_rows([*zip(parts, crosses, strict=True)])
    aside = ((dp ^ (-own % n_own)) // 2).astype(jnp.int32)[None]
    squares = [squares_of(aside, near)]
    squares += [flip(squares[0], "dp", mask) for mask in range(1, n_dp)]
    square_grad = total_of(squares)
    far = hop(after(near, square_grad), [((held[o] ^ 1, o), (held[o], o)) for o in owners])
    full = by_layer(near, far)
    chip = [hop(array, [((held[o], o), (held[o], o ^ 2)) for o in owners]) for array in full]

    part_act = add((keep_act, after(near_act, square_grad)))
    cross_act = flip(part_act, "dp", 2)

    done = step([part_act, cross_act, *full, *chip])
    (part_act, cross_act), full, chip = done[:2], done[2:][:layers], done[2 + layers :]
    full_act = add((part_act, cross_act))
    halves = [squares_of(aside * 0, full_act)]
    halves += [flip(halves[0], "dp", 1)]
    packet = packet_of(halves, square_grad)
    back_act = flip(after(full_act, packet), "dp", 1)
    packets = [packet] + [flip(packet, "owner", mask) for mask in range(1, n_own)]
    source = -dp % n_own
    home = jnp.where(own == source, 0, jnp.where(own == source ^ 2, 1, 2)).astype(jnp.int32)[None]
    full = pick(after(home, *packets), [*zip(full, chip, strict=True)])
    to_core = [((held[o], o ^ b), (held[o], o ^ b ^ 1)) for o in owners for b in (0, 2)]
    core = [hop(array, to_core) for array in full]
    factors, new_act, new_grad = eigenvalues(scalars, states, packets, n_dp)
    grads = pick(home // 2, [*zip(full, core, strict=True)])
    grams = gram_of(grads, full_act)

    grams, factors, back_act, *grads = step([grams, factors, back_act, *grads])
    return finish(grads, back_act, grams, factors), new_act, new_grad


def solution(mesh):
    placed = (
        P("groups", "dp", None),
        P("groups", "dp", None),
        P("groups", "dp", "owner"),
        P("groups", "dp", "owner"),
        P(),
        P("groups"),
        P("owner", "groups"),
        P("owner", "groups"),
    )
    square = mesh.shape["dp"] == 4 and mesh.shape["owner"] == 4
    return jax.shard_map(
        line_plan if square else gather_plan,
        mesh=mesh,
        in_specs=placed,
        out_specs=(P("groups", "dp", "owner"), P("owner", "groups"), P("owner", "groups")),
        check_vma=False,
    )
```

```python
import jax
import jax.numpy as jnp
from jax import lax
from jax.experimental import pallas as pl
from jax.experimental.pallas import tpu as pltpu
from jax.sharding import PartitionSpec as P

decay_rate = 0.25
damping_rate = 0.1
vmem_spec = pl.BlockSpec(memory_space=pltpu.VMEM)
scalar_spec = pl.BlockSpec(memory_space=pltpu.SMEM)
light = pl.CostEstimate(flops=0, bytes_accessed=0, transcendentals=0)


def spread(array, axis, root):
    mine = lax.axis_index(axis) == root
    return lax.psum(jnp.where(mine, array, jnp.zeros_like(array)), axis)


def gather_plan(activations, out_grads, basis_act, basis_grad, owner_of, counts, state_act, state_grad):
    layers = activations.shape[0]
    tok_rows = activations.shape[1]
    tile_rows = basis_act.shape[1]
    tile_cols = basis_act.shape[2]
    slot_count = state_act.shape[0]
    dp_index = lax.axis_index("dp")
    own_index = lax.axis_index("owner")
    valid_rows = (jnp.arange(tok_rows) < counts[dp_index]).astype(jnp.float32)[:, None]
    valid_total = jnp.sum(counts).astype(jnp.float32)
    square_acts = []
    square_grads = []
    gram_tiles = []
    for layer_index in range(layers):
        panel_act = jnp.dot(
            activations[layer_index],
            lax.all_gather(basis_act[layer_index], "dp", axis=0, tiled=True),
            preferred_element_type=jnp.float32,
        )
        panel_grad = jnp.dot(
            out_grads[layer_index],
            lax.all_gather(basis_grad[layer_index], "dp", axis=0, tiled=True),
            preferred_element_type=jnp.float32,
        )
        panel_act = (panel_act * valid_rows).astype(jnp.bfloat16)
        panel_grad = (panel_grad * valid_rows).astype(jnp.bfloat16)
        full_act = lax.all_gather(panel_act, "owner", axis=1, tiled=True)
        full_grad = lax.all_gather(panel_grad, "owner", axis=1, tiled=True)
        square_act = jnp.sum(jnp.square(full_act.astype(jnp.float32)), axis=0)
        square_grad = jnp.sum(jnp.square(full_grad.astype(jnp.float32)), axis=0)
        gram_term = lax.dot_general(
            full_grad, panel_act, (((0,), (0,)), ((), ())), preferred_element_type=jnp.float32
        )
        gram_tiles.append(
            lax.psum_scatter(
                gram_term.astype(jnp.bfloat16), "dp", scatter_dimension=0, tiled=True
            ).astype(jnp.float32)
            / valid_total
        )
        square_act, square_grad = lax.psum((square_act, square_grad), "dp")
        square_acts.append(square_act)
        square_grads.append(square_grad)
    new_act = state_act
    new_grad = state_grad
    results = []
    for layer_index in range(layers):
        owner_now = owner_of[layer_index]
        slot_rank = jnp.sum((owner_of[:layer_index] == owner_now).astype(jnp.int32))
        selector = (jnp.arange(slot_count) == slot_rank).astype(jnp.float32)[:, None]
        local_act = decay_rate * jnp.sum(state_act * selector, axis=0) + (
            1.0 - decay_rate
        ) * (square_acts[layer_index] / valid_total)
        local_grad = decay_rate * jnp.sum(state_grad * selector, axis=0) + (
            1.0 - decay_rate
        ) * (square_grads[layer_index] / valid_total)
        eigen_act = spread(local_act, "owner", owner_now)
        eigen_grad = spread(local_grad, "owner", owner_now)
        replace_rows = ((jnp.arange(slot_count) == slot_rank) & (own_index == owner_now))[:, None]
        new_act = jnp.where(replace_rows, eigen_act[None, :], new_act)
        new_grad = jnp.where(replace_rows, eigen_grad[None, :], new_grad)
        damping = damping_rate * jnp.mean(eigen_grad) * jnp.mean(eigen_act)
        grad_eigen = lax.dynamic_slice_in_dim(eigen_grad, dp_index * tile_rows, tile_rows)
        act_eigen = lax.dynamic_slice_in_dim(eigen_act, own_index * tile_cols, tile_cols)
        scaled = gram_tiles[layer_index] / (grad_eigen[:, None] * act_eigen[None, :] + damping)
        results.append(scaled.astype(jnp.bfloat16))
    return (jnp.stack(results), new_act, new_grad)


def flip(array, axis, mask):
    return lax.ppermute(array, axis, [(i, i ^ mask) for i in range(lax.axis_size(axis))])


def hop(array, pairs):
    owners = lax.axis_size("owner")
    flat = [(a * owners + b, c * owners + e) for (a, b), (c, e) in pairs]
    return lax.ppermute(array, ("dp", "owner"), flat)


def project_rows(scalars, tokens, pieces, basis, n_own, n_dp):
    layers, tok_rows, _ = tokens.shape
    tile, cols = basis.shape[1:]
    part_rows = tok_rows // n_own
    packed = 3 * n_dp * tok_rows // 4
    half = packed // 2
    shapes = [(layers, half, cols)] * 2

    def kernel(scalar_ref, tokens_hbm, basis_hbm, *refs):
        piece_refs, refs = refs[: len(pieces)], refs[len(pieces) :]
        out_refs, (tokens_ref, basis_ref, sems) = refs[: len(shapes)], refs[len(shapes) :]
        dp, own = scalar_ref[0], scalar_ref[1]
        at = pl.ds(pl.multiple_of(dp * tile, tile), tile)
        copies = []
        for layer in range(layers):
            copies.append(
                [
                    pltpu.make_async_copy(
                        tokens_hbm.at[layer, :, at], tokens_ref.at[layer], sems.at[2 * layer]
                    ),
                    pltpu.make_async_copy(basis_hbm.at[layer], basis_ref.at[layer], sems.at[2 * layer + 1]),
                ]
            )
            for copy in copies[-1]:
                copy.start()
        col = lax.broadcasted_iota(jnp.int32, (1, n_dp * tok_rows), 1)
        turn = (col - tok_rows) // part_rows
        peer = turn // (n_dp - 1)
        peer = own ^ (((peer & 1) << 1) | (peer >> 1))
        mine = col < tok_rows
        mask = jnp.where(mine, 0, turn % (n_dp - 1) + 1)
        index = jnp.where(mine, col, peer * part_rows + col % part_rows)
        place = jnp.full_like(col, -1)
        for number in range(n_dp):
            shard = dp ^ number
            start = jnp.int32(0)
            for other in range(n_dp):
                start += jnp.where(other < shard, scalar_ref[2 + other], 0)
            here = (mask == number) & (index < scalar_ref[2 + shard])
            place = jnp.where(here, start + index, place)
        row = lax.broadcasted_iota(jnp.int32, (packed, n_dp * tok_rows), 0)
        row = row + jnp.where(dp % 2 == 0, 0, jnp.where(row < half, half, -half))
        select = (row == place).astype(jnp.bfloat16)
        for layer in range(layers):
            copies[layer][0].wait()
            rows = jnp.concatenate([tokens_ref[layer]] + [p[layer] for p in piece_refs], axis=0)
            chosen = jnp.dot(select, rows, preferred_element_type=jnp.float32).astype(jnp.bfloat16)
            copies[layer][1].wait()
            result = jnp.dot(chosen, basis_ref[layer], preferred_element_type=jnp.float32).astype(
                jnp.bfloat16
            )
            out_refs[0][layer] = result[:half]
            out_refs[1][layer] = result[half:]

    return pl.pallas_call(
        kernel,
        out_shape=[jax.ShapeDtypeStruct(shape, jnp.bfloat16) for shape in shapes],
        in_specs=[scalar_spec] + [pl.BlockSpec(memory_space=pltpu.HBM), pl.BlockSpec(memory_space=pl.ANY)] + [vmem_spec] * len(pieces),
        out_specs=[vmem_spec] * len(shapes),
        scratch_shapes=[
            pltpu.VMEM((layers, tok_rows, tile), jnp.bfloat16),
            pltpu.VMEM((layers, tile, cols), jnp.bfloat16),
            pltpu.SemaphoreType.DMA((2 * layers,)),
        ],
        compiler_params=pltpu.CompilerParams(vmem_limit_bytes=16 * 1024 * 1024),
        cost_estimate=light,
    )(scalars, pltpu.with_memory_space_constraint(tokens, pltpu.HBM), basis, *pieces)


def add(*pairs):
    layers = pairs[0][0].shape[0]

    def kernel(*refs):
        for number in range(len(pairs)):
            total = refs[2 * number][...].astype(jnp.float32) + refs[2 * number + 1][...].astype(jnp.float32)
            refs[-1][number * layers : (number + 1) * layers] = total.astype(refs[-1].dtype)

    first = pairs[0][0]
    return pl.pallas_call(
        kernel,
        out_shape=jax.ShapeDtypeStruct((layers * len(pairs), *first.shape[1:]), first.dtype),
        in_specs=[vmem_spec] * (2 * len(pairs)),
        out_specs=vmem_spec,
        compiler_params=pltpu.CompilerParams(vmem_limit_bytes=8 * 1024 * 1024),
        cost_estimate=light,
    )(*[array for pair in pairs for array in pair])


def add_rows(near, far, cut):
    layers, height, cols = near.shape
    spans = [(0, cut), (cut, height)]

    def kernel(near_ref, far_ref, *out_refs):
        for out_ref, (start, stop) in zip(out_refs, spans, strict=True):
            total = near_ref[:, start:stop].astype(jnp.float32) + far_ref[:, start:stop].astype(jnp.float32)
            out_ref[...] = total.astype(out_ref.dtype)

    return pl.pallas_call(
        kernel,
        out_shape=[jax.ShapeDtypeStruct((layers, stop - start, cols), near.dtype) for start, stop in spans],
        in_specs=[vmem_spec] * 2,
        out_specs=[vmem_spec] * len(spans),
        compiler_params=pltpu.CompilerParams(vmem_limit_bytes=8 * 1024 * 1024),
        cost_estimate=light,
    )(near, far)


def by_layer(nears, fars):
    layers, _, cols = nears[0].shape
    count = len(nears)
    height = sum(array.shape[1] for array in nears)

    def kernel(*refs):
        for side in range(2):
            start = 0
            for ref in refs[side * count : (side + 1) * count]:
                for layer, out_ref in enumerate(refs[2 * count :]):
                    out_ref[side, start : start + ref.shape[1]] = ref[layer]
                start += ref.shape[1]

    return pl.pallas_call(
        kernel,
        out_shape=[jax.ShapeDtypeStruct((2, height, cols), nears[0].dtype)] * layers,
        in_specs=[vmem_spec] * (2 * count),
        out_specs=[vmem_spec] * layers,
        compiler_params=pltpu.CompilerParams(vmem_limit_bytes=8 * 1024 * 1024),
        cost_estimate=light,
    )(*nears, *fars)


def join(arrays):
    layers, rows, cols = arrays[0].shape

    def kernel(*refs):
        for number, ref in enumerate(refs[:-1]):
            refs[-1][:, number * rows : (number + 1) * rows] = ref[...]

    return pl.pallas_call(
        kernel,
        out_shape=jax.ShapeDtypeStruct((layers, len(arrays) * rows, cols), arrays[0].dtype),
        in_specs=[vmem_spec] * len(arrays),
        out_specs=vmem_spec,
        compiler_params=pltpu.CompilerParams(vmem_limit_bytes=8 * 1024 * 1024),
        cost_estimate=light,
    )(*arrays)


def cut_rows(arrays, tile, n_own, n_dp):
    layers, tok_rows, _ = arrays[0].shape
    part_rows = tok_rows // n_own
    peers = n_dp - 1

    def kernel(*refs):
        in_refs, out_refs, sems = refs[: len(arrays)], refs[len(arrays) : -1], refs[-1]
        dp, own = lax.axis_index("dp"), lax.axis_index("owner")
        rows = pl.ds(pl.multiple_of(own * part_rows, part_rows), part_rows)
        copies = []
        for number, out_ref in enumerate(out_refs):
            block = dp ^ (number % peers + 1)
            cols = pl.ds(pl.multiple_of(block * tile, tile), tile)
            copies.append(
                pltpu.make_async_copy(in_refs[number // peers].at[:, rows, cols], out_ref, sems.at[number])
            )
            copies[-1].start()
        for copy in copies:
            copy.wait()

    count = len(arrays) * peers
    return pl.pallas_call(
        kernel,
        out_shape=[jax.ShapeDtypeStruct((layers, part_rows, tile), arrays[0].dtype)] * count,
        in_specs=[pl.BlockSpec(memory_space=pltpu.HBM)] * len(arrays),
        out_specs=[vmem_spec] * count,
        scratch_shapes=[pltpu.SemaphoreType.DMA((count,))],
        compiler_params=pltpu.CompilerParams(vmem_limit_bytes=8 * 1024 * 1024),
        cost_estimate=light,
    )(*[pltpu.with_memory_space_constraint(array, pltpu.HBM) for array in arrays])


def pick(home, choices):
    flat = [array for arrays in choices for array in arrays]
    count = len(choices[0])

    def kernel(home_ref, *refs):
        for index in range(count):

            @pl.when(home_ref[0] == index)
            def _(index=index):
                for number, out_ref in enumerate(refs[len(flat) :]):
                    out_ref[...] = refs[number * count + index][...]

    return pl.pallas_call(
        kernel,
        out_shape=[jax.ShapeDtypeStruct(arrays[0].shape, arrays[0].dtype) for arrays in choices],
        in_specs=[scalar_spec] + [vmem_spec] * len(flat),
        out_specs=[vmem_spec] * len(choices),
        compiler_params=pltpu.CompilerParams(vmem_limit_bytes=12 * 1024 * 1024),
        cost_estimate=light,
    )(home, *flat)


def squares_of(aside, panels):
    layers, _, cols = panels[0].shape

    def kernel(aside_ref, *refs):
        for layer in range(layers):
            total = jnp.zeros((1, cols), jnp.float32)
            for ref in refs[:-1]:
                wide = ref[layer].astype(jnp.float32)
                total += jnp.sum(wide * wide, axis=0, keepdims=True)
            refs[-1][layer : layer + 1] = jnp.where(aside_ref[0] == 0, total, 0.0)

    return pl.pallas_call(
        kernel,
        out_shape=jax.ShapeDtypeStruct((layers, cols), jnp.float32),
        in_specs=[scalar_spec] + [vmem_spec] * len(panels),
        out_specs=vmem_spec,
        compiler_params=pltpu.CompilerParams(vmem_limit_bytes=8 * 1024 * 1024),
        cost_estimate=light,
    )(aside, *panels)


def halves_of(act, near, far):
    layers, _, cols = act.shape

    def kernel(act_ref, near_ref, far_ref, out_ref):
        for layer in range(layers):
            wide = act_ref[layer].astype(jnp.float32)
            out_ref[layer : layer + 1] = jnp.sum(wide * wide, axis=0, keepdims=True)
        out_ref[layers:] = near_ref[...] + far_ref[...]

    return pl.pallas_call(
        kernel,
        out_shape=jax.ShapeDtypeStruct((2 * layers, cols), jnp.float32),
        in_specs=[vmem_spec] * 3,
        out_specs=vmem_spec,
        compiler_params=pltpu.CompilerParams(vmem_limit_bytes=8 * 1024 * 1024),
        cost_estimate=light,
    )(act, near, far)


def total_of(near, far):
    def kernel(near_ref, far_ref, out_ref):
        out_ref[...] = near_ref[...] + far_ref[...]

    return pl.pallas_call(
        kernel,
        out_shape=jax.ShapeDtypeStruct(near.shape, near.dtype),
        in_specs=[vmem_spec] * 2,
        out_specs=vmem_spec,
        compiler_params=pltpu.CompilerParams(vmem_limit_bytes=4 * 1024 * 1024),
        cost_estimate=light,
    )(near, far)


def gram_of(grads, act):
    layers, _, cols = act.shape

    def kernel(*refs):
        for layer in range(layers):
            refs[-1][layer] = product_of(refs[layer][0], refs[-2][layer])

    return pl.pallas_call(
        kernel,
        out_shape=jax.ShapeDtypeStruct((layers, grads[0].shape[2], cols), jnp.float32),
        in_specs=[vmem_spec] * (layers + 1),
        out_specs=vmem_spec,
        compiler_params=pltpu.CompilerParams(vmem_limit_bytes=16 * 1024 * 1024),
        cost_estimate=light,
    )(*grads, act)


def product_of(grad, act):
    return lax.dot_general(grad, act, (((0,), (0,)), ((), ())), preferred_element_type=jnp.float32)


def finish(grads, act, grams, factors):
    layers, tile, cols = grams.shape

    def kernel(*refs):
        grad_refs, (act_ref, gram_ref, factor_ref, out_ref) = refs[:layers], refs[layers:]
        for layer in range(layers):
            gram = gram_ref[layer] + product_of(grad_refs[layer][1], act_ref[layer])
            out_ref[layer] = (gram * factor_ref[layer]).astype(jnp.bfloat16)

    return pl.pallas_call(
        kernel,
        out_shape=jax.ShapeDtypeStruct((layers, tile, cols), jnp.bfloat16),
        in_specs=[vmem_spec] * (layers + 3),
        out_specs=vmem_spec,
        compiler_params=pltpu.CompilerParams(vmem_limit_bytes=24 * 1024 * 1024),
        cost_estimate=light,
    )(*grads, act, grams, factors)


def eigenvalues(scalars, states, packets, n_dp):
    n_own = len(packets)
    layers, tile = packets[0].shape[0] // 2, packets[0].shape[1]
    slot_count, width = states[0].shape[0] // 2, states[0].shape[1]

    def kernel(scalar_ref, *refs):
        state_refs, packet_refs, refs = refs[:n_own], refs[n_own : 2 * n_own], refs[2 * n_own :]
        out_ref, new_act_ref, new_grad_ref, act_full, grad_full = refs
        dp, own = scalar_ref[0], scalar_ref[1]
        total = scalar_ref[2]
        for index in range(1, n_dp):
            total += scalar_ref[2 + index]
        total = total.astype(jnp.float32)
        owners = [scalar_ref[2 + n_dp + layer] for layer in range(layers)]
        for mask in range(n_own):
            at = pl.ds(pl.multiple_of((own ^ mask) * tile, tile), tile)
            act_full[:, at] = packet_refs[mask][:layers] / total
            at = pl.ds(pl.multiple_of((n_own - (own ^ mask)) % n_own * tile, tile), tile)
            grad_full[:, at] = packet_refs[mask][layers:] / total
        new_act_ref[...] = state_refs[0][:slot_count]
        new_grad_ref[...] = state_refs[0][slot_count:]
        for layer in range(layers):
            owner_now = owners[layer]
            rank = jnp.int32(0)
            for earlier in range(layer):
                rank += jnp.where(owners[earlier] == owner_now, 1, 0)
            old_act = jnp.zeros((1, width), jnp.float32)
            old_grad = jnp.zeros((1, width), jnp.float32)
            for mask in range(n_own):
                for slot in range(slot_count):
                    here = (owner_now == own ^ mask) & (rank == slot)
                    down = slot_count + slot
                    old_act = jnp.where(here, state_refs[mask][slot : slot + 1], old_act)
                    old_grad = jnp.where(here, state_refs[mask][down : down + 1], old_grad)
            eigen_act = decay_rate * old_act + (1.0 - decay_rate) * act_full[layer : layer + 1]
            eigen_grad = decay_rate * old_grad + (1.0 - decay_rate) * grad_full[layer : layer + 1]
            act_full[layer : layer + 1] = eigen_act
            grad_full[layer : layer + 1] = eigen_grad
            for slot in range(slot_count):

                @pl.when((owner_now == own) & (rank == slot))
                def _(slot=slot, eigen_act=eigen_act, eigen_grad=eigen_grad):
                    new_act_ref[slot : slot + 1] = eigen_act
                    new_grad_ref[slot : slot + 1] = eigen_grad

            damping = damping_rate * (jnp.sum(eigen_grad) / width) * (jnp.sum(eigen_act) / width)
            rows = grad_full[layer : layer + 1, pl.ds(pl.multiple_of(dp * tile, tile), tile)]
            cols = act_full[layer : layer + 1, pl.ds(pl.multiple_of(own * tile, tile), tile)]
            rows = jnp.transpose(jnp.broadcast_to(rows, (128, tile)))
            rows = jnp.concatenate([rows] * (tile // 128), axis=1)
            out_ref[layer] = 1.0 / (total * (rows * cols + damping))

    out_shape = [
        jax.ShapeDtypeStruct((layers, tile, tile), jnp.float32),
        jax.ShapeDtypeStruct((slot_count, width), jnp.float32),
        jax.ShapeDtypeStruct((slot_count, width), jnp.float32),
    ]
    return pl.pallas_call(
        kernel,
        out_shape=out_shape,
        in_specs=[scalar_spec] + [vmem_spec] * (2 * n_own),
        out_specs=[vmem_spec] * len(out_shape),
        scratch_shapes=[pltpu.VMEM((layers, width), jnp.float32)] * 2,
        compiler_params=pltpu.CompilerParams(vmem_limit_bytes=16 * 1024 * 1024),
        cost_estimate=light,
    )(scalars, *states, *packets)


def line_plan(activations, out_grads, basis_act, basis_grad, owner_of, counts, state_act, state_grad):
    layers, tok_rows, width = activations.shape
    tile = basis_act.shape[1]
    n_dp = lax.axis_size("dp")
    n_own = lax.axis_size("owner")
    dp = lax.axis_index("dp")
    own = lax.axis_index("owner")
    scalars = jnp.concatenate([jnp.stack([dp, own]), counts, owner_of]).astype(jnp.int32)

    def after(array, *others):
        return lax.optimization_barrier((array, *others))[0]

    def step(arrays, *others):
        return lax.optimization_barrier((*arrays, *others))[: len(arrays)]

    owners = range(n_own)
    held = [-o % n_own for o in owners]
    cuts = cut_rows((out_grads, activations), tile, n_own, n_dp)
    cuts = [flip(cut, "dp", number % (n_dp - 1) + 1) for number, cut in enumerate(cuts)]
    got_grad, got_act = cuts[: n_dp - 1], cuts[n_dp - 1 :]
    pieces = got_grad[:-1] + [after(got_grad[-1], got_act[0])]
    pieces += [flip(piece, "owner", 2) for piece in pieces]
    pieces += [flip(piece, "owner", 1) for piece in pieces]
    stay = pltpu.with_memory_space_constraint(basis_grad, pltpu.HBM)
    keep, send = project_rows(scalars, out_grads, pieces, stay, n_own, n_dp)

    near = flip(after(send, *got_act), "dp", 1)
    pieces = [join(got_act)]
    pieces += [flip(pieces[0], "owner", 2)]
    pieces += [flip(piece, "owner", 1) for piece in pieces]
    stay = pltpu.with_memory_space_constraint(basis_act, pltpu.HBM)
    keep_act, send_act = project_rows(scalars, activations, pieces, stay, n_own, n_dp)

    state = after(jnp.concatenate([state_act, state_grad], axis=0), keep)
    states = [state] + [flip(state, "owner", mask) for mask in range(1, n_own)]

    keep, near, keep_act, send_act, *states = step([keep, near, keep_act, send_act, *states])
    parts = add_rows(keep, near, keep.shape[1] // 2)
    parts = [lax.ppermute(array, "owner", [*enumerate(held)]) for array in parts]
    to_pair = [((a, o), (a ^ 2, o)) for a in range(n_dp) for o in owners if (a ^ held[o]) & 2]
    crosses = [hop(array, to_pair) for array in parts]
    near_act = flip(send_act, "dp", 1)

    nears = [add(pair) for pair in zip(parts, crosses, strict=True)]
    aside = ((dp ^ (-own % n_own)) // 2).astype(jnp.int32)[None]
    square_grad = squares_of(aside, nears)
    square_far = flip(square_grad, "dp", 2)
    fars = [hop(array, [((held[o] ^ 1, o), (held[o], o)) for o in owners]) for array in nears]
    full = by_layer(nears, fars)
    chip = [hop(array, [((held[o], o), (held[o], o ^ 2)) for o in owners]) for array in full]

    part_act = add((keep_act, near_act))
    cross_act = flip(part_act, "dp", 2)

    done = step([part_act, cross_act, square_grad, square_far, *full, *chip])
    (part_act, cross_act, square_grad, square_far), full, chip = done[:4], done[4:][:layers], done[4 + layers :]
    full_act = add((part_act, cross_act))
    half = halves_of(full_act, square_grad, square_far)
    packet = total_of(half, flip(half, "dp", 1))
    back_act = flip(after(full_act, packet), "dp", 1)
    packets = [packet] + [flip(packet, "owner", mask) for mask in range(1, n_own)]
    source = -dp % n_own
    home = jnp.where(own == source, 0, jnp.where(own == source ^ 2, 1, 2)).astype(jnp.int32)[None]
    full = pick(after(home, *packets), [*zip(full, chip, strict=True)])
    to_core = [((held[o], o ^ b), (held[o], o ^ b ^ 1)) for o in owners for b in (0, 2)]
    core = [hop(array, to_core) for array in full]
    factors, new_act, new_grad = eigenvalues(scalars, states, packets, n_dp)
    grads = pick(home // 2, [*zip(full, core, strict=True)])
    grams = gram_of(grads, full_act)

    grams, factors, back_act, *grads = step([grams, factors, back_act, *grads])
    return finish(grads, back_act, grams, factors), new_act, new_grad


def solution(mesh):
    placed = (
        P("groups", "dp", None),
        P("groups", "dp", None),
        P("groups", "dp", "owner"),
        P("groups", "dp", "owner"),
        P(),
        P("groups"),
        P("owner", "groups"),
        P("owner", "groups"),
    )
    square = mesh.shape["dp"] == 4 and mesh.shape["owner"] == 4
    return jax.shard_map(
        line_plan if square else gather_plan,
        mesh=mesh,
        in_specs=placed,
        out_specs=(P("groups", "dp", "owner"), P("owner", "groups"), P("owner", "groups")),
        check_vma=False,
    )
```

```python
import jax
import jax.numpy as jnp
from jax import lax
from jax.experimental import pallas as pl
from jax.experimental.pallas import tpu as pltpu
from jax.sharding import PartitionSpec as P

decay_rate = 0.25
damping_rate = 0.1
vmem_spec = pl.BlockSpec(memory_space=pltpu.VMEM)
scalar_spec = pl.BlockSpec(memory_space=pltpu.SMEM)
light = pl.CostEstimate(flops=0, bytes_accessed=0, transcendentals=0)


def spread(array, axis, root):
    mine = lax.axis_index(axis) == root
    return lax.psum(jnp.where(mine, array, jnp.zeros_like(array)), axis)


def gather_plan(activations, out_grads, basis_act, basis_grad, owner_of, counts, state_act, state_grad):
    layers = activations.shape[0]
    tok_rows = activations.shape[1]
    tile_rows = basis_act.shape[1]
    tile_cols = basis_act.shape[2]
    slot_count = state_act.shape[0]
    dp_index = lax.axis_index("dp")
    own_index = lax.axis_index("owner")
    valid_rows = (jnp.arange(tok_rows) < counts[dp_index]).astype(jnp.float32)[:, None]
    valid_total = jnp.sum(counts).astype(jnp.float32)
    square_acts = []
    square_grads = []
    gram_tiles = []
    for layer_index in range(layers):
        panel_act = jnp.dot(
            activations[layer_index],
            lax.all_gather(basis_act[layer_index], "dp", axis=0, tiled=True),
            preferred_element_type=jnp.float32,
        )
        panel_grad = jnp.dot(
            out_grads[layer_index],
            lax.all_gather(basis_grad[layer_index], "dp", axis=0, tiled=True),
            preferred_element_type=jnp.float32,
        )
        panel_act = (panel_act * valid_rows).astype(jnp.bfloat16)
        panel_grad = (panel_grad * valid_rows).astype(jnp.bfloat16)
        full_act = lax.all_gather(panel_act, "owner", axis=1, tiled=True)
        full_grad = lax.all_gather(panel_grad, "owner", axis=1, tiled=True)
        square_act = jnp.sum(jnp.square(full_act.astype(jnp.float32)), axis=0)
        square_grad = jnp.sum(jnp.square(full_grad.astype(jnp.float32)), axis=0)
        gram_term = lax.dot_general(
            full_grad, panel_act, (((0,), (0,)), ((), ())), preferred_element_type=jnp.float32
        )
        gram_tiles.append(
            lax.psum_scatter(
                gram_term.astype(jnp.bfloat16), "dp", scatter_dimension=0, tiled=True
            ).astype(jnp.float32)
            / valid_total
        )
        square_act, square_grad = lax.psum((square_act, square_grad), "dp")
        square_acts.append(square_act)
        square_grads.append(square_grad)
    new_act = state_act
    new_grad = state_grad
    results = []
    for layer_index in range(layers):
        owner_now = owner_of[layer_index]
        slot_rank = jnp.sum((owner_of[:layer_index] == owner_now).astype(jnp.int32))
        selector = (jnp.arange(slot_count) == slot_rank).astype(jnp.float32)[:, None]
        local_act = decay_rate * jnp.sum(state_act * selector, axis=0) + (
            1.0 - decay_rate
        ) * (square_acts[layer_index] / valid_total)
        local_grad = decay_rate * jnp.sum(state_grad * selector, axis=0) + (
            1.0 - decay_rate
        ) * (square_grads[layer_index] / valid_total)
        eigen_act = spread(local_act, "owner", owner_now)
        eigen_grad = spread(local_grad, "owner", owner_now)
        replace_rows = ((jnp.arange(slot_count) == slot_rank) & (own_index == owner_now))[:, None]
        new_act = jnp.where(replace_rows, eigen_act[None, :], new_act)
        new_grad = jnp.where(replace_rows, eigen_grad[None, :], new_grad)
        damping = damping_rate * jnp.mean(eigen_grad) * jnp.mean(eigen_act)
        grad_eigen = lax.dynamic_slice_in_dim(eigen_grad, dp_index * tile_rows, tile_rows)
        act_eigen = lax.dynamic_slice_in_dim(eigen_act, own_index * tile_cols, tile_cols)
        scaled = gram_tiles[layer_index] / (grad_eigen[:, None] * act_eigen[None, :] + damping)
        results.append(scaled.astype(jnp.bfloat16))
    return (jnp.stack(results), new_act, new_grad)


def flip(array, axis, mask):
    return lax.ppermute(array, axis, [(i, i ^ mask) for i in range(lax.axis_size(axis))])


def hop(array, pairs):
    owners = lax.axis_size("owner")
    flat = [(a * owners + b, c * owners + e) for (a, b), (c, e) in pairs]
    return lax.ppermute(array, ("dp", "owner"), flat)


def project_rows(scalars, tokens, pieces, basis, n_own, n_dp):
    layers, tok_rows, _ = tokens.shape
    tile, cols = basis.shape[1:]
    part_rows = tok_rows // n_own
    packed = 3 * n_dp * tok_rows // 4
    half = packed // 2
    shapes = [(layers, half, cols)] * 2

    def kernel(scalar_ref, tokens_hbm, basis_hbm, *refs):
        piece_refs, refs = refs[: len(pieces)], refs[len(pieces) :]
        out_refs, (tokens_ref, basis_ref, sems) = refs[: len(shapes)], refs[len(shapes) :]
        dp, own = scalar_ref[0], scalar_ref[1]
        at = pl.ds(pl.multiple_of(dp * tile, tile), tile)
        copies = []
        for layer in range(layers):
            copies.append(
                [
                    pltpu.make_async_copy(
                        tokens_hbm.at[layer, :, at], tokens_ref.at[layer], sems.at[2 * layer]
                    ),
                    pltpu.make_async_copy(basis_hbm.at[layer], basis_ref.at[layer], sems.at[2 * layer + 1]),
                ]
            )
            for copy in copies[-1]:
                copy.start()
        col = lax.broadcasted_iota(jnp.int32, (1, n_dp * tok_rows), 1)
        turn = (col - tok_rows) // part_rows
        peer = turn // (n_dp - 1)
        peer = own ^ (((peer & 1) << 1) | (peer >> 1))
        mine = col < tok_rows
        mask = jnp.where(mine, 0, turn % (n_dp - 1) + 1)
        index = jnp.where(mine, col, peer * part_rows + col % part_rows)
        place = jnp.full_like(col, -1)
        for number in range(n_dp):
            shard = dp ^ number
            start = jnp.int32(0)
            for other in range(n_dp):
                start += jnp.where(other < shard, scalar_ref[2 + other], 0)
            here = (mask == number) & (index < scalar_ref[2 + shard])
            place = jnp.where(here, start + index, place)
        row = lax.broadcasted_iota(jnp.int32, (packed, n_dp * tok_rows), 0)
        row = row + jnp.where(dp % 2 == 0, 0, jnp.where(row < half, half, -half))
        select = (row == place).astype(jnp.bfloat16)
        for layer in range(layers):
            copies[layer][0].wait()
            rows = jnp.concatenate([tokens_ref[layer]] + [p[layer] for p in piece_refs], axis=0)
            chosen = jnp.dot(select, rows, preferred_element_type=jnp.float32).astype(jnp.bfloat16)
            copies[layer][1].wait()
            result = jnp.dot(chosen, basis_ref[layer], preferred_element_type=jnp.float32).astype(
                jnp.bfloat16
            )
            out_refs[0][layer] = result[:half]
            out_refs[1][layer] = result[half:]

    return pl.pallas_call(
        kernel,
        out_shape=[jax.ShapeDtypeStruct(shape, jnp.bfloat16) for shape in shapes],
        in_specs=[scalar_spec] + [pl.BlockSpec(memory_space=pltpu.HBM), pl.BlockSpec(memory_space=pl.ANY)] + [vmem_spec] * len(pieces),
        out_specs=[vmem_spec] * len(shapes),
        scratch_shapes=[
            pltpu.VMEM((layers, tok_rows, tile), jnp.bfloat16),
            pltpu.VMEM((layers, tile, cols), jnp.bfloat16),
            pltpu.SemaphoreType.DMA((2 * layers,)),
        ],
        compiler_params=pltpu.CompilerParams(vmem_limit_bytes=16 * 1024 * 1024),
        cost_estimate=light,
    )(scalars, pltpu.with_memory_space_constraint(tokens, pltpu.HBM), basis, *pieces)


def add(*pairs):
    layers = pairs[0][0].shape[0]

    def kernel(*refs):
        for number in range(len(pairs)):
            total = refs[2 * number][...].astype(jnp.float32) + refs[2 * number + 1][...].astype(jnp.float32)
            refs[-1][number * layers : (number + 1) * layers] = total.astype(refs[-1].dtype)

    first = pairs[0][0]
    return pl.pallas_call(
        kernel,
        out_shape=jax.ShapeDtypeStruct((layers * len(pairs), *first.shape[1:]), first.dtype),
        in_specs=[vmem_spec] * (2 * len(pairs)),
        out_specs=vmem_spec,
        compiler_params=pltpu.CompilerParams(vmem_limit_bytes=8 * 1024 * 1024),
        cost_estimate=light,
    )(*[array for pair in pairs for array in pair])


def add_rows(near, far, cut):
    layers, height, cols = near.shape
    spans = [(0, cut), (cut, height)]

    def kernel(near_ref, far_ref, *out_refs):
        for out_ref, (start, stop) in zip(out_refs, spans, strict=True):
            total = near_ref[:, start:stop].astype(jnp.float32) + far_ref[:, start:stop].astype(jnp.float32)
            out_ref[...] = total.astype(out_ref.dtype)

    return pl.pallas_call(
        kernel,
        out_shape=[jax.ShapeDtypeStruct((layers, stop - start, cols), near.dtype) for start, stop in spans],
        in_specs=[vmem_spec] * 2,
        out_specs=[vmem_spec] * len(spans),
        compiler_params=pltpu.CompilerParams(vmem_limit_bytes=8 * 1024 * 1024),
        cost_estimate=light,
    )(near, far)


def by_layer(nears, fars):
    layers, _, cols = nears[0].shape
    count = len(nears)
    height = sum(array.shape[1] for array in nears)

    def kernel(*refs):
        for side in range(2):
            start = 0
            for ref in refs[side * count : (side + 1) * count]:
                for layer, out_ref in enumerate(refs[2 * count :]):
                    out_ref[side, start : start + ref.shape[1]] = ref[layer]
                start += ref.shape[1]

    return pl.pallas_call(
        kernel,
        out_shape=[jax.ShapeDtypeStruct((2, height, cols), nears[0].dtype)] * layers,
        in_specs=[vmem_spec] * (2 * count),
        out_specs=[vmem_spec] * layers,
        compiler_params=pltpu.CompilerParams(vmem_limit_bytes=8 * 1024 * 1024),
        cost_estimate=light,
    )(*nears, *fars)


def join(arrays):
    layers, rows, cols = arrays[0].shape

    def kernel(*refs):
        for number, ref in enumerate(refs[:-1]):
            refs[-1][:, number * rows : (number + 1) * rows] = ref[...]

    return pl.pallas_call(
        kernel,
        out_shape=jax.ShapeDtypeStruct((layers, len(arrays) * rows, cols), arrays[0].dtype),
        in_specs=[vmem_spec] * len(arrays),
        out_specs=vmem_spec,
        compiler_params=pltpu.CompilerParams(vmem_limit_bytes=8 * 1024 * 1024),
        cost_estimate=light,
    )(*arrays)


def cut_rows(arrays, tile, n_own, n_dp):
    layers, tok_rows, _ = arrays[0].shape
    part_rows = tok_rows // n_own
    peers = n_dp - 1

    def kernel(*refs):
        in_refs, out_refs, sems = refs[: len(arrays)], refs[len(arrays) : -1], refs[-1]
        dp, own = lax.axis_index("dp"), lax.axis_index("owner")
        rows = pl.ds(pl.multiple_of(own * part_rows, part_rows), part_rows)
        copies = []
        for number, out_ref in enumerate(out_refs):
            block = dp ^ (number % peers + 1)
            cols = pl.ds(pl.multiple_of(block * tile, tile), tile)
            copies.append(
                pltpu.make_async_copy(in_refs[number // peers].at[:, rows, cols], out_ref, sems.at[number])
            )
            copies[-1].start()
        for copy in copies:
            copy.wait()

    count = len(arrays) * peers
    return pl.pallas_call(
        kernel,
        out_shape=[jax.ShapeDtypeStruct((layers, part_rows, tile), arrays[0].dtype)] * count,
        in_specs=[pl.BlockSpec(memory_space=pltpu.HBM)] * len(arrays),
        out_specs=[vmem_spec] * count,
        scratch_shapes=[pltpu.SemaphoreType.DMA((count,))],
        compiler_params=pltpu.CompilerParams(vmem_limit_bytes=8 * 1024 * 1024),
        cost_estimate=light,
    )(*[pltpu.with_memory_space_constraint(array, pltpu.HBM) for array in arrays])


def pick(home, choices):
    flat = [array for arrays in choices for array in arrays]
    count = len(choices[0])

    def kernel(home_ref, *refs):
        for index in range(count):

            @pl.when(home_ref[0] == index)
            def _(index=index):
                for number, out_ref in enumerate(refs[len(flat) :]):
                    out_ref[...] = refs[number * count + index][...]

    return pl.pallas_call(
        kernel,
        out_shape=[jax.ShapeDtypeStruct(arrays[0].shape, arrays[0].dtype) for arrays in choices],
        in_specs=[scalar_spec] + [vmem_spec] * len(flat),
        out_specs=[vmem_spec] * len(choices),
        compiler_params=pltpu.CompilerParams(vmem_limit_bytes=12 * 1024 * 1024),
        cost_estimate=light,
    )(home, *flat)


def squares_of(aside, panels):
    layers, _, cols = panels[0].shape

    def kernel(aside_ref, *refs):
        for layer in range(layers):
            total = jnp.zeros((1, cols), jnp.float32)
            for ref in refs[:-1]:
                wide = ref[layer].astype(jnp.float32)
                total += jnp.sum(wide * wide, axis=0, keepdims=True)
            refs[-1][layer : layer + 1] = jnp.where(aside_ref[0] == 0, total, 0.0)

    return pl.pallas_call(
        kernel,
        out_shape=jax.ShapeDtypeStruct((layers, cols), jnp.float32),
        in_specs=[scalar_spec] + [vmem_spec] * len(panels),
        out_specs=vmem_spec,
        compiler_params=pltpu.CompilerParams(vmem_limit_bytes=8 * 1024 * 1024),
        cost_estimate=light,
    )(aside, *panels)


def halves_of(act, near, far):
    layers, _, cols = act.shape

    def kernel(act_ref, near_ref, far_ref, out_ref):
        for layer in range(layers):
            wide = act_ref[layer].astype(jnp.float32)
            out_ref[layer : layer + 1] = jnp.sum(wide * wide, axis=0, keepdims=True)
        out_ref[layers:] = near_ref[...] + far_ref[...]

    return pl.pallas_call(
        kernel,
        out_shape=jax.ShapeDtypeStruct((2 * layers, cols), jnp.float32),
        in_specs=[vmem_spec] * 3,
        out_specs=vmem_spec,
        compiler_params=pltpu.CompilerParams(vmem_limit_bytes=8 * 1024 * 1024),
        cost_estimate=light,
    )(act, near, far)


def total_of(near, far):
    def kernel(near_ref, far_ref, out_ref):
        out_ref[...] = near_ref[...] + far_ref[...]

    return pl.pallas_call(
        kernel,
        out_shape=jax.ShapeDtypeStruct(near.shape, near.dtype),
        in_specs=[vmem_spec] * 2,
        out_specs=vmem_spec,
        compiler_params=pltpu.CompilerParams(vmem_limit_bytes=4 * 1024 * 1024),
        cost_estimate=light,
    )(near, far)


def gram_of(grads, act):
    layers, _, cols = act.shape

    def kernel(*refs):
        for layer in range(layers):
            refs[-1][layer] = product_of(refs[layer][0], refs[-2][layer])

    return pl.pallas_call(
        kernel,
        out_shape=jax.ShapeDtypeStruct((layers, grads[0].shape[2], cols), jnp.float32),
        in_specs=[vmem_spec] * (layers + 1),
        out_specs=vmem_spec,
        compiler_params=pltpu.CompilerParams(vmem_limit_bytes=16 * 1024 * 1024),
        cost_estimate=light,
    )(*grads, act)


def product_of(grad, act):
    return lax.dot_general(grad, act, (((0,), (0,)), ((), ())), preferred_element_type=jnp.float32)


def finish(grads, act, grams, factors):
    layers, tile, cols = grams.shape

    def kernel(*refs):
        grad_refs, (act_ref, gram_ref, factor_ref, out_ref) = refs[:layers], refs[layers:]
        for layer in range(layers):
            gram = gram_ref[layer] + product_of(grad_refs[layer][1], act_ref[layer])
            out_ref[layer] = (gram * factor_ref[layer]).astype(jnp.bfloat16)

    return pl.pallas_call(
        kernel,
        out_shape=jax.ShapeDtypeStruct((layers, tile, cols), jnp.bfloat16),
        in_specs=[vmem_spec] * (layers + 3),
        out_specs=vmem_spec,
        compiler_params=pltpu.CompilerParams(vmem_limit_bytes=24 * 1024 * 1024),
        cost_estimate=light,
    )(*grads, act, grams, factors)


def eigenvalues(scalars, states, packets, n_dp):
    n_own = len(packets)
    layers, tile = packets[0].shape[0] // 2, packets[0].shape[1]
    slot_count, width = states[0].shape[0] // 2, states[0].shape[1]

    def kernel(scalar_ref, *refs):
        state_refs, packet_refs, refs = refs[:n_own], refs[n_own : 2 * n_own], refs[2 * n_own :]
        out_ref, new_act_ref, new_grad_ref, act_full, grad_full = refs
        dp, own = scalar_ref[0], scalar_ref[1]
        total = scalar_ref[2]
        for index in range(1, n_dp):
            total += scalar_ref[2 + index]
        total = total.astype(jnp.float32)
        owners = [scalar_ref[2 + n_dp + layer] for layer in range(layers)]
        for mask in range(n_own):
            at = pl.ds(pl.multiple_of((own ^ mask) * tile, tile), tile)
            act_full[:, at] = packet_refs[mask][:layers] / total
            at = pl.ds(pl.multiple_of((n_own - (own ^ mask)) % n_own * tile, tile), tile)
            grad_full[:, at] = packet_refs[mask][layers:] / total
        new_act_ref[...] = state_refs[0][:slot_count]
        new_grad_ref[...] = state_refs[0][slot_count:]
        for layer in range(layers):
            owner_now = owners[layer]
            rank = jnp.int32(0)
            for earlier in range(layer):
                rank += jnp.where(owners[earlier] == owner_now, 1, 0)
            old_act = jnp.zeros((1, width), jnp.float32)
            old_grad = jnp.zeros((1, width), jnp.float32)
            for mask in range(n_own):
                for slot in range(slot_count):
                    here = (owner_now == own ^ mask) & (rank == slot)
                    down = slot_count + slot
                    old_act = jnp.where(here, state_refs[mask][slot : slot + 1], old_act)
                    old_grad = jnp.where(here, state_refs[mask][down : down + 1], old_grad)
            eigen_act = decay_rate * old_act + (1.0 - decay_rate) * act_full[layer : layer + 1]
            eigen_grad = decay_rate * old_grad + (1.0 - decay_rate) * grad_full[layer : layer + 1]
            act_full[layer : layer + 1] = eigen_act
            grad_full[layer : layer + 1] = eigen_grad
            for slot in range(slot_count):

                @pl.when((owner_now == own) & (rank == slot))
                def _(slot=slot, eigen_act=eigen_act, eigen_grad=eigen_grad):
                    new_act_ref[slot : slot + 1] = eigen_act
                    new_grad_ref[slot : slot + 1] = eigen_grad

            damping = damping_rate * (jnp.sum(eigen_grad) / width) * (jnp.sum(eigen_act) / width)
            rows = grad_full[layer : layer + 1, pl.ds(pl.multiple_of(dp * tile, tile), tile)]
            cols = act_full[layer : layer + 1, pl.ds(pl.multiple_of(own * tile, tile), tile)]
            rows = jnp.transpose(jnp.broadcast_to(rows, (128, tile)))
            rows = jnp.concatenate([rows] * (tile // 128), axis=1)
            out_ref[layer] = 1.0 / (total * (rows * cols + damping))

    out_shape = [
        jax.ShapeDtypeStruct((layers, tile, tile), jnp.float32),
        jax.ShapeDtypeStruct((slot_count, width), jnp.float32),
        jax.ShapeDtypeStruct((slot_count, width), jnp.float32),
    ]
    return pl.pallas_call(
        kernel,
        out_shape=out_shape,
        in_specs=[scalar_spec] + [vmem_spec] * (2 * n_own),
        out_specs=[vmem_spec] * len(out_shape),
        scratch_shapes=[pltpu.VMEM((layers, width), jnp.float32)] * 2,
        compiler_params=pltpu.CompilerParams(vmem_limit_bytes=16 * 1024 * 1024),
        cost_estimate=light,
    )(scalars, *states, *packets)


def line_plan(activations, out_grads, basis_act, basis_grad, owner_of, counts, state_act, state_grad):
    layers, tok_rows, width = activations.shape
    tile = basis_act.shape[1]
    n_dp = lax.axis_size("dp")
    n_own = lax.axis_size("owner")
    dp = lax.axis_index("dp")
    own = lax.axis_index("owner")
    scalars = jnp.concatenate([jnp.stack([dp, own]), counts, owner_of]).astype(jnp.int32)

    def after(array, *others):
        return lax.optimization_barrier((array, *others))[0]

    def step(arrays, *others):
        return lax.optimization_barrier((*arrays, *others))[: len(arrays)]

    owners = range(n_own)
    held = [-o % n_own for o in owners]
    cuts = cut_rows((out_grads, activations), tile, n_own, n_dp)
    cuts = [flip(cut, "dp", number % (n_dp - 1) + 1) for number, cut in enumerate(cuts)]
    got_grad, got_act = cuts[: n_dp - 1], cuts[n_dp - 1 :]
    pieces = got_grad[:-1] + [after(got_grad[-1], got_act[0])]
    pieces += [flip(piece, "owner", 2) for piece in pieces]
    pieces += [flip(piece, "owner", 1) for piece in pieces]
    stay = pltpu.with_memory_space_constraint(basis_grad, pltpu.HBM)
    keep, send = project_rows(scalars, out_grads, pieces, stay, n_own, n_dp)

    near = flip(after(send, *got_act), "dp", 1)
    pieces = [join(got_act[:-1]), got_act[-1]]
    pieces += [flip(after(piece, keep), "owner", 2) for piece in pieces]
    pieces += [flip(piece, "owner", 1) for piece in pieces]
    stay = pltpu.with_memory_space_constraint(basis_act, pltpu.HBM)
    keep_act, send_act = project_rows(scalars, activations, pieces, stay, n_own, n_dp)

    state = jnp.concatenate([state_act, state_grad], axis=0)
    keep, near, keep_act, send_act, state = step([keep, near, keep_act, send_act, state])
    states = [state] + [flip(state, "owner", mask) for mask in range(1, n_own)]
    parts = add_rows(keep, near, keep.shape[1] // 2)
    parts = [lax.ppermute(array, "owner", [*enumerate(held)]) for array in parts]
    to_pair = [((a, o), (a ^ 2, o)) for a in range(n_dp) for o in owners if (a ^ held[o]) & 2]
    crosses = [hop(array, to_pair) for array in parts]
    near_act = flip(send_act, "dp", 1)

    crosses[0] = after(crosses[0], *states)
    nears = [add(pair) for pair in zip(parts, crosses, strict=True)]
    aside = ((dp ^ (-own % n_own)) // 2).astype(jnp.int32)[None]
    square_grad = squares_of(aside, nears)
    square_far = flip(square_grad, "dp", 2)
    fars = [hop(array, [((held[o] ^ 1, o), (held[o], o)) for o in owners]) for array in nears]
    full = by_layer(nears, fars)
    chip = [hop(array, [((held[o], o), (held[o], o ^ 2)) for o in owners]) for array in full]

    part_act = add((keep_act, near_act))
    cross_act = flip(part_act, "dp", 2)

    done = step([part_act, cross_act, square_grad, square_far, *full, *chip])
    (part_act, cross_act, square_grad, square_far), full, chip = done[:4], done[4:][:layers], done[4 + layers :]
    full_act = add((part_act, cross_act))
    half = halves_of(full_act, square_grad, square_far)
    packet = total_of(half, flip(half, "dp", 1))
    back_act = flip(after(full_act, packet), "dp", 1)
    packets = [packet] + [flip(packet, "owner", mask) for mask in range(1, n_own)]
    source = -dp % n_own
    home = jnp.where(own == source, 0, jnp.where(own == source ^ 2, 1, 2)).astype(jnp.int32)[None]
    full = pick(after(home, *packets), [*zip(full, chip, strict=True)])
    to_core = [((held[o], o ^ b), (held[o], o ^ b ^ 1)) for o in owners for b in (0, 2)]
    core = [hop(array, to_core) for array in full]
    factors, new_act, new_grad = eigenvalues(scalars, states, packets, n_dp)
    grads = pick(home // 2, [*zip(full, core, strict=True)])
    grams = gram_of(grads, full_act)

    grams, factors, back_act, *grads = step([grams, factors, back_act, *grads])
    return finish(grads, back_act, grams, factors), new_act, new_grad


def solution(mesh):
    placed = (
        P("groups", "dp", None),
        P("groups", "dp", None),
        P("groups", "dp", "owner"),
        P("groups", "dp", "owner"),
        P(),
        P("groups"),
        P("owner", "groups"),
        P("owner", "groups"),
    )
    square = mesh.shape["dp"] == 4 and mesh.shape["owner"] == 4
    return jax.shard_map(
        line_plan if square else gather_plan,
        mesh=mesh,
        in_specs=placed,
        out_specs=(P("groups", "dp", "owner"), P("owner", "groups"), P("owner", "groups")),
        check_vma=False,
    )
```

```python
import jax
import jax.numpy as jnp
from jax import lax
from jax.experimental import pallas as pl
from jax.experimental.pallas import tpu as pltpu
from jax.sharding import PartitionSpec as P

decay_rate = 0.25
damping_rate = 0.1
vmem_spec = pl.BlockSpec(memory_space=pltpu.VMEM)
scalar_spec = pl.BlockSpec(memory_space=pltpu.SMEM)
light = pl.CostEstimate(flops=0, bytes_accessed=0, transcendentals=0)


def spread(array, axis, root):
    mine = lax.axis_index(axis) == root
    return lax.psum(jnp.where(mine, array, jnp.zeros_like(array)), axis)


def gather_plan(activations, out_grads, basis_act, basis_grad, owner_of, counts, state_act, state_grad):
    layers = activations.shape[0]
    tok_rows = activations.shape[1]
    tile_rows = basis_act.shape[1]
    tile_cols = basis_act.shape[2]
    slot_count = state_act.shape[0]
    dp_index = lax.axis_index("dp")
    own_index = lax.axis_index("owner")
    valid_rows = (jnp.arange(tok_rows) < counts[dp_index]).astype(jnp.float32)[:, None]
    valid_total = jnp.sum(counts).astype(jnp.float32)
    square_acts = []
    square_grads = []
    gram_tiles = []
    for layer_index in range(layers):
        panel_act = jnp.dot(
            activations[layer_index],
            lax.all_gather(basis_act[layer_index], "dp", axis=0, tiled=True),
            preferred_element_type=jnp.float32,
        )
        panel_grad = jnp.dot(
            out_grads[layer_index],
            lax.all_gather(basis_grad[layer_index], "dp", axis=0, tiled=True),
            preferred_element_type=jnp.float32,
        )
        panel_act = (panel_act * valid_rows).astype(jnp.bfloat16)
        panel_grad = (panel_grad * valid_rows).astype(jnp.bfloat16)
        full_act = lax.all_gather(panel_act, "owner", axis=1, tiled=True)
        full_grad = lax.all_gather(panel_grad, "owner", axis=1, tiled=True)
        square_act = jnp.sum(jnp.square(full_act.astype(jnp.float32)), axis=0)
        square_grad = jnp.sum(jnp.square(full_grad.astype(jnp.float32)), axis=0)
        gram_term = lax.dot_general(
            full_grad, panel_act, (((0,), (0,)), ((), ())), preferred_element_type=jnp.float32
        )
        gram_tiles.append(
            lax.psum_scatter(
                gram_term.astype(jnp.bfloat16), "dp", scatter_dimension=0, tiled=True
            ).astype(jnp.float32)
            / valid_total
        )
        square_act, square_grad = lax.psum((square_act, square_grad), "dp")
        square_acts.append(square_act)
        square_grads.append(square_grad)
    new_act = state_act
    new_grad = state_grad
    results = []
    for layer_index in range(layers):
        owner_now = owner_of[layer_index]
        slot_rank = jnp.sum((owner_of[:layer_index] == owner_now).astype(jnp.int32))
        selector = (jnp.arange(slot_count) == slot_rank).astype(jnp.float32)[:, None]
        local_act = decay_rate * jnp.sum(state_act * selector, axis=0) + (
            1.0 - decay_rate
        ) * (square_acts[layer_index] / valid_total)
        local_grad = decay_rate * jnp.sum(state_grad * selector, axis=0) + (
            1.0 - decay_rate
        ) * (square_grads[layer_index] / valid_total)
        eigen_act = spread(local_act, "owner", owner_now)
        eigen_grad = spread(local_grad, "owner", owner_now)
        replace_rows = ((jnp.arange(slot_count) == slot_rank) & (own_index == owner_now))[:, None]
        new_act = jnp.where(replace_rows, eigen_act[None, :], new_act)
        new_grad = jnp.where(replace_rows, eigen_grad[None, :], new_grad)
        damping = damping_rate * jnp.mean(eigen_grad) * jnp.mean(eigen_act)
        grad_eigen = lax.dynamic_slice_in_dim(eigen_grad, dp_index * tile_rows, tile_rows)
        act_eigen = lax.dynamic_slice_in_dim(eigen_act, own_index * tile_cols, tile_cols)
        scaled = gram_tiles[layer_index] / (grad_eigen[:, None] * act_eigen[None, :] + damping)
        results.append(scaled.astype(jnp.bfloat16))
    return (jnp.stack(results), new_act, new_grad)


def flip(array, axis, mask):
    return lax.ppermute(array, axis, [(i, i ^ mask) for i in range(lax.axis_size(axis))])


def hop(array, pairs):
    owners = lax.axis_size("owner")
    flat = [(a * owners + b, c * owners + e) for (a, b), (c, e) in pairs]
    return lax.ppermute(array, ("dp", "owner"), flat)


def load(arrays, cut, *gates):
    tile = arrays[-1].shape[1]
    shapes = [(*array.shape[:2], tile) if number < cut else array.shape for number, array in enumerate(arrays)]

    def kernel(*refs):
        in_refs, out_refs, sems = refs[: len(arrays)], refs[len(arrays) + len(gates) : -1], refs[-1]
        cols = pl.ds(pl.multiple_of(lax.axis_index("dp") * tile, tile), tile)
        copies = []
        for number, (in_ref, out_ref) in enumerate(zip(in_refs, out_refs, strict=True)):
            source = in_ref.at[:, :, cols] if number < cut else in_ref
            copies.append(pltpu.make_async_copy(source, out_ref, sems.at[number]))
            copies[-1].start()
        for copy in copies:
            copy.wait()

    return pl.pallas_call(
        kernel,
        out_shape=[
            jax.ShapeDtypeStruct(shape, array.dtype) for shape, array in zip(shapes, arrays, strict=True)
        ],
        in_specs=[pl.BlockSpec(memory_space=pltpu.HBM)] * len(arrays) + [pl.BlockSpec(memory_space=pl.ANY)] * len(gates),
        out_specs=[vmem_spec] * len(arrays),
        scratch_shapes=[pltpu.SemaphoreType.DMA((len(arrays),))],
        compiler_params=pltpu.CompilerParams(vmem_limit_bytes=8 * 1024 * 1024),
        cost_estimate=light,
    )(*[pltpu.with_memory_space_constraint(array, pltpu.HBM) for array in arrays], *gates)


def project_rows(scalars, tokens, pieces, basis, n_own, n_dp):
    layers, tok_rows, tile = tokens.shape
    cols = basis.shape[2]
    part_rows = tok_rows // n_own
    packed = 3 * n_dp * tok_rows // 4
    half = packed // 2
    shapes = [(layers, half, cols)] * 2

    def kernel(scalar_ref, tokens_ref, basis_ref, *refs):
        piece_refs, out_refs = refs[: len(pieces)], refs[len(pieces) :]
        dp, own = scalar_ref[0], scalar_ref[1]
        col = lax.broadcasted_iota(jnp.int32, (1, n_dp * tok_rows), 1)
        turn = (col - tok_rows) // part_rows
        peer = turn // (n_dp - 1)
        peer = own ^ (((peer & 1) << 1) | (peer >> 1))
        mine = col < tok_rows
        mask = jnp.where(mine, 0, turn % (n_dp - 1) + 1)
        index = jnp.where(mine, col, peer * part_rows + col % part_rows)
        place = jnp.full_like(col, -1)
        for number in range(n_dp):
            shard = dp ^ number
            start = jnp.int32(0)
            for other in range(n_dp):
                start += jnp.where(other < shard, scalar_ref[2 + other], 0)
            here = (mask == number) & (index < scalar_ref[2 + shard])
            place = jnp.where(here, start + index, place)
        row = lax.broadcasted_iota(jnp.int32, (packed, n_dp * tok_rows), 0)
        row = row + jnp.where(dp % 2 == 0, 0, jnp.where(row < half, half, -half))
        select = (row == place).astype(jnp.bfloat16)
        for layer in range(layers):
            rows = jnp.concatenate([tokens_ref[layer]] + [p[layer] for p in piece_refs], axis=0)
            chosen = jnp.dot(select, rows, preferred_element_type=jnp.float32).astype(jnp.bfloat16)
            result = jnp.dot(chosen, basis_ref[layer], preferred_element_type=jnp.float32).astype(
                jnp.bfloat16
            )
            out_refs[0][layer] = result[:half]
            out_refs[1][layer] = result[half:]

    return pl.pallas_call(
        kernel,
        out_shape=[jax.ShapeDtypeStruct(shape, jnp.bfloat16) for shape in shapes],
        in_specs=[scalar_spec] + [vmem_spec] * (2 + len(pieces)),
        out_specs=[vmem_spec] * len(shapes),
        compiler_params=pltpu.CompilerParams(vmem_limit_bytes=16 * 1024 * 1024),
        cost_estimate=light,
    )(scalars, tokens, basis, *pieces)


def add(*pairs):
    layers = pairs[0][0].shape[0]

    def kernel(*refs):
        for number in range(len(pairs)):
            total = refs[2 * number][...].astype(jnp.float32) + refs[2 * number + 1][...].astype(jnp.float32)
            refs[-1][number * layers : (number + 1) * layers] = total.astype(refs[-1].dtype)

    first = pairs[0][0]
    return pl.pallas_call(
        kernel,
        out_shape=jax.ShapeDtypeStruct((layers * len(pairs), *first.shape[1:]), first.dtype),
        in_specs=[vmem_spec] * (2 * len(pairs)),
        out_specs=vmem_spec,
        compiler_params=pltpu.CompilerParams(vmem_limit_bytes=8 * 1024 * 1024),
        cost_estimate=light,
    )(*[array for pair in pairs for array in pair])


def add_rows(near, far, cut):
    layers, height, cols = near.shape
    spans = [(0, cut), (cut, height)]

    def kernel(near_ref, far_ref, *out_refs):
        for out_ref, (start, stop) in zip(out_refs, spans, strict=True):
            total = near_ref[:, start:stop].astype(jnp.float32) + far_ref[:, start:stop].astype(jnp.float32)
            out_ref[...] = total.astype(out_ref.dtype)

    return pl.pallas_call(
        kernel,
        out_shape=[jax.ShapeDtypeStruct((layers, stop - start, cols), near.dtype) for start, stop in spans],
        in_specs=[vmem_spec] * 2,
        out_specs=[vmem_spec] * len(spans),
        compiler_params=pltpu.CompilerParams(vmem_limit_bytes=8 * 1024 * 1024),
        cost_estimate=light,
    )(near, far)


def by_layer(nears, fars):
    layers, _, cols = nears[0].shape
    count = len(nears)
    height = sum(array.shape[1] for array in nears)

    def kernel(*refs):
        for side in range(2):
            start = 0
            for ref in refs[side * count : (side + 1) * count]:
                for layer, out_ref in enumerate(refs[2 * count :]):
                    out_ref[side, start : start + ref.shape[1]] = ref[layer]
                start += ref.shape[1]

    return pl.pallas_call(
        kernel,
        out_shape=[jax.ShapeDtypeStruct((2, height, cols), nears[0].dtype)] * layers,
        in_specs=[vmem_spec] * (2 * count),
        out_specs=[vmem_spec] * layers,
        compiler_params=pltpu.CompilerParams(vmem_limit_bytes=8 * 1024 * 1024),
        cost_estimate=light,
    )(*nears, *fars)


def join(arrays):
    layers, rows, cols = arrays[0].shape

    def kernel(*refs):
        for number, ref in enumerate(refs[:-1]):
            refs[-1][:, number * rows : (number + 1) * rows] = ref[...]

    return pl.pallas_call(
        kernel,
        out_shape=jax.ShapeDtypeStruct((layers, len(arrays) * rows, cols), arrays[0].dtype),
        in_specs=[vmem_spec] * len(arrays),
        out_specs=vmem_spec,
        compiler_params=pltpu.CompilerParams(vmem_limit_bytes=8 * 1024 * 1024),
        cost_estimate=light,
    )(*arrays)


def cut_rows(arrays, tile, n_own, n_dp):
    layers, tok_rows, _ = arrays[0].shape
    part_rows = tok_rows // n_own
    peers = n_dp - 1

    def kernel(*refs):
        in_refs, out_refs, sems = refs[: len(arrays)], refs[len(arrays) : -1], refs[-1]
        dp, own = lax.axis_index("dp"), lax.axis_index("owner")
        rows = pl.ds(pl.multiple_of(own * part_rows, part_rows), part_rows)
        copies = []
        for number, out_ref in enumerate(out_refs):
            block = dp ^ (number % peers + 1)
            cols = pl.ds(pl.multiple_of(block * tile, tile), tile)
            copies.append(
                pltpu.make_async_copy(in_refs[number // peers].at[:, rows, cols], out_ref, sems.at[number])
            )
            copies[-1].start()
        for copy in copies:
            copy.wait()

    count = len(arrays) * peers
    return pl.pallas_call(
        kernel,
        out_shape=[jax.ShapeDtypeStruct((layers, part_rows, tile), arrays[0].dtype)] * count,
        in_specs=[pl.BlockSpec(memory_space=pltpu.HBM)] * len(arrays),
        out_specs=[vmem_spec] * count,
        scratch_shapes=[pltpu.SemaphoreType.DMA((count,))],
        compiler_params=pltpu.CompilerParams(vmem_limit_bytes=8 * 1024 * 1024),
        cost_estimate=light,
    )(*[pltpu.with_memory_space_constraint(array, pltpu.HBM) for array in arrays])


def pick(home, choices):
    flat = [array for arrays in choices for array in arrays]
    count = len(choices[0])

    def kernel(home_ref, *refs):
        for index in range(count):

            @pl.when(home_ref[0] == index)
            def _(index=index):
                for number, out_ref in enumerate(refs[len(flat) :]):
                    out_ref[...] = refs[number * count + index][...]

    return pl.pallas_call(
        kernel,
        out_shape=[jax.ShapeDtypeStruct(arrays[0].shape, arrays[0].dtype) for arrays in choices],
        in_specs=[scalar_spec] + [vmem_spec] * len(flat),
        out_specs=[vmem_spec] * len(choices),
        compiler_params=pltpu.CompilerParams(vmem_limit_bytes=12 * 1024 * 1024),
        cost_estimate=light,
    )(home, *flat)


def squares_of(aside, panels):
    layers, _, cols = panels[0].shape

    def kernel(aside_ref, *refs):
        for layer in range(layers):
            total = jnp.zeros((1, cols), jnp.float32)
            for ref in refs[:-1]:
                wide = ref[layer].astype(jnp.float32)
                total += jnp.sum(wide * wide, axis=0, keepdims=True)
            refs[-1][layer : layer + 1] = jnp.where(aside_ref[0] == 0, total, 0.0)

    return pl.pallas_call(
        kernel,
        out_shape=jax.ShapeDtypeStruct((layers, cols), jnp.float32),
        in_specs=[scalar_spec] + [vmem_spec] * len(panels),
        out_specs=vmem_spec,
        compiler_params=pltpu.CompilerParams(vmem_limit_bytes=8 * 1024 * 1024),
        cost_estimate=light,
    )(aside, *panels)


def halves_of(act, near, far):
    layers, _, cols = act.shape

    def kernel(act_ref, near_ref, far_ref, out_ref):
        for layer in range(layers):
            wide = act_ref[layer].astype(jnp.float32)
            out_ref[layer : layer + 1] = jnp.sum(wide * wide, axis=0, keepdims=True)
        out_ref[layers:] = near_ref[...] + far_ref[...]

    return pl.pallas_call(
        kernel,
        out_shape=jax.ShapeDtypeStruct((2 * layers, cols), jnp.float32),
        in_specs=[vmem_spec] * 3,
        out_specs=vmem_spec,
        compiler_params=pltpu.CompilerParams(vmem_limit_bytes=8 * 1024 * 1024),
        cost_estimate=light,
    )(act, near, far)


def total_of(near, far):
    def kernel(near_ref, far_ref, out_ref):
        out_ref[...] = near_ref[...] + far_ref[...]

    return pl.pallas_call(
        kernel,
        out_shape=jax.ShapeDtypeStruct(near.shape, near.dtype),
        in_specs=[vmem_spec] * 2,
        out_specs=vmem_spec,
        compiler_params=pltpu.CompilerParams(vmem_limit_bytes=4 * 1024 * 1024),
        cost_estimate=light,
    )(near, far)


def gram_of(grads, act):
    layers, _, cols = act.shape

    def kernel(*refs):
        for layer in range(layers):
            refs[-1][layer] = product_of(refs[layer][0], refs[-2][layer])

    return pl.pallas_call(
        kernel,
        out_shape=jax.ShapeDtypeStruct((layers, grads[0].shape[2], cols), jnp.float32),
        in_specs=[vmem_spec] * (layers + 1),
        out_specs=vmem_spec,
        compiler_params=pltpu.CompilerParams(vmem_limit_bytes=16 * 1024 * 1024),
        cost_estimate=light,
    )(*grads, act)


def product_of(grad, act):
    return lax.dot_general(grad, act, (((0,), (0,)), ((), ())), preferred_element_type=jnp.float32)


def finish(grads, act, grams, factors):
    layers, tile, cols = grams.shape

    def kernel(*refs):
        grad_refs, (act_ref, gram_ref, factor_ref, out_ref) = refs[:layers], refs[layers:]
        for layer in range(layers):
            gram = gram_ref[layer] + product_of(grad_refs[layer][1], act_ref[layer])
            out_ref[layer] = (gram * factor_ref[layer]).astype(jnp.bfloat16)

    return pl.pallas_call(
        kernel,
        out_shape=jax.ShapeDtypeStruct((layers, tile, cols), jnp.bfloat16),
        in_specs=[vmem_spec] * (layers + 3),
        out_specs=vmem_spec,
        compiler_params=pltpu.CompilerParams(vmem_limit_bytes=24 * 1024 * 1024),
        cost_estimate=light,
    )(*grads, act, grams, factors)


def eigenvalues(scalars, states, packets, n_dp):
    n_own = len(packets)
    layers, tile = packets[0].shape[0] // 2, packets[0].shape[1]
    slot_count, width = states[0].shape[0] // 2, states[0].shape[1]

    def kernel(scalar_ref, *refs):
        state_refs, packet_refs, refs = refs[:n_own], refs[n_own : 2 * n_own], refs[2 * n_own :]
        out_ref, new_act_ref, new_grad_ref, act_full, grad_full = refs
        dp, own = scalar_ref[0], scalar_ref[1]
        total = scalar_ref[2]
        for index in range(1, n_dp):
            total += scalar_ref[2 + index]
        total = total.astype(jnp.float32)
        owners = [scalar_ref[2 + n_dp + layer] for layer in range(layers)]
        for mask in range(n_own):
            at = pl.ds(pl.multiple_of((own ^ mask) * tile, tile), tile)
            act_full[:, at] = packet_refs[mask][:layers] / total
            at = pl.ds(pl.multiple_of((n_own - (own ^ mask)) % n_own * tile, tile), tile)
            grad_full[:, at] = packet_refs[mask][layers:] / total
        new_act_ref[...] = state_refs[0][:slot_count]
        new_grad_ref[...] = state_refs[0][slot_count:]
        for layer in range(layers):
            owner_now = owners[layer]
            rank = jnp.int32(0)
            for earlier in range(layer):
                rank += jnp.where(owners[earlier] == owner_now, 1, 0)
            old_act = jnp.zeros((1, width), jnp.float32)
            old_grad = jnp.zeros((1, width), jnp.float32)
            for mask in range(n_own):
                for slot in range(slot_count):
                    here = (owner_now == own ^ mask) & (rank == slot)
                    down = slot_count + slot
                    old_act = jnp.where(here, state_refs[mask][slot : slot + 1], old_act)
                    old_grad = jnp.where(here, state_refs[mask][down : down + 1], old_grad)
            eigen_act = decay_rate * old_act + (1.0 - decay_rate) * act_full[layer : layer + 1]
            eigen_grad = decay_rate * old_grad + (1.0 - decay_rate) * grad_full[layer : layer + 1]
            act_full[layer : layer + 1] = eigen_act
            grad_full[layer : layer + 1] = eigen_grad
            for slot in range(slot_count):

                @pl.when((owner_now == own) & (rank == slot))
                def _(slot=slot, eigen_act=eigen_act, eigen_grad=eigen_grad):
                    new_act_ref[slot : slot + 1] = eigen_act
                    new_grad_ref[slot : slot + 1] = eigen_grad

            damping = damping_rate * (jnp.sum(eigen_grad) / width) * (jnp.sum(eigen_act) / width)
            rows = grad_full[layer : layer + 1, pl.ds(pl.multiple_of(dp * tile, tile), tile)]
            cols = act_full[layer : layer + 1, pl.ds(pl.multiple_of(own * tile, tile), tile)]
            rows = jnp.transpose(jnp.broadcast_to(rows, (128, tile)))
            rows = jnp.concatenate([rows] * (tile // 128), axis=1)
            out_ref[layer] = 1.0 / (total * (rows * cols + damping))

    out_shape = [
        jax.ShapeDtypeStruct((layers, tile, tile), jnp.float32),
        jax.ShapeDtypeStruct((slot_count, width), jnp.float32),
        jax.ShapeDtypeStruct((slot_count, width), jnp.float32),
    ]
    return pl.pallas_call(
        kernel,
        out_shape=out_shape,
        in_specs=[scalar_spec] + [vmem_spec] * (2 * n_own),
        out_specs=[vmem_spec] * len(out_shape),
        scratch_shapes=[pltpu.VMEM((layers, width), jnp.float32)] * 2,
        compiler_params=pltpu.CompilerParams(vmem_limit_bytes=16 * 1024 * 1024),
        cost_estimate=light,
    )(scalars, *states, *packets)


def line_plan(activations, out_grads, basis_act, basis_grad, owner_of, counts, state_act, state_grad):
    layers, tok_rows, width = activations.shape
    tile = basis_act.shape[1]
    n_dp = lax.axis_size("dp")
    n_own = lax.axis_size("owner")
    dp = lax.axis_index("dp")
    own = lax.axis_index("owner")
    scalars = jnp.concatenate([jnp.stack([dp, own]), counts, owner_of]).astype(jnp.int32)

    def after(array, *others):
        return lax.optimization_barrier((array, *others))[0]

    def step(arrays, *others):
        return lax.optimization_barrier((*arrays, *others))[: len(arrays)]

    owners = range(n_own)
    held = [-o % n_own for o in owners]
    cuts = cut_rows((out_grads, activations), tile, n_own, n_dp)
    cuts = [flip(cut, "dp", number % (n_dp - 1) + 1) for number, cut in enumerate(cuts)]
    got_grad, got_act = cuts[: n_dp - 1], cuts[n_dp - 1 :]
    own_grad, stay_grad = load((out_grads, basis_grad), 1)
    pieces = got_grad[:-1] + [after(got_grad[-1], got_act[0], own_grad)]
    pieces += [flip(piece, "owner", 2) for piece in pieces]
    pieces += [flip(piece, "owner", 1) for piece in pieces]
    keep, send = project_rows(scalars, own_grad, pieces, stay_grad, n_own, n_dp)

    near = flip(after(send, *got_act), "dp", 1)
    pieces = [join(got_act[:-1]), got_act[-1]]
    pieces += [flip(after(piece, keep), "owner", 2) for piece in pieces]
    own_act, stay_act = load((activations, basis_act), 1, keep)
    pieces += [flip(after(piece, own_act), "owner", 1) for piece in pieces]
    keep_act, send_act = project_rows(scalars, own_act, pieces, stay_act, n_own, n_dp)

    state = jnp.concatenate([state_act, state_grad], axis=0)
    keep, near, keep_act, send_act, state = step([keep, near, keep_act, send_act, state])
    states = [state] + [flip(state, "owner", mask) for mask in range(1, n_own)]
    parts = add_rows(keep, near, keep.shape[1] // 2)
    parts = [lax.ppermute(array, "owner", [*enumerate(held)]) for array in parts]
    to_pair = [((a, o), (a ^ 2, o)) for a in range(n_dp) for o in owners if (a ^ held[o]) & 2]
    crosses = [hop(array, to_pair) for array in parts]
    near_act = flip(send_act, "dp", 1)

    crosses[0] = after(crosses[0], *states)
    nears = [add(pair) for pair in zip(parts, crosses, strict=True)]
    aside = ((dp ^ (-own % n_own)) // 2).astype(jnp.int32)[None]
    square_grad = squares_of(aside, nears)
    square_far = flip(square_grad, "dp", 2)
    fars = [hop(array, [((held[o] ^ 1, o), (held[o], o)) for o in owners]) for array in nears]
    full = by_layer(nears, fars)
    chip = [hop(array, [((held[o], o), (held[o], o ^ 2)) for o in owners]) for array in full]

    part_act = add((keep_act, near_act))
    cross_act = flip(part_act, "dp", 2)

    done = step([part_act, cross_act, square_grad, square_far, *full, *chip])
    (part_act, cross_act, square_grad, square_far), full, chip = done[:4], done[4:][:layers], done[4 + layers :]
    full_act = add((part_act, cross_act))
    half = halves_of(full_act, square_grad, square_far)
    packet = total_of(half, flip(half, "dp", 1))
    back_act = flip(after(full_act, packet), "dp", 1)
    packets = [packet] + [flip(packet, "owner", mask) for mask in range(1, n_own)]
    source = -dp % n_own
    home = jnp.where(own == source, 0, jnp.where(own == source ^ 2, 1, 2)).astype(jnp.int32)[None]
    full = pick(after(home, *packets), [*zip(full, chip, strict=True)])
    to_core = [((held[o], o ^ b), (held[o], o ^ b ^ 1)) for o in owners for b in (0, 2)]
    core = [hop(array, to_core) for array in full]
    factors, new_act, new_grad = eigenvalues(scalars, states, packets, n_dp)
    grads = pick(home // 2, [*zip(full, core, strict=True)])
    grams = gram_of(grads, full_act)

    grams, factors, back_act, *grads = step([grams, factors, back_act, *grads])
    return finish(grads, back_act, grams, factors), new_act, new_grad


def solution(mesh):
    placed = (
        P("groups", "dp", None),
        P("groups", "dp", None),
        P("groups", "dp", "owner"),
        P("groups", "dp", "owner"),
        P(),
        P("groups"),
        P("owner", "groups"),
        P("owner", "groups"),
    )
    square = mesh.shape["dp"] == 4 and mesh.shape["owner"] == 4
    return jax.shard_map(
        line_plan if square else gather_plan,
        mesh=mesh,
        in_specs=placed,
        out_specs=(P("groups", "dp", "owner"), P("owner", "groups"), P("owner", "groups")),
        check_vma=False,
    )
```

```python
import jax
import jax.numpy as jnp
from jax import lax
from jax.experimental import pallas as pl
from jax.experimental.pallas import tpu as pltpu
from jax.sharding import PartitionSpec as P

decay_rate = 0.25
damping_rate = 0.1
vmem_spec = pl.BlockSpec(memory_space=pltpu.VMEM)
scalar_spec = pl.BlockSpec(memory_space=pltpu.SMEM)
light = pl.CostEstimate(flops=0, bytes_accessed=0, transcendentals=0)


def spread(array, axis, root):
    mine = lax.axis_index(axis) == root
    return lax.psum(jnp.where(mine, array, jnp.zeros_like(array)), axis)


def gather_plan(activations, out_grads, basis_act, basis_grad, owner_of, counts, state_act, state_grad):
    layers = activations.shape[0]
    tok_rows = activations.shape[1]
    tile_rows = basis_act.shape[1]
    tile_cols = basis_act.shape[2]
    slot_count = state_act.shape[0]
    dp_index = lax.axis_index("dp")
    own_index = lax.axis_index("owner")
    valid_rows = (jnp.arange(tok_rows) < counts[dp_index]).astype(jnp.float32)[:, None]
    valid_total = jnp.sum(counts).astype(jnp.float32)
    square_acts = []
    square_grads = []
    gram_tiles = []
    for layer_index in range(layers):
        panel_act = jnp.dot(
            activations[layer_index],
            lax.all_gather(basis_act[layer_index], "dp", axis=0, tiled=True),
            preferred_element_type=jnp.float32,
        )
        panel_grad = jnp.dot(
            out_grads[layer_index],
            lax.all_gather(basis_grad[layer_index], "dp", axis=0, tiled=True),
            preferred_element_type=jnp.float32,
        )
        panel_act = (panel_act * valid_rows).astype(jnp.bfloat16)
        panel_grad = (panel_grad * valid_rows).astype(jnp.bfloat16)
        full_act = lax.all_gather(panel_act, "owner", axis=1, tiled=True)
        full_grad = lax.all_gather(panel_grad, "owner", axis=1, tiled=True)
        square_act = jnp.sum(jnp.square(full_act.astype(jnp.float32)), axis=0)
        square_grad = jnp.sum(jnp.square(full_grad.astype(jnp.float32)), axis=0)
        gram_term = lax.dot_general(
            full_grad, panel_act, (((0,), (0,)), ((), ())), preferred_element_type=jnp.float32
        )
        gram_tiles.append(
            lax.psum_scatter(
                gram_term.astype(jnp.bfloat16), "dp", scatter_dimension=0, tiled=True
            ).astype(jnp.float32)
            / valid_total
        )
        square_act, square_grad = lax.psum((square_act, square_grad), "dp")
        square_acts.append(square_act)
        square_grads.append(square_grad)
    new_act = state_act
    new_grad = state_grad
    results = []
    for layer_index in range(layers):
        owner_now = owner_of[layer_index]
        slot_rank = jnp.sum((owner_of[:layer_index] == owner_now).astype(jnp.int32))
        selector = (jnp.arange(slot_count) == slot_rank).astype(jnp.float32)[:, None]
        local_act = decay_rate * jnp.sum(state_act * selector, axis=0) + (
            1.0 - decay_rate
        ) * (square_acts[layer_index] / valid_total)
        local_grad = decay_rate * jnp.sum(state_grad * selector, axis=0) + (
            1.0 - decay_rate
        ) * (square_grads[layer_index] / valid_total)
        eigen_act = spread(local_act, "owner", owner_now)
        eigen_grad = spread(local_grad, "owner", owner_now)
        replace_rows = ((jnp.arange(slot_count) == slot_rank) & (own_index == owner_now))[:, None]
        new_act = jnp.where(replace_rows, eigen_act[None, :], new_act)
        new_grad = jnp.where(replace_rows, eigen_grad[None, :], new_grad)
        damping = damping_rate * jnp.mean(eigen_grad) * jnp.mean(eigen_act)
        grad_eigen = lax.dynamic_slice_in_dim(eigen_grad, dp_index * tile_rows, tile_rows)
        act_eigen = lax.dynamic_slice_in_dim(eigen_act, own_index * tile_cols, tile_cols)
        scaled = gram_tiles[layer_index] / (grad_eigen[:, None] * act_eigen[None, :] + damping)
        results.append(scaled.astype(jnp.bfloat16))
    return (jnp.stack(results), new_act, new_grad)


def flip(array, axis, mask):
    return lax.ppermute(array, axis, [(i, i ^ mask) for i in range(lax.axis_size(axis))])


def hop(array, pairs):
    owners = lax.axis_size("owner")
    flat = [(a * owners + b, c * owners + e) for (a, b), (c, e) in pairs]
    return lax.ppermute(array, ("dp", "owner"), flat)


def load(arrays, cut, *gates):
    tile = arrays[-1].shape[1]
    shapes = [(*array.shape[:2], tile) if number < cut else array.shape for number, array in enumerate(arrays)]

    def kernel(*refs):
        in_refs, out_refs, sems = refs[: len(arrays)], refs[len(arrays) + len(gates) : -1], refs[-1]
        cols = pl.ds(pl.multiple_of(lax.axis_index("dp") * tile, tile), tile)
        copies = []
        for number, (in_ref, out_ref) in enumerate(zip(in_refs, out_refs, strict=True)):
            source = in_ref.at[:, :, cols] if number < cut else in_ref
            copies.append(pltpu.make_async_copy(source, out_ref, sems.at[number]))
            copies[-1].start()
        for copy in copies:
            copy.wait()

    return pl.pallas_call(
        kernel,
        out_shape=[
            jax.ShapeDtypeStruct(shape, array.dtype) for shape, array in zip(shapes, arrays, strict=True)
        ],
        in_specs=[pl.BlockSpec(memory_space=pltpu.HBM)] * len(arrays) + [pl.BlockSpec(memory_space=pl.ANY)] * len(gates),
        out_specs=[vmem_spec] * len(arrays),
        scratch_shapes=[pltpu.SemaphoreType.DMA((len(arrays),))],
        compiler_params=pltpu.CompilerParams(vmem_limit_bytes=8 * 1024 * 1024),
        cost_estimate=light,
    )(*[pltpu.with_memory_space_constraint(array, pltpu.HBM) for array in arrays], *gates)


def project_rows(scalars, tokens, pieces, basis, n_own, n_dp):
    layers, tok_rows, tile = tokens.shape
    cols = basis.shape[2]
    part_rows = tok_rows // n_own
    packed = 3 * n_dp * tok_rows // 4
    half = packed // 2
    shapes = [(layers, half, cols)] * 2

    def kernel(scalar_ref, tokens_ref, basis_ref, *refs):
        piece_refs, out_refs = refs[: len(pieces)], refs[len(pieces) :]
        dp, own = scalar_ref[0], scalar_ref[1]
        col = lax.broadcasted_iota(jnp.int32, (1, n_dp * tok_rows), 1)
        turn = (col - tok_rows) // part_rows
        peer = turn // (n_dp - 1)
        peer = own ^ (((peer & 1) << 1) | (peer >> 1))
        mine = col < tok_rows
        mask = jnp.where(mine, 0, turn % (n_dp - 1) + 1)
        index = jnp.where(mine, col, peer * part_rows + col % part_rows)
        place = jnp.full_like(col, -1)
        for number in range(n_dp):
            shard = dp ^ number
            start = jnp.int32(0)
            for other in range(n_dp):
                start += jnp.where(other < shard, scalar_ref[2 + other], 0)
            here = (mask == number) & (index < scalar_ref[2 + shard])
            place = jnp.where(here, start + index, place)
        row = lax.broadcasted_iota(jnp.int32, (packed, n_dp * tok_rows), 0)
        row = row + jnp.where(dp % 2 == 0, 0, jnp.where(row < half, half, -half))
        select = (row == place).astype(jnp.bfloat16)
        for layer in range(layers):
            rows = jnp.concatenate([tokens_ref[layer]] + [p[layer] for p in piece_refs], axis=0)
            chosen = jnp.dot(select, rows, preferred_element_type=jnp.float32).astype(jnp.bfloat16)
            result = jnp.dot(chosen, basis_ref[layer], preferred_element_type=jnp.float32).astype(
                jnp.bfloat16
            )
            out_refs[0][layer] = result[:half]
            out_refs[1][layer] = result[half:]

    return pl.pallas_call(
        kernel,
        out_shape=[jax.ShapeDtypeStruct(shape, jnp.bfloat16) for shape in shapes],
        in_specs=[scalar_spec] + [vmem_spec] * (2 + len(pieces)),
        out_specs=[vmem_spec] * len(shapes),
        compiler_params=pltpu.CompilerParams(vmem_limit_bytes=16 * 1024 * 1024),
        cost_estimate=light,
    )(scalars, tokens, basis, *pieces)


def add(*pairs):
    layers = pairs[0][0].shape[0]

    def kernel(*refs):
        for number in range(len(pairs)):
            total = refs[2 * number][...].astype(jnp.float32) + refs[2 * number + 1][...].astype(jnp.float32)
            refs[-1][number * layers : (number + 1) * layers] = total.astype(refs[-1].dtype)

    first = pairs[0][0]
    return pl.pallas_call(
        kernel,
        out_shape=jax.ShapeDtypeStruct((layers * len(pairs), *first.shape[1:]), first.dtype),
        in_specs=[vmem_spec] * (2 * len(pairs)),
        out_specs=vmem_spec,
        compiler_params=pltpu.CompilerParams(vmem_limit_bytes=8 * 1024 * 1024),
        cost_estimate=light,
    )(*[array for pair in pairs for array in pair])


def add_rows(near, far, cut):
    layers, height, cols = near.shape
    spans = [(0, cut), (cut, height)]

    def kernel(near_ref, far_ref, *out_refs):
        for out_ref, (start, stop) in zip(out_refs, spans, strict=True):
            total = near_ref[:, start:stop].astype(jnp.float32) + far_ref[:, start:stop].astype(jnp.float32)
            out_ref[...] = total.astype(out_ref.dtype)

    return pl.pallas_call(
        kernel,
        out_shape=[jax.ShapeDtypeStruct((layers, stop - start, cols), near.dtype) for start, stop in spans],
        in_specs=[vmem_spec] * 2,
        out_specs=[vmem_spec] * len(spans),
        compiler_params=pltpu.CompilerParams(vmem_limit_bytes=8 * 1024 * 1024),
        cost_estimate=light,
    )(near, far)


def by_layer(nears, fars):
    layers, _, cols = nears[0].shape
    count = len(nears)
    height = sum(array.shape[1] for array in nears)

    def kernel(*refs):
        for side in range(2):
            start = 0
            for ref in refs[side * count : (side + 1) * count]:
                for layer, out_ref in enumerate(refs[2 * count :]):
                    out_ref[side, start : start + ref.shape[1]] = ref[layer]
                start += ref.shape[1]

    return pl.pallas_call(
        kernel,
        out_shape=[jax.ShapeDtypeStruct((2, height, cols), nears[0].dtype)] * layers,
        in_specs=[vmem_spec] * (2 * count),
        out_specs=[vmem_spec] * layers,
        compiler_params=pltpu.CompilerParams(vmem_limit_bytes=8 * 1024 * 1024),
        cost_estimate=light,
    )(*nears, *fars)


def join(arrays):
    layers, rows, cols = arrays[0].shape

    def kernel(*refs):
        for number, ref in enumerate(refs[:-1]):
            refs[-1][:, number * rows : (number + 1) * rows] = ref[...]

    return pl.pallas_call(
        kernel,
        out_shape=jax.ShapeDtypeStruct((layers, len(arrays) * rows, cols), arrays[0].dtype),
        in_specs=[vmem_spec] * len(arrays),
        out_specs=vmem_spec,
        compiler_params=pltpu.CompilerParams(vmem_limit_bytes=8 * 1024 * 1024),
        cost_estimate=light,
    )(*arrays)


def cut_rows(arrays, tile, n_own, n_dp):
    layers, tok_rows, _ = arrays[0].shape
    part_rows = tok_rows // n_own
    peers = n_dp - 1

    def kernel(*refs):
        in_refs, out_refs, sems = refs[: len(arrays)], refs[len(arrays) : -1], refs[-1]
        dp, own = lax.axis_index("dp"), lax.axis_index("owner")
        rows = pl.ds(pl.multiple_of(own * part_rows, part_rows), part_rows)
        copies = []
        for number, out_ref in enumerate(out_refs):
            block = dp ^ (number % peers + 1)
            cols = pl.ds(pl.multiple_of(block * tile, tile), tile)
            copies.append(
                pltpu.make_async_copy(in_refs[number // peers].at[:, rows, cols], out_ref, sems.at[number])
            )
            copies[-1].start()
        for copy in copies:
            copy.wait()

    count = len(arrays) * peers
    return pl.pallas_call(
        kernel,
        out_shape=[jax.ShapeDtypeStruct((layers, part_rows, tile), arrays[0].dtype)] * count,
        in_specs=[pl.BlockSpec(memory_space=pltpu.HBM)] * len(arrays),
        out_specs=[vmem_spec] * count,
        scratch_shapes=[pltpu.SemaphoreType.DMA((count,))],
        compiler_params=pltpu.CompilerParams(vmem_limit_bytes=8 * 1024 * 1024),
        cost_estimate=light,
    )(*[pltpu.with_memory_space_constraint(array, pltpu.HBM) for array in arrays])


def pick(home, choices):
    flat = [array for arrays in choices for array in arrays]
    count = len(choices[0])

    def kernel(home_ref, *refs):
        for index in range(count):

            @pl.when(home_ref[0] == index)
            def _(index=index):
                for number, out_ref in enumerate(refs[len(flat) :]):
                    out_ref[...] = refs[number * count + index][...]

    return pl.pallas_call(
        kernel,
        out_shape=[jax.ShapeDtypeStruct(arrays[0].shape, arrays[0].dtype) for arrays in choices],
        in_specs=[scalar_spec] + [vmem_spec] * len(flat),
        out_specs=[vmem_spec] * len(choices),
        compiler_params=pltpu.CompilerParams(vmem_limit_bytes=12 * 1024 * 1024),
        cost_estimate=light,
    )(home, *flat)


def squares_of(aside, panels):
    layers, _, cols = panels[0].shape

    def kernel(aside_ref, *refs):
        for layer in range(layers):
            total = jnp.zeros((1, cols), jnp.float32)
            for ref in refs[:-1]:
                wide = ref[layer].astype(jnp.float32)
                total += jnp.sum(wide * wide, axis=0, keepdims=True)
            refs[-1][layer : layer + 1] = jnp.where(aside_ref[0] == 0, total, 0.0)

    return pl.pallas_call(
        kernel,
        out_shape=jax.ShapeDtypeStruct((layers, cols), jnp.float32),
        in_specs=[scalar_spec] + [vmem_spec] * len(panels),
        out_specs=vmem_spec,
        compiler_params=pltpu.CompilerParams(vmem_limit_bytes=8 * 1024 * 1024),
        cost_estimate=light,
    )(aside, *panels)


def settle(part, cross, near, far):
    layers, _, cols = part.shape

    def kernel(part_ref, cross_ref, near_ref, far_ref, act_ref, out_ref):
        for layer in range(layers):
            total = part_ref[layer].astype(jnp.float32) + cross_ref[layer].astype(jnp.float32)
            total = total.astype(act_ref.dtype)
            act_ref[layer] = total
            wide = total.astype(jnp.float32)
            out_ref[layer : layer + 1] = jnp.sum(wide * wide, axis=0, keepdims=True)
        out_ref[layers:] = near_ref[...] + far_ref[...]

    return pl.pallas_call(
        kernel,
        out_shape=[
            jax.ShapeDtypeStruct(part.shape, part.dtype),
            jax.ShapeDtypeStruct((2 * layers, cols), jnp.float32),
        ],
        in_specs=[vmem_spec] * 4,
        out_specs=[vmem_spec] * 2,
        compiler_params=pltpu.CompilerParams(vmem_limit_bytes=8 * 1024 * 1024),
        cost_estimate=light,
    )(part, cross, near, far)


def total_of(near, far):
    def kernel(near_ref, far_ref, out_ref):
        out_ref[...] = near_ref[...] + far_ref[...]

    return pl.pallas_call(
        kernel,
        out_shape=jax.ShapeDtypeStruct(near.shape, near.dtype),
        in_specs=[vmem_spec] * 2,
        out_specs=vmem_spec,
        compiler_params=pltpu.CompilerParams(vmem_limit_bytes=4 * 1024 * 1024),
        cost_estimate=light,
    )(near, far)


def gram_of(grads, act):
    layers, _, cols = act.shape

    def kernel(*refs):
        for layer in range(layers):
            refs[-1][layer] = product_of(refs[layer][0], refs[-2][layer])

    return pl.pallas_call(
        kernel,
        out_shape=jax.ShapeDtypeStruct((layers, grads[0].shape[2], cols), jnp.float32),
        in_specs=[vmem_spec] * (layers + 1),
        out_specs=vmem_spec,
        compiler_params=pltpu.CompilerParams(vmem_limit_bytes=16 * 1024 * 1024),
        cost_estimate=light,
    )(*grads, act)


def product_of(grad, act):
    return lax.dot_general(grad, act, (((0,), (0,)), ((), ())), preferred_element_type=jnp.float32)


def finish(grads, act, grams, factors):
    layers, tile, cols = grams.shape

    def kernel(*refs):
        grad_refs, (act_ref, gram_ref, factor_ref, out_ref) = refs[:layers], refs[layers:]
        for layer in range(layers):
            gram = gram_ref[layer] + product_of(grad_refs[layer][1], act_ref[layer])
            out_ref[layer] = (gram * factor_ref[layer]).astype(jnp.bfloat16)

    return pl.pallas_call(
        kernel,
        out_shape=jax.ShapeDtypeStruct((layers, tile, cols), jnp.bfloat16),
        in_specs=[vmem_spec] * (layers + 3),
        out_specs=vmem_spec,
        compiler_params=pltpu.CompilerParams(vmem_limit_bytes=24 * 1024 * 1024),
        cost_estimate=light,
    )(*grads, act, grams, factors)


def eigenvalues(scalars, states, packets, n_dp):
    n_own = len(packets)
    layers, tile = packets[0].shape[0] // 2, packets[0].shape[1]
    slot_count, width = states[0].shape[0] // 2, states[0].shape[1]

    def kernel(scalar_ref, *refs):
        state_refs, packet_refs, refs = refs[:n_own], refs[n_own : 2 * n_own], refs[2 * n_own :]
        out_ref, new_act_ref, new_grad_ref, act_full, grad_full = refs
        dp, own = scalar_ref[0], scalar_ref[1]
        total = scalar_ref[2]
        for index in range(1, n_dp):
            total += scalar_ref[2 + index]
        total = total.astype(jnp.float32)
        owners = [scalar_ref[2 + n_dp + layer] for layer in range(layers)]
        for mask in range(n_own):
            at = pl.ds(pl.multiple_of((own ^ mask) * tile, tile), tile)
            act_full[:, at] = packet_refs[mask][:layers] / total
            at = pl.ds(pl.multiple_of((n_own - (own ^ mask)) % n_own * tile, tile), tile)
            grad_full[:, at] = packet_refs[mask][layers:] / total
        new_act_ref[...] = state_refs[0][:slot_count]
        new_grad_ref[...] = state_refs[0][slot_count:]
        for layer in range(layers):
            owner_now = owners[layer]
            rank = jnp.int32(0)
            for earlier in range(layer):
                rank += jnp.where(owners[earlier] == owner_now, 1, 0)
            old_act = jnp.zeros((1, width), jnp.float32)
            old_grad = jnp.zeros((1, width), jnp.float32)
            for mask in range(n_own):
                for slot in range(slot_count):
                    here = (owner_now == own ^ mask) & (rank == slot)
                    down = slot_count + slot
                    old_act = jnp.where(here, state_refs[mask][slot : slot + 1], old_act)
                    old_grad = jnp.where(here, state_refs[mask][down : down + 1], old_grad)
            eigen_act = decay_rate * old_act + (1.0 - decay_rate) * act_full[layer : layer + 1]
            eigen_grad = decay_rate * old_grad + (1.0 - decay_rate) * grad_full[layer : layer + 1]
            act_full[layer : layer + 1] = eigen_act
            grad_full[layer : layer + 1] = eigen_grad
            for slot in range(slot_count):

                @pl.when((owner_now == own) & (rank == slot))
                def _(slot=slot, eigen_act=eigen_act, eigen_grad=eigen_grad):
                    new_act_ref[slot : slot + 1] = eigen_act
                    new_grad_ref[slot : slot + 1] = eigen_grad

            damping = damping_rate * (jnp.sum(eigen_grad) / width) * (jnp.sum(eigen_act) / width)
            rows = grad_full[layer : layer + 1, pl.ds(pl.multiple_of(dp * tile, tile), tile)]
            cols = act_full[layer : layer + 1, pl.ds(pl.multiple_of(own * tile, tile), tile)]
            rows = jnp.transpose(jnp.broadcast_to(rows, (128, tile)))
            rows = jnp.concatenate([rows] * (tile // 128), axis=1)
            out_ref[layer] = 1.0 / (total * (rows * cols + damping))

    out_shape = [
        jax.ShapeDtypeStruct((layers, tile, tile), jnp.float32),
        jax.ShapeDtypeStruct((slot_count, width), jnp.float32),
        jax.ShapeDtypeStruct((slot_count, width), jnp.float32),
    ]
    return pl.pallas_call(
        kernel,
        out_shape=out_shape,
        in_specs=[scalar_spec] + [vmem_spec] * (2 * n_own),
        out_specs=[vmem_spec] * len(out_shape),
        scratch_shapes=[pltpu.VMEM((layers, width), jnp.float32)] * 2,
        compiler_params=pltpu.CompilerParams(vmem_limit_bytes=16 * 1024 * 1024),
        cost_estimate=light,
    )(scalars, *states, *packets)


def line_plan(activations, out_grads, basis_act, basis_grad, owner_of, counts, state_act, state_grad):
    layers, tok_rows, width = activations.shape
    tile = basis_act.shape[1]
    n_dp = lax.axis_size("dp")
    n_own = lax.axis_size("owner")
    dp = lax.axis_index("dp")
    own = lax.axis_index("owner")
    scalars = jnp.concatenate([jnp.stack([dp, own]), counts, owner_of]).astype(jnp.int32)

    def after(array, *others):
        return lax.optimization_barrier((array, *others))[0]

    def step(arrays, *others):
        return lax.optimization_barrier((*arrays, *others))[: len(arrays)]

    owners = range(n_own)
    held = [-o % n_own for o in owners]
    cuts = cut_rows((out_grads, activations), tile, n_own, n_dp)
    cuts = [flip(cut, "dp", number % (n_dp - 1) + 1) for number, cut in enumerate(cuts)]
    got_grad, got_act = cuts[: n_dp - 1], cuts[n_dp - 1 :]
    own_grad, stay_grad = load((out_grads, basis_grad), 1)
    pieces = got_grad[:-1] + [after(got_grad[-1], got_act[0], own_grad)]
    pieces += [flip(piece, "owner", 2) for piece in pieces]
    pieces += [flip(piece, "owner", 1) for piece in pieces]
    keep, send = project_rows(scalars, own_grad, pieces, stay_grad, n_own, n_dp)

    near = flip(after(send, *got_act), "dp", 1)
    pieces = [join(got_act[:-1]), got_act[-1]]
    pieces += [flip(after(piece, keep), "owner", 2) for piece in pieces]
    own_act, stay_act = load((activations, basis_act), 1, keep)
    pieces += [flip(after(piece, own_act), "owner", 1) for piece in pieces]
    keep_act, send_act = project_rows(scalars, own_act, pieces, stay_act, n_own, n_dp)

    state = jnp.concatenate([state_act, state_grad], axis=0)
    keep, near, keep_act, send_act, state = step([keep, near, keep_act, send_act, state])
    states = [state] + [flip(state, "owner", mask) for mask in range(1, n_own)]
    parts = add_rows(keep, near, keep.shape[1] // 2)
    parts = [lax.ppermute(array, "owner", [*enumerate(held)]) for array in parts]
    to_pair = [((a, o), (a ^ 2, o)) for a in range(n_dp) for o in owners if (a ^ held[o]) & 2]
    crosses = [hop(array, to_pair) for array in parts]
    near_act = flip(send_act, "dp", 1)

    crosses[0] = after(crosses[0], *states)
    nears = [add(pair) for pair in zip(parts, crosses, strict=True)]
    aside = ((dp ^ (-own % n_own)) // 2).astype(jnp.int32)[None]
    square_grad = squares_of(aside, nears)
    square_far = flip(square_grad, "dp", 2)
    fars = [hop(array, [((held[o] ^ 1, o), (held[o], o)) for o in owners]) for array in nears]
    full = by_layer(nears, fars)
    chip = [hop(array, [((held[o], o), (held[o], o ^ 2)) for o in owners]) for array in full]

    part_act = add((keep_act, near_act))
    cross_act = flip(part_act, "dp", 2)

    done = step([part_act, cross_act, square_grad, square_far, *full, *chip])
    (part_act, cross_act, square_grad, square_far), full, chip = done[:4], done[4:][:layers], done[4 + layers :]
    full_act, half = settle(part_act, cross_act, square_grad, square_far)
    other = flip(half, "dp", 1)
    source = -dp % n_own
    home = jnp.where(own == source, 0, jnp.where(own == source ^ 2, 1, 2)).astype(jnp.int32)[None]
    full = pick(after(home, half), [*zip(full, chip, strict=True)])
    back_act = flip(after(full_act, other, *full), "dp", 1)
    packet = total_of(half, other)
    packets = [packet] + [flip(packet, "owner", mask) for mask in range(1, n_own)]
    to_core = [((held[o], o ^ b), (held[o], o ^ b ^ 1)) for o in owners for b in (0, 2)]
    core = [hop(after(array, *packets), to_core) for array in full]
    factors, new_act, new_grad = eigenvalues(scalars, states, packets, n_dp)
    grads = pick(home // 2, [*zip(full, core, strict=True)])
    grams = gram_of(grads, full_act)

    grams, factors, back_act, *grads = step([grams, factors, back_act, *grads])
    return finish(grads, back_act, grams, factors), new_act, new_grad


def solution(mesh):
    placed = (
        P("groups", "dp", None),
        P("groups", "dp", None),
        P("groups", "dp", "owner"),
        P("groups", "dp", "owner"),
        P(),
        P("groups"),
        P("owner", "groups"),
        P("owner", "groups"),
    )
    square = mesh.shape["dp"] == 4 and mesh.shape["owner"] == 4
    return jax.shard_map(
        line_plan if square else gather_plan,
        mesh=mesh,
        in_specs=placed,
        out_specs=(P("groups", "dp", "owner"), P("owner", "groups"), P("owner", "groups")),
        check_vma=False,
    )
```

```python
import jax
import jax.numpy as jnp
from jax import lax
from jax.experimental import pallas as pl
from jax.experimental.pallas import tpu as pltpu
from jax.sharding import PartitionSpec as P

decay_rate = 0.25
damping_rate = 0.1
vmem_spec = pl.BlockSpec(memory_space=pltpu.VMEM)
scalar_spec = pl.BlockSpec(memory_space=pltpu.SMEM)
light = pl.CostEstimate(flops=0, bytes_accessed=0, transcendentals=0)


def spread(array, axis, root):
    mine = lax.axis_index(axis) == root
    return lax.psum(jnp.where(mine, array, jnp.zeros_like(array)), axis)


def gather_plan(activations, out_grads, basis_act, basis_grad, owner_of, counts, state_act, state_grad):
    layers = activations.shape[0]
    tok_rows = activations.shape[1]
    tile_rows = basis_act.shape[1]
    tile_cols = basis_act.shape[2]
    slot_count = state_act.shape[0]
    dp_index = lax.axis_index("dp")
    own_index = lax.axis_index("owner")
    valid_rows = (jnp.arange(tok_rows) < counts[dp_index]).astype(jnp.float32)[:, None]
    valid_total = jnp.sum(counts).astype(jnp.float32)
    square_acts = []
    square_grads = []
    gram_tiles = []
    for layer_index in range(layers):
        panel_act = jnp.dot(
            activations[layer_index],
            lax.all_gather(basis_act[layer_index], "dp", axis=0, tiled=True),
            preferred_element_type=jnp.float32,
        )
        panel_grad = jnp.dot(
            out_grads[layer_index],
            lax.all_gather(basis_grad[layer_index], "dp", axis=0, tiled=True),
            preferred_element_type=jnp.float32,
        )
        panel_act = (panel_act * valid_rows).astype(jnp.bfloat16)
        panel_grad = (panel_grad * valid_rows).astype(jnp.bfloat16)
        full_act = lax.all_gather(panel_act, "owner", axis=1, tiled=True)
        full_grad = lax.all_gather(panel_grad, "owner", axis=1, tiled=True)
        square_act = jnp.sum(jnp.square(full_act.astype(jnp.float32)), axis=0)
        square_grad = jnp.sum(jnp.square(full_grad.astype(jnp.float32)), axis=0)
        gram_term = lax.dot_general(
            full_grad, panel_act, (((0,), (0,)), ((), ())), preferred_element_type=jnp.float32
        )
        gram_tiles.append(
            lax.psum_scatter(
                gram_term.astype(jnp.bfloat16), "dp", scatter_dimension=0, tiled=True
            ).astype(jnp.float32)
            / valid_total
        )
        square_act, square_grad = lax.psum((square_act, square_grad), "dp")
        square_acts.append(square_act)
        square_grads.append(square_grad)
    new_act = state_act
    new_grad = state_grad
    results = []
    for layer_index in range(layers):
        owner_now = owner_of[layer_index]
        slot_rank = jnp.sum((owner_of[:layer_index] == owner_now).astype(jnp.int32))
        selector = (jnp.arange(slot_count) == slot_rank).astype(jnp.float32)[:, None]
        local_act = decay_rate * jnp.sum(state_act * selector, axis=0) + (
            1.0 - decay_rate
        ) * (square_acts[layer_index] / valid_total)
        local_grad = decay_rate * jnp.sum(state_grad * selector, axis=0) + (
            1.0 - decay_rate
        ) * (square_grads[layer_index] / valid_total)
        eigen_act = spread(local_act, "owner", owner_now)
        eigen_grad = spread(local_grad, "owner", owner_now)
        replace_rows = ((jnp.arange(slot_count) == slot_rank) & (own_index == owner_now))[:, None]
        new_act = jnp.where(replace_rows, eigen_act[None, :], new_act)
        new_grad = jnp.where(replace_rows, eigen_grad[None, :], new_grad)
        damping = damping_rate * jnp.mean(eigen_grad) * jnp.mean(eigen_act)
        grad_eigen = lax.dynamic_slice_in_dim(eigen_grad, dp_index * tile_rows, tile_rows)
        act_eigen = lax.dynamic_slice_in_dim(eigen_act, own_index * tile_cols, tile_cols)
        scaled = gram_tiles[layer_index] / (grad_eigen[:, None] * act_eigen[None, :] + damping)
        results.append(scaled.astype(jnp.bfloat16))
    return (jnp.stack(results), new_act, new_grad)


def flip(array, axis, mask):
    return lax.ppermute(array, axis, [(i, i ^ mask) for i in range(lax.axis_size(axis))])


def hop(array, pairs):
    owners = lax.axis_size("owner")
    flat = [(a * owners + b, c * owners + e) for (a, b), (c, e) in pairs]
    return lax.ppermute(array, ("dp", "owner"), flat)


def load(arrays, cut, *gates):
    tile = arrays[-1].shape[1]
    shapes = [(*array.shape[:2], tile) if number < cut else array.shape for number, array in enumerate(arrays)]

    def kernel(*refs):
        in_refs, out_refs, sems = refs[: len(arrays)], refs[len(arrays) + len(gates) : -1], refs[-1]
        cols = pl.ds(pl.multiple_of(lax.axis_index("dp") * tile, tile), tile)
        copies = []
        for number, (in_ref, out_ref) in enumerate(zip(in_refs, out_refs, strict=True)):
            source = in_ref.at[:, :, cols] if number < cut else in_ref
            copies.append(pltpu.make_async_copy(source, out_ref, sems.at[number]))
            copies[-1].start()
        for copy in copies:
            copy.wait()

    return pl.pallas_call(
        kernel,
        out_shape=[
            jax.ShapeDtypeStruct(shape, array.dtype) for shape, array in zip(shapes, arrays, strict=True)
        ],
        in_specs=[pl.BlockSpec(memory_space=pltpu.HBM)] * len(arrays) + [pl.BlockSpec(memory_space=pl.ANY)] * len(gates),
        out_specs=[vmem_spec] * len(arrays),
        scratch_shapes=[pltpu.SemaphoreType.DMA((len(arrays),))],
        compiler_params=pltpu.CompilerParams(vmem_limit_bytes=8 * 1024 * 1024),
        cost_estimate=light,
    )(*[pltpu.with_memory_space_constraint(array, pltpu.HBM) for array in arrays], *gates)


def project_rows(scalars, tokens, pieces, basis, n_own, n_dp):
    layers, tok_rows, tile = tokens.shape
    cols = basis.shape[2]
    part_rows = tok_rows // n_own
    packed = 3 * n_dp * tok_rows // 4
    half = packed // 2
    shapes = [(layers, half, cols)] * 2

    def kernel(scalar_ref, tokens_ref, basis_ref, *refs):
        piece_refs, out_refs = refs[: len(pieces)], refs[len(pieces) :]
        dp, own = scalar_ref[0], scalar_ref[1]
        col = lax.broadcasted_iota(jnp.int32, (1, n_dp * tok_rows), 1)
        turn = (col - tok_rows) // part_rows
        peer = turn // (n_dp - 1)
        peer = own ^ (((peer & 1) << 1) | (peer >> 1))
        mine = col < tok_rows
        mask = jnp.where(mine, 0, turn % (n_dp - 1) + 1)
        index = jnp.where(mine, col, peer * part_rows + col % part_rows)
        place = jnp.full_like(col, -1)
        for number in range(n_dp):
            shard = dp ^ number
            start = jnp.int32(0)
            for other in range(n_dp):
                start += jnp.where(other < shard, scalar_ref[2 + other], 0)
            here = (mask == number) & (index < scalar_ref[2 + shard])
            place = jnp.where(here, start + index, place)
        row = lax.broadcasted_iota(jnp.int32, (packed, n_dp * tok_rows), 0)
        row = row + jnp.where(dp % 2 == 0, 0, jnp.where(row < half, half, -half))
        select = (row == place).astype(jnp.bfloat16)
        for layer in range(layers):
            rows = jnp.concatenate([tokens_ref[layer]] + [p[layer] for p in piece_refs], axis=0)
            chosen = jnp.dot(select, rows, preferred_element_type=jnp.float32).astype(jnp.bfloat16)
            result = jnp.dot(chosen, basis_ref[layer], preferred_element_type=jnp.float32).astype(
                jnp.bfloat16
            )
            out_refs[0][layer] = result[:half]
            out_refs[1][layer] = result[half:]

    return pl.pallas_call(
        kernel,
        out_shape=[jax.ShapeDtypeStruct(shape, jnp.bfloat16) for shape in shapes],
        in_specs=[scalar_spec] + [vmem_spec] * (2 + len(pieces)),
        out_specs=[vmem_spec] * len(shapes),
        compiler_params=pltpu.CompilerParams(vmem_limit_bytes=16 * 1024 * 1024),
        cost_estimate=light,
    )(scalars, tokens, basis, *pieces)


def add(*pairs):
    layers = pairs[0][0].shape[0]

    def kernel(*refs):
        for number in range(len(pairs)):
            total = refs[2 * number][...].astype(jnp.float32) + refs[2 * number + 1][...].astype(jnp.float32)
            refs[-1][number * layers : (number + 1) * layers] = total.astype(refs[-1].dtype)

    first = pairs[0][0]
    return pl.pallas_call(
        kernel,
        out_shape=jax.ShapeDtypeStruct((layers * len(pairs), *first.shape[1:]), first.dtype),
        in_specs=[vmem_spec] * (2 * len(pairs)),
        out_specs=vmem_spec,
        compiler_params=pltpu.CompilerParams(vmem_limit_bytes=8 * 1024 * 1024),
        cost_estimate=light,
    )(*[array for pair in pairs for array in pair])


def add_rows(near, far, cut):
    layers, height, cols = near.shape
    spans = [(0, cut), (cut, height)]

    def kernel(near_ref, far_ref, *out_refs):
        for out_ref, (start, stop) in zip(out_refs, spans, strict=True):
            total = near_ref[:, start:stop].astype(jnp.float32) + far_ref[:, start:stop].astype(jnp.float32)
            out_ref[...] = total.astype(out_ref.dtype)

    return pl.pallas_call(
        kernel,
        out_shape=[jax.ShapeDtypeStruct((layers, stop - start, cols), near.dtype) for start, stop in spans],
        in_specs=[vmem_spec] * 2,
        out_specs=[vmem_spec] * len(spans),
        compiler_params=pltpu.CompilerParams(vmem_limit_bytes=8 * 1024 * 1024),
        cost_estimate=light,
    )(near, far)


def by_layer(nears, fars):
    layers, _, cols = nears[0].shape
    count = len(nears)
    height = sum(array.shape[1] for array in nears)

    def kernel(*refs):
        for side in range(2):
            start = 0
            for ref in refs[side * count : (side + 1) * count]:
                for layer, out_ref in enumerate(refs[2 * count :]):
                    out_ref[side, start : start + ref.shape[1]] = ref[layer]
                start += ref.shape[1]

    return pl.pallas_call(
        kernel,
        out_shape=[jax.ShapeDtypeStruct((2, height, cols), nears[0].dtype)] * layers,
        in_specs=[vmem_spec] * (2 * count),
        out_specs=[vmem_spec] * layers,
        compiler_params=pltpu.CompilerParams(vmem_limit_bytes=8 * 1024 * 1024),
        cost_estimate=light,
    )(*nears, *fars)


def join(arrays):
    layers, rows, cols = arrays[0].shape

    def kernel(*refs):
        for number, ref in enumerate(refs[:-1]):
            refs[-1][:, number * rows : (number + 1) * rows] = ref[...]

    return pl.pallas_call(
        kernel,
        out_shape=jax.ShapeDtypeStruct((layers, len(arrays) * rows, cols), arrays[0].dtype),
        in_specs=[vmem_spec] * len(arrays),
        out_specs=vmem_spec,
        compiler_params=pltpu.CompilerParams(vmem_limit_bytes=8 * 1024 * 1024),
        cost_estimate=light,
    )(*arrays)


def cut_rows(arrays, tile, n_own, n_dp):
    layers, tok_rows, _ = arrays[0].shape
    part_rows = tok_rows // n_own
    peers = n_dp - 1

    def kernel(*refs):
        in_refs, out_refs, sems = refs[: len(arrays)], refs[len(arrays) : -1], refs[-1]
        dp, own = lax.axis_index("dp"), lax.axis_index("owner")
        rows = pl.ds(pl.multiple_of(own * part_rows, part_rows), part_rows)
        copies = []
        for number, out_ref in enumerate(out_refs):
            block = dp ^ (number % peers + 1)
            cols = pl.ds(pl.multiple_of(block * tile, tile), tile)
            copies.append(
                pltpu.make_async_copy(in_refs[number // peers].at[:, rows, cols], out_ref, sems.at[number])
            )
            copies[-1].start()
        for copy in copies:
            copy.wait()

    count = len(arrays) * peers
    return pl.pallas_call(
        kernel,
        out_shape=[jax.ShapeDtypeStruct((layers, part_rows, tile), arrays[0].dtype)] * count,
        in_specs=[pl.BlockSpec(memory_space=pltpu.HBM)] * len(arrays),
        out_specs=[vmem_spec] * count,
        scratch_shapes=[pltpu.SemaphoreType.DMA((count,))],
        compiler_params=pltpu.CompilerParams(vmem_limit_bytes=8 * 1024 * 1024),
        cost_estimate=light,
    )(*[pltpu.with_memory_space_constraint(array, pltpu.HBM) for array in arrays])


def pick(home, choices):
    flat = [array for arrays in choices for array in arrays]
    count = len(choices[0])

    def kernel(home_ref, *refs):
        for index in range(count):

            @pl.when(home_ref[0] == index)
            def _(index=index):
                for number, out_ref in enumerate(refs[len(flat) :]):
                    out_ref[...] = refs[number * count + index][...]

    return pl.pallas_call(
        kernel,
        out_shape=[jax.ShapeDtypeStruct(arrays[0].shape, arrays[0].dtype) for arrays in choices],
        in_specs=[scalar_spec] + [vmem_spec] * len(flat),
        out_specs=[vmem_spec] * len(choices),
        compiler_params=pltpu.CompilerParams(vmem_limit_bytes=12 * 1024 * 1024),
        cost_estimate=light,
    )(home, *flat)


def squares_of(aside, panels):
    layers, _, cols = panels[0].shape

    def kernel(aside_ref, *refs):
        for layer in range(layers):
            total = jnp.zeros((1, cols), jnp.float32)
            for ref in refs[:-1]:
                wide = ref[layer].astype(jnp.float32)
                total += jnp.sum(wide * wide, axis=0, keepdims=True)
            refs[-1][layer : layer + 1] = jnp.where(aside_ref[0] == 0, total, 0.0)

    return pl.pallas_call(
        kernel,
        out_shape=jax.ShapeDtypeStruct((layers, cols), jnp.float32),
        in_specs=[scalar_spec] + [vmem_spec] * len(panels),
        out_specs=vmem_spec,
        compiler_params=pltpu.CompilerParams(vmem_limit_bytes=8 * 1024 * 1024),
        cost_estimate=light,
    )(aside, *panels)


def halves_of(act, near, far):
    layers, _, cols = act.shape

    def kernel(act_ref, near_ref, far_ref, out_ref):
        for layer in range(layers):
            wide = act_ref[layer].astype(jnp.float32)
            out_ref[layer : layer + 1] = jnp.sum(wide * wide, axis=0, keepdims=True)
        out_ref[layers:] = near_ref[...] + far_ref[...]

    return pl.pallas_call(
        kernel,
        out_shape=jax.ShapeDtypeStruct((2 * layers, cols), jnp.float32),
        in_specs=[vmem_spec] * 3,
        out_specs=vmem_spec,
        compiler_params=pltpu.CompilerParams(vmem_limit_bytes=8 * 1024 * 1024),
        cost_estimate=light,
    )(act, near, far)


def total_of(near, far):
    def kernel(near_ref, far_ref, out_ref):
        out_ref[...] = near_ref[...] + far_ref[...]

    return pl.pallas_call(
        kernel,
        out_shape=jax.ShapeDtypeStruct(near.shape, near.dtype),
        in_specs=[vmem_spec] * 2,
        out_specs=vmem_spec,
        compiler_params=pltpu.CompilerParams(vmem_limit_bytes=4 * 1024 * 1024),
        cost_estimate=light,
    )(near, far)


def gram_of(grads, act):
    layers, _, cols = act.shape

    def kernel(*refs):
        for layer in range(layers):
            refs[-1][layer] = product_of(refs[layer][0], refs[-2][layer])

    return pl.pallas_call(
        kernel,
        out_shape=jax.ShapeDtypeStruct((layers, grads[0].shape[2], cols), jnp.float32),
        in_specs=[vmem_spec] * (layers + 1),
        out_specs=vmem_spec,
        compiler_params=pltpu.CompilerParams(vmem_limit_bytes=16 * 1024 * 1024),
        cost_estimate=light,
    )(*grads, act)


def product_of(grad, act):
    return lax.dot_general(grad, act, (((0,), (0,)), ((), ())), preferred_element_type=jnp.float32)


def finish(grads, act, grams, factors):
    layers, tile, cols = grams.shape

    def kernel(*refs):
        grad_refs, (act_ref, gram_ref, factor_ref, out_hbm, out_ref, sems) = refs[:layers], refs[layers:]
        copies = []
        for layer in range(layers):
            gram = gram_ref[layer] + product_of(grad_refs[layer][1], act_ref[layer])
            out_ref[layer] = (gram * factor_ref[layer]).astype(jnp.bfloat16)
            copies.append(pltpu.make_async_copy(out_ref.at[layer], out_hbm.at[layer], sems.at[layer]))
            copies[-1].start()
        for copy in copies:
            copy.wait()

    return pl.pallas_call(
        kernel,
        out_shape=jax.ShapeDtypeStruct((layers, tile, cols), jnp.bfloat16),
        in_specs=[vmem_spec] * (layers + 3),
        out_specs=pl.BlockSpec(memory_space=pl.ANY),
        scratch_shapes=[pltpu.VMEM((layers, tile, cols), jnp.bfloat16), pltpu.SemaphoreType.DMA((layers,))],
        compiler_params=pltpu.CompilerParams(vmem_limit_bytes=24 * 1024 * 1024),
        cost_estimate=light,
    )(*grads, act, grams, factors)


def eigenvalues(scalars, states, packets, n_dp):
    n_own = len(packets)
    layers, tile = packets[0].shape[0] // 2, packets[0].shape[1]
    slot_count, width = states[0].shape[0] // 2, states[0].shape[1]

    def kernel(scalar_ref, *refs):
        state_refs, packet_refs, refs = refs[:n_own], refs[n_own : 2 * n_own], refs[2 * n_own :]
        out_ref, new_act_ref, new_grad_ref, act_full, grad_full = refs
        dp, own = scalar_ref[0], scalar_ref[1]
        total = scalar_ref[2]
        for index in range(1, n_dp):
            total += scalar_ref[2 + index]
        total = total.astype(jnp.float32)
        owners = [scalar_ref[2 + n_dp + layer] for layer in range(layers)]
        for mask in range(n_own):
            at = pl.ds(pl.multiple_of((own ^ mask) * tile, tile), tile)
            act_full[:, at] = packet_refs[mask][:layers] / total
            at = pl.ds(pl.multiple_of((n_own - (own ^ mask)) % n_own * tile, tile), tile)
            grad_full[:, at] = packet_refs[mask][layers:] / total
        new_act_ref[...] = state_refs[0][:slot_count]
        new_grad_ref[...] = state_refs[0][slot_count:]
        for layer in range(layers):
            owner_now = owners[layer]
            rank = jnp.int32(0)
            for earlier in range(layer):
                rank += jnp.where(owners[earlier] == owner_now, 1, 0)
            old_act = jnp.zeros((1, width), jnp.float32)
            old_grad = jnp.zeros((1, width), jnp.float32)
            for mask in range(n_own):
                for slot in range(slot_count):
                    here = (owner_now == own ^ mask) & (rank == slot)
                    down = slot_count + slot
                    old_act = jnp.where(here, state_refs[mask][slot : slot + 1], old_act)
                    old_grad = jnp.where(here, state_refs[mask][down : down + 1], old_grad)
            eigen_act = decay_rate * old_act + (1.0 - decay_rate) * act_full[layer : layer + 1]
            eigen_grad = decay_rate * old_grad + (1.0 - decay_rate) * grad_full[layer : layer + 1]
            act_full[layer : layer + 1] = eigen_act
            grad_full[layer : layer + 1] = eigen_grad
            for slot in range(slot_count):

                @pl.when((owner_now == own) & (rank == slot))
                def _(slot=slot, eigen_act=eigen_act, eigen_grad=eigen_grad):
                    new_act_ref[slot : slot + 1] = eigen_act
                    new_grad_ref[slot : slot + 1] = eigen_grad

            damping = damping_rate * (jnp.sum(eigen_grad) / width) * (jnp.sum(eigen_act) / width)
            rows = grad_full[layer : layer + 1, pl.ds(pl.multiple_of(dp * tile, tile), tile)]
            cols = act_full[layer : layer + 1, pl.ds(pl.multiple_of(own * tile, tile), tile)]
            rows = jnp.transpose(jnp.broadcast_to(rows, (128, tile)))
            rows = jnp.concatenate([rows] * (tile // 128), axis=1)
            out_ref[layer] = 1.0 / (total * (rows * cols + damping))

    out_shape = [
        jax.ShapeDtypeStruct((layers, tile, tile), jnp.float32),
        jax.ShapeDtypeStruct((slot_count, width), jnp.float32),
        jax.ShapeDtypeStruct((slot_count, width), jnp.float32),
    ]
    return pl.pallas_call(
        kernel,
        out_shape=out_shape,
        in_specs=[scalar_spec] + [vmem_spec] * (2 * n_own),
        out_specs=[vmem_spec] * len(out_shape),
        scratch_shapes=[pltpu.VMEM((layers, width), jnp.float32)] * 2,
        compiler_params=pltpu.CompilerParams(vmem_limit_bytes=16 * 1024 * 1024),
        cost_estimate=light,
    )(scalars, *states, *packets)


def line_plan(activations, out_grads, basis_act, basis_grad, owner_of, counts, state_act, state_grad):
    layers, tok_rows, width = activations.shape
    tile = basis_act.shape[1]
    n_dp = lax.axis_size("dp")
    n_own = lax.axis_size("owner")
    dp = lax.axis_index("dp")
    own = lax.axis_index("owner")
    scalars = jnp.concatenate([jnp.stack([dp, own]), counts, owner_of]).astype(jnp.int32)

    def after(array, *others):
        return lax.optimization_barrier((array, *others))[0]

    def step(arrays, *others):
        return lax.optimization_barrier((*arrays, *others))[: len(arrays)]

    owners = range(n_own)
    held = [-o % n_own for o in owners]
    cuts = cut_rows((out_grads, activations), tile, n_own, n_dp)
    cuts = [flip(cut, "dp", number % (n_dp - 1) + 1) for number, cut in enumerate(cuts)]
    got_grad, got_act = cuts[: n_dp - 1], cuts[n_dp - 1 :]
    own_grad, stay_grad = load((out_grads, basis_grad), 1)
    pieces = got_grad[:-1] + [after(got_grad[-1], got_act[0], own_grad)]
    pieces += [flip(piece, "owner", 2) for piece in pieces]
    pieces += [flip(piece, "owner", 1) for piece in pieces]
    keep, send = project_rows(scalars, own_grad, pieces, stay_grad, n_own, n_dp)

    near = flip(after(send, *got_act), "dp", 1)
    pieces = [join(got_act[:-1]), got_act[-1]]
    pieces += [flip(after(piece, keep), "owner", 2) for piece in pieces]
    own_act, stay_act = load((activations, basis_act), 1, keep)
    pieces += [flip(after(piece, own_act), "owner", 1) for piece in pieces]
    keep_act, send_act = project_rows(scalars, own_act, pieces, stay_act, n_own, n_dp)

    state = jnp.concatenate([state_act, state_grad], axis=0)
    keep, near, keep_act, send_act, state = step([keep, near, keep_act, send_act, state])
    states = [state] + [flip(state, "owner", mask) for mask in range(1, n_own)]
    parts = add_rows(keep, near, keep.shape[1] // 2)
    parts = [lax.ppermute(array, "owner", [*enumerate(held)]) for array in parts]
    to_pair = [((a, o), (a ^ 2, o)) for a in range(n_dp) for o in owners if (a ^ held[o]) & 2]
    crosses = [hop(array, to_pair) for array in parts]
    near_act = flip(send_act, "dp", 1)

    crosses[0] = after(crosses[0], *states)
    nears = [add(pair) for pair in zip(parts, crosses, strict=True)]
    aside = ((dp ^ (-own % n_own)) // 2).astype(jnp.int32)[None]
    square_grad = squares_of(aside, nears)
    square_far = flip(square_grad, "dp", 2)
    fars = [hop(array, [((held[o] ^ 1, o), (held[o], o)) for o in owners]) for array in nears]
    full = by_layer(nears, fars)
    chip = [hop(array, [((held[o], o), (held[o], o ^ 2)) for o in owners]) for array in full]

    part_act = add((keep_act, near_act))
    cross_act = flip(part_act, "dp", 2)

    done = step([part_act, cross_act, square_grad, square_far, *full, *chip])
    (part_act, cross_act, square_grad, square_far), full, chip = done[:4], done[4:][:layers], done[4 + layers :]
    full_act = add((part_act, cross_act))
    half = halves_of(full_act, square_grad, square_far)
    packet = total_of(half, flip(half, "dp", 1))
    back_act = flip(after(full_act, packet), "dp", 1)
    packets = [packet] + [flip(packet, "owner", mask) for mask in range(1, n_own)]
    source = -dp % n_own
    home = jnp.where(own == source, 0, jnp.where(own == source ^ 2, 1, 2)).astype(jnp.int32)[None]
    full = pick(after(home, *packets), [*zip(full, chip, strict=True)])
    to_core = [((held[o], o ^ b), (held[o], o ^ b ^ 1)) for o in owners for b in (0, 2)]
    core = [hop(array, to_core) for array in full]
    factors, new_act, new_grad = eigenvalues(scalars, states, packets, n_dp)
    grads = pick(home // 2, [*zip(full, core, strict=True)])
    grams = gram_of(grads, full_act)

    grams, factors, back_act, *grads = step([grams, factors, back_act, *grads])
    return finish(grads, back_act, grams, factors), new_act, new_grad


def solution(mesh):
    placed = (
        P("groups", "dp", None),
        P("groups", "dp", None),
        P("groups", "dp", "owner"),
        P("groups", "dp", "owner"),
        P(),
        P("groups"),
        P("owner", "groups"),
        P("owner", "groups"),
    )
    square = mesh.shape["dp"] == 4 and mesh.shape["owner"] == 4
    return jax.shard_map(
        line_plan if square else gather_plan,
        mesh=mesh,
        in_specs=placed,
        out_specs=(P("groups", "dp", "owner"), P("owner", "groups"), P("owner", "groups")),
        check_vma=False,
    )
```

```python
import jax
import jax.numpy as jnp
from jax import lax
from jax.experimental import pallas as pl
from jax.experimental.pallas import tpu as pltpu
from jax.sharding import PartitionSpec as P

decay_rate = 0.25
damping_rate = 0.1
vmem_spec = pl.BlockSpec(memory_space=pltpu.VMEM)
scalar_spec = pl.BlockSpec(memory_space=pltpu.SMEM)
light = pl.CostEstimate(flops=0, bytes_accessed=0, transcendentals=0)


def spread(array, axis, root):
    mine = lax.axis_index(axis) == root
    return lax.psum(jnp.where(mine, array, jnp.zeros_like(array)), axis)


def gather_plan(activations, out_grads, basis_act, basis_grad, owner_of, counts, state_act, state_grad):
    layers = activations.shape[0]
    tok_rows = activations.shape[1]
    tile_rows = basis_act.shape[1]
    tile_cols = basis_act.shape[2]
    slot_count = state_act.shape[0]
    dp_index = lax.axis_index("dp")
    own_index = lax.axis_index("owner")
    valid_rows = (jnp.arange(tok_rows) < counts[dp_index]).astype(jnp.float32)[:, None]
    valid_total = jnp.sum(counts).astype(jnp.float32)
    square_acts = []
    square_grads = []
    gram_tiles = []
    for layer_index in range(layers):
        panel_act = jnp.dot(
            activations[layer_index],
            lax.all_gather(basis_act[layer_index], "dp", axis=0, tiled=True),
            preferred_element_type=jnp.float32,
        )
        panel_grad = jnp.dot(
            out_grads[layer_index],
            lax.all_gather(basis_grad[layer_index], "dp", axis=0, tiled=True),
            preferred_element_type=jnp.float32,
        )
        panel_act = (panel_act * valid_rows).astype(jnp.bfloat16)
        panel_grad = (panel_grad * valid_rows).astype(jnp.bfloat16)
        full_act = lax.all_gather(panel_act, "owner", axis=1, tiled=True)
        full_grad = lax.all_gather(panel_grad, "owner", axis=1, tiled=True)
        square_act = jnp.sum(jnp.square(full_act.astype(jnp.float32)), axis=0)
        square_grad = jnp.sum(jnp.square(full_grad.astype(jnp.float32)), axis=0)
        gram_term = lax.dot_general(
            full_grad, panel_act, (((0,), (0,)), ((), ())), preferred_element_type=jnp.float32
        )
        gram_tiles.append(
            lax.psum_scatter(
                gram_term.astype(jnp.bfloat16), "dp", scatter_dimension=0, tiled=True
            ).astype(jnp.float32)
            / valid_total
        )
        square_act, square_grad = lax.psum((square_act, square_grad), "dp")
        square_acts.append(square_act)
        square_grads.append(square_grad)
    new_act = state_act
    new_grad = state_grad
    results = []
    for layer_index in range(layers):
        owner_now = owner_of[layer_index]
        slot_rank = jnp.sum((owner_of[:layer_index] == owner_now).astype(jnp.int32))
        selector = (jnp.arange(slot_count) == slot_rank).astype(jnp.float32)[:, None]
        local_act = decay_rate * jnp.sum(state_act * selector, axis=0) + (
            1.0 - decay_rate
        ) * (square_acts[layer_index] / valid_total)
        local_grad = decay_rate * jnp.sum(state_grad * selector, axis=0) + (
            1.0 - decay_rate
        ) * (square_grads[layer_index] / valid_total)
        eigen_act = spread(local_act, "owner", owner_now)
        eigen_grad = spread(local_grad, "owner", owner_now)
        replace_rows = ((jnp.arange(slot_count) == slot_rank) & (own_index == owner_now))[:, None]
        new_act = jnp.where(replace_rows, eigen_act[None, :], new_act)
        new_grad = jnp.where(replace_rows, eigen_grad[None, :], new_grad)
        damping = damping_rate * jnp.mean(eigen_grad) * jnp.mean(eigen_act)
        grad_eigen = lax.dynamic_slice_in_dim(eigen_grad, dp_index * tile_rows, tile_rows)
        act_eigen = lax.dynamic_slice_in_dim(eigen_act, own_index * tile_cols, tile_cols)
        scaled = gram_tiles[layer_index] / (grad_eigen[:, None] * act_eigen[None, :] + damping)
        results.append(scaled.astype(jnp.bfloat16))
    return (jnp.stack(results), new_act, new_grad)


def flip(array, axis, mask):
    return lax.ppermute(array, axis, [(i, i ^ mask) for i in range(lax.axis_size(axis))])


def hop(array, pairs):
    owners = lax.axis_size("owner")
    flat = [(a * owners + b, c * owners + e) for (a, b), (c, e) in pairs]
    return lax.ppermute(array, ("dp", "owner"), flat)


def load(arrays, cut, *gates):
    tile = arrays[-1].shape[1]
    shapes = [(*array.shape[:2], tile) if number < cut else array.shape for number, array in enumerate(arrays)]

    def kernel(*refs):
        in_refs, out_refs, sems = refs[: len(arrays)], refs[len(arrays) + len(gates) : -1], refs[-1]
        cols = pl.ds(pl.multiple_of(lax.axis_index("dp") * tile, tile), tile)
        copies = []
        for number, (in_ref, out_ref) in enumerate(zip(in_refs, out_refs, strict=True)):
            source = in_ref.at[:, :, cols] if number < cut else in_ref
            copies.append(pltpu.make_async_copy(source, out_ref, sems.at[number]))
            copies[-1].start()
        for copy in copies:
            copy.wait()

    return pl.pallas_call(
        kernel,
        out_shape=[
            jax.ShapeDtypeStruct(shape, array.dtype) for shape, array in zip(shapes, arrays, strict=True)
        ],
        in_specs=[pl.BlockSpec(memory_space=pltpu.HBM)] * len(arrays) + [pl.BlockSpec(memory_space=pl.ANY)] * len(gates),
        out_specs=[vmem_spec] * len(arrays),
        scratch_shapes=[pltpu.SemaphoreType.DMA((len(arrays),))],
        compiler_params=pltpu.CompilerParams(vmem_limit_bytes=8 * 1024 * 1024),
        cost_estimate=light,
    )(*[pltpu.with_memory_space_constraint(array, pltpu.HBM) for array in arrays], *gates)


def project_rows(scalars, tokens, pieces, basis, n_own, n_dp):
    layers, tok_rows, tile = tokens.shape
    cols = basis.shape[2]
    part_rows = tok_rows // n_own
    packed = 3 * n_dp * tok_rows // 4
    half = packed // 2
    shapes = [(layers, half, cols)] * 2

    def kernel(scalar_ref, tokens_ref, basis_ref, *refs):
        piece_refs, out_refs = refs[: len(pieces)], refs[len(pieces) :]
        dp, own = scalar_ref[0], scalar_ref[1]
        col = lax.broadcasted_iota(jnp.int32, (1, n_dp * tok_rows), 1)
        turn = (col - tok_rows) // part_rows
        peer = turn // (n_dp - 1)
        peer = own ^ (((peer & 1) << 1) | (peer >> 1))
        mine = col < tok_rows
        mask = jnp.where(mine, 0, turn % (n_dp - 1) + 1)
        index = jnp.where(mine, col, peer * part_rows + col % part_rows)
        place = jnp.full_like(col, -1)
        for number in range(n_dp):
            shard = dp ^ number
            start = jnp.int32(0)
            for other in range(n_dp):
                start += jnp.where(other < shard, scalar_ref[2 + other], 0)
            here = (mask == number) & (index < scalar_ref[2 + shard])
            place = jnp.where(here, start + index, place)
        row = lax.broadcasted_iota(jnp.int32, (packed, n_dp * tok_rows), 0)
        row = row + jnp.where(dp % 2 == 0, 0, jnp.where(row < half, half, -half))
        select = (row == place).astype(jnp.bfloat16)
        for layer in range(layers):
            rows = jnp.concatenate([tokens_ref[layer]] + [p[layer] for p in piece_refs], axis=0)
            chosen = jnp.dot(select, rows, preferred_element_type=jnp.float32).astype(jnp.bfloat16)
            result = jnp.dot(chosen, basis_ref[layer], preferred_element_type=jnp.float32).astype(
                jnp.bfloat16
            )
            out_refs[0][layer] = result[:half]
            out_refs[1][layer] = result[half:]

    return pl.pallas_call(
        kernel,
        out_shape=[jax.ShapeDtypeStruct(shape, jnp.bfloat16) for shape in shapes],
        in_specs=[scalar_spec] + [vmem_spec] * (2 + len(pieces)),
        out_specs=[vmem_spec] * len(shapes),
        compiler_params=pltpu.CompilerParams(vmem_limit_bytes=16 * 1024 * 1024),
        cost_estimate=light,
    )(scalars, tokens, basis, *pieces)


def add(*pairs):
    layers = pairs[0][0].shape[0]

    def kernel(*refs):
        for number in range(len(pairs)):
            total = refs[2 * number][...].astype(jnp.float32) + refs[2 * number + 1][...].astype(jnp.float32)
            refs[-1][number * layers : (number + 1) * layers] = total.astype(refs[-1].dtype)

    first = pairs[0][0]
    return pl.pallas_call(
        kernel,
        out_shape=jax.ShapeDtypeStruct((layers * len(pairs), *first.shape[1:]), first.dtype),
        in_specs=[vmem_spec] * (2 * len(pairs)),
        out_specs=vmem_spec,
        compiler_params=pltpu.CompilerParams(vmem_limit_bytes=8 * 1024 * 1024),
        cost_estimate=light,
    )(*[array for pair in pairs for array in pair])


def add_rows(near, far, cut):
    layers, height, cols = near.shape
    spans = [(0, cut), (cut, height)]

    def kernel(near_ref, far_ref, *out_refs):
        for out_ref, (start, stop) in zip(out_refs, spans, strict=True):
            total = near_ref[:, start:stop].astype(jnp.float32) + far_ref[:, start:stop].astype(jnp.float32)
            out_ref[...] = total.astype(out_ref.dtype)

    return pl.pallas_call(
        kernel,
        out_shape=[jax.ShapeDtypeStruct((layers, stop - start, cols), near.dtype) for start, stop in spans],
        in_specs=[vmem_spec] * 2,
        out_specs=[vmem_spec] * len(spans),
        compiler_params=pltpu.CompilerParams(vmem_limit_bytes=8 * 1024 * 1024),
        cost_estimate=light,
    )(near, far)


def by_layer(nears, fars):
    layers, _, cols = nears[0].shape
    count = len(nears)
    height = sum(array.shape[1] for array in nears)

    def kernel(*refs):
        for side in range(2):
            start = 0
            for ref in refs[side * count : (side + 1) * count]:
                for layer, out_ref in enumerate(refs[2 * count :]):
                    out_ref[side, start : start + ref.shape[1]] = ref[layer]
                start += ref.shape[1]

    return pl.pallas_call(
        kernel,
        out_shape=[jax.ShapeDtypeStruct((2, height, cols), nears[0].dtype)] * layers,
        in_specs=[vmem_spec] * (2 * count),
        out_specs=[vmem_spec] * layers,
        compiler_params=pltpu.CompilerParams(vmem_limit_bytes=8 * 1024 * 1024),
        cost_estimate=light,
    )(*nears, *fars)


def join(arrays):
    layers, rows, cols = arrays[0].shape

    def kernel(*refs):
        for number, ref in enumerate(refs[:-1]):
            refs[-1][:, number * rows : (number + 1) * rows] = ref[...]

    return pl.pallas_call(
        kernel,
        out_shape=jax.ShapeDtypeStruct((layers, len(arrays) * rows, cols), arrays[0].dtype),
        in_specs=[vmem_spec] * len(arrays),
        out_specs=vmem_spec,
        compiler_params=pltpu.CompilerParams(vmem_limit_bytes=8 * 1024 * 1024),
        cost_estimate=light,
    )(*arrays)


def cut_rows(arrays, tile, n_own, n_dp):
    layers, tok_rows, _ = arrays[0].shape
    part_rows = tok_rows // n_own
    peers = n_dp - 1

    def kernel(*refs):
        in_refs, out_refs, sems = refs[: len(arrays)], refs[len(arrays) : -1], refs[-1]
        dp, own = lax.axis_index("dp"), lax.axis_index("owner")
        rows = pl.ds(pl.multiple_of(own * part_rows, part_rows), part_rows)
        copies = []
        for number, out_ref in enumerate(out_refs):
            block = dp ^ (number % peers + 1)
            cols = pl.ds(pl.multiple_of(block * tile, tile), tile)
            copies.append(
                pltpu.make_async_copy(in_refs[number // peers].at[:, rows, cols], out_ref, sems.at[number])
            )
            copies[-1].start()
        for copy in copies:
            copy.wait()

    count = len(arrays) * peers
    return pl.pallas_call(
        kernel,
        out_shape=[jax.ShapeDtypeStruct((layers, part_rows, tile), arrays[0].dtype)] * count,
        in_specs=[pl.BlockSpec(memory_space=pltpu.HBM)] * len(arrays),
        out_specs=[vmem_spec] * count,
        scratch_shapes=[pltpu.SemaphoreType.DMA((count,))],
        compiler_params=pltpu.CompilerParams(vmem_limit_bytes=8 * 1024 * 1024),
        cost_estimate=light,
    )(*[pltpu.with_memory_space_constraint(array, pltpu.HBM) for array in arrays])


def pick(home, choices):
    flat = [array for arrays in choices for array in arrays]
    count = len(choices[0])

    def kernel(home_ref, *refs):
        for index in range(count):

            @pl.when(home_ref[0] == index)
            def _(index=index):
                for number, out_ref in enumerate(refs[len(flat) :]):
                    out_ref[...] = refs[number * count + index][...]

    return pl.pallas_call(
        kernel,
        out_shape=[jax.ShapeDtypeStruct(arrays[0].shape, arrays[0].dtype) for arrays in choices],
        in_specs=[scalar_spec] + [vmem_spec] * len(flat),
        out_specs=[vmem_spec] * len(choices),
        compiler_params=pltpu.CompilerParams(vmem_limit_bytes=12 * 1024 * 1024),
        cost_estimate=light,
    )(home, *flat)


def squares_of(aside, panels):
    layers, _, cols = panels[0].shape

    def kernel(aside_ref, *refs):
        for layer in range(layers):
            total = jnp.zeros((1, cols), jnp.float32)
            for ref in refs[:-1]:
                wide = ref[layer].astype(jnp.float32)
                total += jnp.sum(wide * wide, axis=0, keepdims=True)
            refs[-1][layer : layer + 1] = jnp.where(aside_ref[0] == 0, total, 0.0)

    return pl.pallas_call(
        kernel,
        out_shape=jax.ShapeDtypeStruct((layers, cols), jnp.float32),
        in_specs=[scalar_spec] + [vmem_spec] * len(panels),
        out_specs=vmem_spec,
        compiler_params=pltpu.CompilerParams(vmem_limit_bytes=8 * 1024 * 1024),
        cost_estimate=light,
    )(aside, *panels)


def halves_of(act, near, far):
    layers, _, cols = act.shape

    def kernel(act_ref, near_ref, far_ref, out_ref):
        for layer in range(layers):
            wide = act_ref[layer].astype(jnp.float32)
            out_ref[layer : layer + 1] = jnp.sum(wide * wide, axis=0, keepdims=True)
        out_ref[layers:] = near_ref[...] + far_ref[...]

    return pl.pallas_call(
        kernel,
        out_shape=jax.ShapeDtypeStruct((2 * layers, cols), jnp.float32),
        in_specs=[vmem_spec] * 3,
        out_specs=vmem_spec,
        compiler_params=pltpu.CompilerParams(vmem_limit_bytes=8 * 1024 * 1024),
        cost_estimate=light,
    )(act, near, far)


def total_of(near, far):
    def kernel(near_ref, far_ref, out_ref):
        out_ref[...] = near_ref[...] + far_ref[...]

    return pl.pallas_call(
        kernel,
        out_shape=jax.ShapeDtypeStruct(near.shape, near.dtype),
        in_specs=[vmem_spec] * 2,
        out_specs=vmem_spec,
        compiler_params=pltpu.CompilerParams(vmem_limit_bytes=4 * 1024 * 1024),
        cost_estimate=light,
    )(near, far)


def gram_of(grads, act):
    layers, _, cols = act.shape

    def kernel(*refs):
        for layer in range(layers):
            refs[-1][layer] = product_of(refs[layer][0], refs[-2][layer])

    return pl.pallas_call(
        kernel,
        out_shape=jax.ShapeDtypeStruct((layers, grads[0].shape[2], cols), jnp.float32),
        in_specs=[vmem_spec] * (layers + 1),
        out_specs=vmem_spec,
        compiler_params=pltpu.CompilerParams(vmem_limit_bytes=16 * 1024 * 1024),
        cost_estimate=light,
    )(*grads, act)


def product_of(grad, act):
    return lax.dot_general(grad, act, (((0,), (0,)), ((), ())), preferred_element_type=jnp.float32)


def finish(grads, act, grams, factors):
    layers, tile, cols = grams.shape

    def kernel(*refs):
        grad_refs, (act_ref, gram_ref, factor_ref, out_hbm, out_ref, sems) = refs[:layers], refs[layers:]
        copies = []
        for layer in range(layers):
            gram = gram_ref[layer] + product_of(grad_refs[layer][1], act_ref[layer])
            out_ref[layer] = (gram * factor_ref[layer]).astype(jnp.bfloat16)
            copies.append(pltpu.make_async_copy(out_ref.at[layer], out_hbm.at[layer], sems.at[layer]))
            copies[-1].start()
        for copy in copies:
            copy.wait()

    return pl.pallas_call(
        kernel,
        out_shape=jax.ShapeDtypeStruct((layers, tile, cols), jnp.bfloat16),
        in_specs=[vmem_spec] * (layers + 3),
        out_specs=pl.BlockSpec(memory_space=pl.ANY),
        scratch_shapes=[pltpu.VMEM((layers, tile, cols), jnp.bfloat16), pltpu.SemaphoreType.DMA((layers,))],
        compiler_params=pltpu.CompilerParams(vmem_limit_bytes=24 * 1024 * 1024),
        cost_estimate=light,
    )(*grads, act, grams, factors)


def eigenvalues(scalars, states, packets, n_dp):
    n_own = len(packets)
    layers, tile = packets[0].shape[0] // 2, packets[0].shape[1]
    slot_count, width = states[0].shape[0] // 2, states[0].shape[1]

    def kernel(scalar_ref, *refs):
        state_refs, packet_refs, refs = refs[:n_own], refs[n_own : 2 * n_own], refs[2 * n_own :]
        out_ref, new_act_ref, new_grad_ref, act_full, grad_full = refs
        dp, own = scalar_ref[0], scalar_ref[1]
        total = scalar_ref[2]
        for index in range(1, n_dp):
            total += scalar_ref[2 + index]
        total = total.astype(jnp.float32)
        owners = [scalar_ref[2 + n_dp + layer] for layer in range(layers)]
        for mask in range(n_own):
            at = pl.ds(pl.multiple_of((own ^ mask) * tile, tile), tile)
            act_full[:, at] = packet_refs[mask][:layers] / total
            at = pl.ds(pl.multiple_of((n_own - (own ^ mask)) % n_own * tile, tile), tile)
            grad_full[:, at] = packet_refs[mask][layers:] / total
        new_acts = [state_refs[0][slot : slot + 1] for slot in range(slot_count)]
        new_grads = [state_refs[0][slot_count + slot : slot_count + slot + 1] for slot in range(slot_count)]
        for layer in range(layers):
            owner_now = owners[layer]
            rank = jnp.int32(0)
            for earlier in range(layer):
                rank += jnp.where(owners[earlier] == owner_now, 1, 0)
            old_act = jnp.zeros((1, width), jnp.float32)
            old_grad = jnp.zeros((1, width), jnp.float32)
            for mask in range(n_own):
                for slot in range(slot_count):
                    here = (owner_now == own ^ mask) & (rank == slot)
                    down = slot_count + slot
                    old_act = jnp.where(here, state_refs[mask][slot : slot + 1], old_act)
                    old_grad = jnp.where(here, state_refs[mask][down : down + 1], old_grad)
            eigen_act = decay_rate * old_act + (1.0 - decay_rate) * act_full[layer : layer + 1]
            eigen_grad = decay_rate * old_grad + (1.0 - decay_rate) * grad_full[layer : layer + 1]
            act_full[layer : layer + 1] = eigen_act
            grad_full[layer : layer + 1] = eigen_grad
            for slot in range(slot_count):
                here = (owner_now == own) & (rank == slot)
                new_acts[slot] = jnp.where(here, eigen_act, new_acts[slot])
                new_grads[slot] = jnp.where(here, eigen_grad, new_grads[slot])

            damping = damping_rate * (jnp.sum(eigen_grad) / width) * (jnp.sum(eigen_act) / width)
            rows = grad_full[layer : layer + 1, pl.ds(pl.multiple_of(dp * tile, tile), tile)]
            cols = act_full[layer : layer + 1, pl.ds(pl.multiple_of(own * tile, tile), tile)]
            rows = jnp.transpose(jnp.broadcast_to(rows, (128, tile)))
            rows = jnp.concatenate([rows] * (tile // 128), axis=1)
            out_ref[layer] = 1.0 / (total * (rows * cols + damping))
        for slot in range(slot_count):
            new_act_ref[slot : slot + 1] = new_acts[slot]
            new_grad_ref[slot : slot + 1] = new_grads[slot]

    out_shape = [
        jax.ShapeDtypeStruct((layers, tile, tile), jnp.float32),
        jax.ShapeDtypeStruct((slot_count, width), jnp.float32),
        jax.ShapeDtypeStruct((slot_count, width), jnp.float32),
    ]
    return pl.pallas_call(
        kernel,
        out_shape=out_shape,
        in_specs=[scalar_spec] + [vmem_spec] * (2 * n_own),
        out_specs=[vmem_spec] * len(out_shape),
        scratch_shapes=[pltpu.VMEM((layers, width), jnp.float32)] * 2,
        compiler_params=pltpu.CompilerParams(vmem_limit_bytes=16 * 1024 * 1024),
        cost_estimate=light,
    )(scalars, *states, *packets)


def line_plan(activations, out_grads, basis_act, basis_grad, owner_of, counts, state_act, state_grad):
    layers, tok_rows, width = activations.shape
    tile = basis_act.shape[1]
    n_dp = lax.axis_size("dp")
    n_own = lax.axis_size("owner")
    dp = lax.axis_index("dp")
    own = lax.axis_index("owner")
    scalars = jnp.concatenate([jnp.stack([dp, own]), counts, owner_of]).astype(jnp.int32)

    def after(array, *others):
        return lax.optimization_barrier((array, *others))[0]

    def step(arrays, *others):
        return lax.optimization_barrier((*arrays, *others))[: len(arrays)]

    owners = range(n_own)
    held = [-o % n_own for o in owners]
    cuts = cut_rows((out_grads, activations), tile, n_own, n_dp)
    cuts = [flip(cut, "dp", number % (n_dp - 1) + 1) for number, cut in enumerate(cuts)]
    got_grad, got_act = cuts[: n_dp - 1], cuts[n_dp - 1 :]
    own_grad, stay_grad = load((out_grads, basis_grad), 1)
    pieces = got_grad[:-1] + [after(got_grad[-1], got_act[0], own_grad)]
    pieces += [flip(piece, "owner", 2) for piece in pieces]
    pieces += [flip(piece, "owner", 1) for piece in pieces]
    keep, send = project_rows(scalars, own_grad, pieces, stay_grad, n_own, n_dp)

    near = flip(after(send, *got_act), "dp", 1)
    pieces = [join(got_act[:-1]), got_act[-1]]
    pieces += [flip(after(piece, keep), "owner", 2) for piece in pieces]
    own_act, stay_act = load((activations, basis_act), 1, keep)
    pieces += [flip(after(piece, own_act), "owner", 1) for piece in pieces]
    keep_act, send_act = project_rows(scalars, own_act, pieces, stay_act, n_own, n_dp)

    state = jnp.concatenate([state_act, state_grad], axis=0)
    keep, near, keep_act, send_act, state = step([keep, near, keep_act, send_act, state])
    states = [state] + [flip(state, "owner", mask) for mask in range(1, n_own)]
    parts = add_rows(keep, near, keep.shape[1] * 7 // 12)
    parts = [lax.ppermute(array, "owner", [*enumerate(held)]) for array in parts]
    to_pair = [((a, o), (a ^ 2, o)) for a in range(n_dp) for o in owners if (a ^ held[o]) & 2]
    crosses = [hop(array, to_pair) for array in parts]
    near_act = flip(send_act, "dp", 1)

    crosses[0] = after(crosses[0], *states)
    nears = [add(pair) for pair in zip(parts, crosses, strict=True)]
    aside = ((dp ^ (-own % n_own)) // 2).astype(jnp.int32)[None]
    square_grad = squares_of(aside, nears)
    square_far = flip(square_grad, "dp", 2)
    fars = [hop(array, [((held[o] ^ 1, o), (held[o], o)) for o in owners]) for array in nears]
    full = by_layer(nears, fars)
    chip = [hop(array, [((held[o], o), (held[o], o ^ 2)) for o in owners]) for array in full]

    part_act = add((keep_act, near_act))
    cross_act = flip(part_act, "dp", 2)

    done = step([part_act, cross_act, square_grad, square_far, *full, *chip])
    (part_act, cross_act, square_grad, square_far), full, chip = done[:4], done[4:][:layers], done[4 + layers :]
    full_act = add((part_act, cross_act))
    half = halves_of(full_act, square_grad, square_far)
    packet = total_of(half, flip(half, "dp", 1))
    back_act = flip(after(full_act, packet), "dp", 1)
    packets = [packet] + [flip(packet, "owner", mask) for mask in range(1, n_own)]
    source = -dp % n_own
    home = jnp.where(own == source, 0, jnp.where(own == source ^ 2, 1, 2)).astype(jnp.int32)[None]
    full = pick(after(home, *packets), [*zip(full, chip, strict=True)])
    to_core = [((held[o], o ^ b), (held[o], o ^ b ^ 1)) for o in owners for b in (0, 2)]
    core = [hop(array, to_core) for array in full]
    factors, new_act, new_grad = eigenvalues(scalars, states, packets, n_dp)
    grads = pick(home // 2, [*zip(full, core, strict=True)])
    grams = gram_of(grads, full_act)

    grams, factors, back_act, *grads = step([grams, factors, back_act, *grads])
    return finish(grads, back_act, grams, factors), new_act, new_grad


def solution(mesh):
    placed = (
        P("groups", "dp", None),
        P("groups", "dp", None),
        P("groups", "dp", "owner"),
        P("groups", "dp", "owner"),
        P(),
        P("groups"),
        P("owner", "groups"),
        P("owner", "groups"),
    )
    square = mesh.shape["dp"] == 4 and mesh.shape["owner"] == 4
    return jax.shard_map(
        line_plan if square else gather_plan,
        mesh=mesh,
        in_specs=placed,
        out_specs=(P("groups", "dp", "owner"), P("owner", "groups"), P("owner", "groups")),
        check_vma=False,
    )
```

```python
import jax
import jax.numpy as jnp
from jax import lax
from jax.experimental import pallas as pl
from jax.experimental.pallas import tpu as pltpu
from jax.sharding import PartitionSpec as P

decay_rate = 0.25
damping_rate = 0.1
vmem_spec = pl.BlockSpec(memory_space=pltpu.VMEM)
scalar_spec = pl.BlockSpec(memory_space=pltpu.SMEM)
light = pl.CostEstimate(flops=0, bytes_accessed=0, transcendentals=0)


def spread(array, axis, root):
    mine = lax.axis_index(axis) == root
    return lax.psum(jnp.where(mine, array, jnp.zeros_like(array)), axis)


def gather_plan(activations, out_grads, basis_act, basis_grad, owner_of, counts, state_act, state_grad):
    layers = activations.shape[0]
    tok_rows = activations.shape[1]
    tile_rows = basis_act.shape[1]
    tile_cols = basis_act.shape[2]
    slot_count = state_act.shape[0]
    dp_index = lax.axis_index("dp")
    own_index = lax.axis_index("owner")
    valid_rows = (jnp.arange(tok_rows) < counts[dp_index]).astype(jnp.float32)[:, None]
    valid_total = jnp.sum(counts).astype(jnp.float32)
    square_acts = []
    square_grads = []
    gram_tiles = []
    for layer_index in range(layers):
        panel_act = jnp.dot(
            activations[layer_index],
            lax.all_gather(basis_act[layer_index], "dp", axis=0, tiled=True),
            preferred_element_type=jnp.float32,
        )
        panel_grad = jnp.dot(
            out_grads[layer_index],
            lax.all_gather(basis_grad[layer_index], "dp", axis=0, tiled=True),
            preferred_element_type=jnp.float32,
        )
        panel_act = (panel_act * valid_rows).astype(jnp.bfloat16)
        panel_grad = (panel_grad * valid_rows).astype(jnp.bfloat16)
        full_act = lax.all_gather(panel_act, "owner", axis=1, tiled=True)
        full_grad = lax.all_gather(panel_grad, "owner", axis=1, tiled=True)
        square_act = jnp.sum(jnp.square(full_act.astype(jnp.float32)), axis=0)
        square_grad = jnp.sum(jnp.square(full_grad.astype(jnp.float32)), axis=0)
        gram_term = lax.dot_general(
            full_grad, panel_act, (((0,), (0,)), ((), ())), preferred_element_type=jnp.float32
        )
        gram_tiles.append(
            lax.psum_scatter(
                gram_term.astype(jnp.bfloat16), "dp", scatter_dimension=0, tiled=True
            ).astype(jnp.float32)
            / valid_total
        )
        square_act, square_grad = lax.psum((square_act, square_grad), "dp")
        square_acts.append(square_act)
        square_grads.append(square_grad)
    new_act = state_act
    new_grad = state_grad
    results = []
    for layer_index in range(layers):
        owner_now = owner_of[layer_index]
        slot_rank = jnp.sum((owner_of[:layer_index] == owner_now).astype(jnp.int32))
        selector = (jnp.arange(slot_count) == slot_rank).astype(jnp.float32)[:, None]
        local_act = decay_rate * jnp.sum(state_act * selector, axis=0) + (
            1.0 - decay_rate
        ) * (square_acts[layer_index] / valid_total)
        local_grad = decay_rate * jnp.sum(state_grad * selector, axis=0) + (
            1.0 - decay_rate
        ) * (square_grads[layer_index] / valid_total)
        eigen_act = spread(local_act, "owner", owner_now)
        eigen_grad = spread(local_grad, "owner", owner_now)
        replace_rows = ((jnp.arange(slot_count) == slot_rank) & (own_index == owner_now))[:, None]
        new_act = jnp.where(replace_rows, eigen_act[None, :], new_act)
        new_grad = jnp.where(replace_rows, eigen_grad[None, :], new_grad)
        damping = damping_rate * jnp.mean(eigen_grad) * jnp.mean(eigen_act)
        grad_eigen = lax.dynamic_slice_in_dim(eigen_grad, dp_index * tile_rows, tile_rows)
        act_eigen = lax.dynamic_slice_in_dim(eigen_act, own_index * tile_cols, tile_cols)
        scaled = gram_tiles[layer_index] / (grad_eigen[:, None] * act_eigen[None, :] + damping)
        results.append(scaled.astype(jnp.bfloat16))
    return (jnp.stack(results), new_act, new_grad)


def flip(array, axis, mask):
    return lax.ppermute(array, axis, [(i, i ^ mask) for i in range(lax.axis_size(axis))])


def hop(array, pairs):
    owners = lax.axis_size("owner")
    flat = [(a * owners + b, c * owners + e) for (a, b), (c, e) in pairs]
    return lax.ppermute(array, ("dp", "owner"), flat)


def load(arrays, cut, *gates):
    tile = arrays[-1].shape[1]
    shapes = [(*array.shape[:2], tile) if number < cut else array.shape for number, array in enumerate(arrays)]

    def kernel(*refs):
        in_refs, out_refs, sems = refs[: len(arrays)], refs[len(arrays) + len(gates) : -1], refs[-1]
        cols = pl.ds(pl.multiple_of(lax.axis_index("dp") * tile, tile), tile)
        copies = []
        for number, (in_ref, out_ref) in enumerate(zip(in_refs, out_refs, strict=True)):
            source = in_ref.at[:, :, cols] if number < cut else in_ref
            copies.append(pltpu.make_async_copy(source, out_ref, sems.at[number]))
            copies[-1].start()
        for copy in copies:
            copy.wait()

    return pl.pallas_call(
        kernel,
        out_shape=[
            jax.ShapeDtypeStruct(shape, array.dtype) for shape, array in zip(shapes, arrays, strict=True)
        ],
        in_specs=[pl.BlockSpec(memory_space=pltpu.HBM)] * len(arrays) + [pl.BlockSpec(memory_space=pl.ANY)] * len(gates),
        out_specs=[vmem_spec] * len(arrays),
        scratch_shapes=[pltpu.SemaphoreType.DMA((len(arrays),))],
        compiler_params=pltpu.CompilerParams(vmem_limit_bytes=8 * 1024 * 1024),
        cost_estimate=light,
    )(*[pltpu.with_memory_space_constraint(array, pltpu.HBM) for array in arrays], *gates)


def project_rows(scalars, tokens, pieces, basis, n_own, n_dp):
    layers, tok_rows, tile = tokens.shape
    cols = basis.shape[2]
    part_rows = tok_rows // n_own
    packed = 3 * n_dp * tok_rows // 4
    half = packed // 2
    shapes = [(layers, half, cols)] * 2

    def kernel(scalar_ref, tokens_ref, basis_ref, *refs):
        piece_refs, out_refs = refs[: len(pieces)], refs[len(pieces) :]
        dp, own = scalar_ref[0], scalar_ref[1]
        col = lax.broadcasted_iota(jnp.int32, (1, n_dp * tok_rows), 1)
        turn = (col - tok_rows) // part_rows
        peer = turn // (n_dp - 1)
        peer = own ^ (((peer & 1) << 1) | (peer >> 1))
        mine = col < tok_rows
        mask = jnp.where(mine, 0, turn % (n_dp - 1) + 1)
        index = jnp.where(mine, col, peer * part_rows + col % part_rows)
        place = jnp.full_like(col, -1)
        for number in range(n_dp):
            shard = dp ^ number
            start = jnp.int32(0)
            for other in range(n_dp):
                start += jnp.where(other < shard, scalar_ref[2 + other], 0)
            here = (mask == number) & (index < scalar_ref[2 + shard])
            place = jnp.where(here, start + index, place)
        row = lax.broadcasted_iota(jnp.int32, (packed, n_dp * tok_rows), 0)
        row = row + jnp.where(dp % 2 == 0, 0, jnp.where(row < half, half, -half))
        select = (row == place).astype(jnp.bfloat16)
        for layer in range(layers):
            rows = jnp.concatenate([tokens_ref[layer]] + [p[layer] for p in piece_refs], axis=0)
            chosen = jnp.dot(select, rows, preferred_element_type=jnp.float32).astype(jnp.bfloat16)
            result = jnp.dot(chosen, basis_ref[layer], preferred_element_type=jnp.float32).astype(
                jnp.bfloat16
            )
            out_refs[0][layer] = result[:half]
            out_refs[1][layer] = result[half:]

    return pl.pallas_call(
        kernel,
        out_shape=[jax.ShapeDtypeStruct(shape, jnp.bfloat16) for shape in shapes],
        in_specs=[scalar_spec] + [vmem_spec] * (2 + len(pieces)),
        out_specs=[vmem_spec] * len(shapes),
        compiler_params=pltpu.CompilerParams(vmem_limit_bytes=16 * 1024 * 1024),
        cost_estimate=light,
    )(scalars, tokens, basis, *pieces)


def add(*pairs):
    layers = pairs[0][0].shape[0]

    def kernel(*refs):
        for number in range(len(pairs)):
            total = refs[2 * number][...].astype(jnp.float32) + refs[2 * number + 1][...].astype(jnp.float32)
            refs[-1][number * layers : (number + 1) * layers] = total.astype(refs[-1].dtype)

    first = pairs[0][0]
    return pl.pallas_call(
        kernel,
        out_shape=jax.ShapeDtypeStruct((layers * len(pairs), *first.shape[1:]), first.dtype),
        in_specs=[vmem_spec] * (2 * len(pairs)),
        out_specs=vmem_spec,
        compiler_params=pltpu.CompilerParams(vmem_limit_bytes=8 * 1024 * 1024),
        cost_estimate=light,
    )(*[array for pair in pairs for array in pair])


def add_rows(near, far, cut):
    layers, height, cols = near.shape
    spans = [(0, cut), (cut, height)]

    def kernel(near_ref, far_ref, *out_refs):
        for out_ref, (start, stop) in zip(out_refs, spans, strict=True):
            total = near_ref[:, start:stop].astype(jnp.float32) + far_ref[:, start:stop].astype(jnp.float32)
            out_ref[...] = total.astype(out_ref.dtype)

    return pl.pallas_call(
        kernel,
        out_shape=[jax.ShapeDtypeStruct((layers, stop - start, cols), near.dtype) for start, stop in spans],
        in_specs=[vmem_spec] * 2,
        out_specs=[vmem_spec] * len(spans),
        compiler_params=pltpu.CompilerParams(vmem_limit_bytes=8 * 1024 * 1024),
        cost_estimate=light,
    )(near, far)


def by_layer(nears, fars):
    layers, _, cols = nears[0].shape
    count = len(nears)
    height = sum(array.shape[1] for array in nears)

    def kernel(*refs):
        for side in range(2):
            start = 0
            for ref in refs[side * count : (side + 1) * count]:
                for layer, out_ref in enumerate(refs[2 * count :]):
                    out_ref[side, start : start + ref.shape[1]] = ref[layer]
                start += ref.shape[1]

    return pl.pallas_call(
        kernel,
        out_shape=[jax.ShapeDtypeStruct((2, height, cols), nears[0].dtype)] * layers,
        in_specs=[vmem_spec] * (2 * count),
        out_specs=[vmem_spec] * layers,
        compiler_params=pltpu.CompilerParams(vmem_limit_bytes=8 * 1024 * 1024),
        cost_estimate=light,
    )(*nears, *fars)


def join(arrays):
    layers, rows, cols = arrays[0].shape

    def kernel(*refs):
        for number, ref in enumerate(refs[:-1]):
            refs[-1][:, number * rows : (number + 1) * rows] = ref[...]

    return pl.pallas_call(
        kernel,
        out_shape=jax.ShapeDtypeStruct((layers, len(arrays) * rows, cols), arrays[0].dtype),
        in_specs=[vmem_spec] * len(arrays),
        out_specs=vmem_spec,
        compiler_params=pltpu.CompilerParams(vmem_limit_bytes=8 * 1024 * 1024),
        cost_estimate=light,
    )(*arrays)


def cut_rows(arrays, tile, n_own, n_dp):
    layers, tok_rows, _ = arrays[0].shape
    part_rows = tok_rows // n_own
    peers = n_dp - 1

    def kernel(*refs):
        in_refs, out_refs, sems = refs[: len(arrays)], refs[len(arrays) : -1], refs[-1]
        dp, own = lax.axis_index("dp"), lax.axis_index("owner")
        rows = pl.ds(pl.multiple_of(own * part_rows, part_rows), part_rows)
        copies = []
        for number, out_ref in enumerate(out_refs):
            block = dp ^ (number % peers + 1)
            cols = pl.ds(pl.multiple_of(block * tile, tile), tile)
            copies.append(
                pltpu.make_async_copy(in_refs[number // peers].at[:, rows, cols], out_ref, sems.at[number])
            )
            copies[-1].start()
        for copy in copies:
            copy.wait()

    count = len(arrays) * peers
    return pl.pallas_call(
        kernel,
        out_shape=[jax.ShapeDtypeStruct((layers, part_rows, tile), arrays[0].dtype)] * count,
        in_specs=[pl.BlockSpec(memory_space=pltpu.HBM)] * len(arrays),
        out_specs=[vmem_spec] * count,
        scratch_shapes=[pltpu.SemaphoreType.DMA((count,))],
        compiler_params=pltpu.CompilerParams(vmem_limit_bytes=8 * 1024 * 1024),
        cost_estimate=light,
    )(*[pltpu.with_memory_space_constraint(array, pltpu.HBM) for array in arrays])


def pick(home, choices):
    flat = [array for arrays in choices for array in arrays]
    count = len(choices[0])

    def kernel(home_ref, *refs):
        for index in range(count):

            @pl.when(home_ref[0] == index)
            def _(index=index):
                for number, out_ref in enumerate(refs[len(flat) :]):
                    out_ref[...] = refs[number * count + index][...]

    return pl.pallas_call(
        kernel,
        out_shape=[jax.ShapeDtypeStruct(arrays[0].shape, arrays[0].dtype) for arrays in choices],
        in_specs=[scalar_spec] + [vmem_spec] * len(flat),
        out_specs=[vmem_spec] * len(choices),
        compiler_params=pltpu.CompilerParams(vmem_limit_bytes=12 * 1024 * 1024),
        cost_estimate=light,
    )(home, *flat)


def squares_of(aside, panels):
    layers, _, cols = panels[0].shape

    def kernel(aside_ref, *refs):
        for layer in range(layers):
            total = jnp.zeros((1, cols), jnp.float32)
            for ref in refs[:-1]:
                wide = ref[layer].astype(jnp.float32)
                total += jnp.sum(wide * wide, axis=0, keepdims=True)
            refs[-1][layer : layer + 1] = jnp.where(aside_ref[0] == 0, total, 0.0)

    return pl.pallas_call(
        kernel,
        out_shape=jax.ShapeDtypeStruct((layers, cols), jnp.float32),
        in_specs=[scalar_spec] + [vmem_spec] * len(panels),
        out_specs=vmem_spec,
        compiler_params=pltpu.CompilerParams(vmem_limit_bytes=8 * 1024 * 1024),
        cost_estimate=light,
    )(aside, *panels)


def settle(part, cross, near, far):
    layers, _, cols = part.shape

    def kernel(part_ref, cross_ref, near_ref, far_ref, act_ref, out_ref):
        for layer in range(layers):
            total = part_ref[layer].astype(jnp.float32) + cross_ref[layer].astype(jnp.float32)
            total = total.astype(act_ref.dtype)
            act_ref[layer] = total
            wide = total.astype(jnp.float32)
            out_ref[layer : layer + 1] = jnp.sum(wide * wide, axis=0, keepdims=True)
        out_ref[layers:] = near_ref[...] + far_ref[...]

    return pl.pallas_call(
        kernel,
        out_shape=[
            jax.ShapeDtypeStruct(part.shape, part.dtype),
            jax.ShapeDtypeStruct((2 * layers, cols), jnp.float32),
        ],
        in_specs=[vmem_spec] * 4,
        out_specs=[vmem_spec] * 2,
        compiler_params=pltpu.CompilerParams(vmem_limit_bytes=8 * 1024 * 1024),
        cost_estimate=light,
    )(part, cross, near, far)


def total_of(near, far):
    def kernel(near_ref, far_ref, out_ref):
        out_ref[...] = near_ref[...] + far_ref[...]

    return pl.pallas_call(
        kernel,
        out_shape=jax.ShapeDtypeStruct(near.shape, near.dtype),
        in_specs=[vmem_spec] * 2,
        out_specs=vmem_spec,
        compiler_params=pltpu.CompilerParams(vmem_limit_bytes=4 * 1024 * 1024),
        cost_estimate=light,
    )(near, far)


def gram_of(grads, act):
    layers, _, cols = act.shape

    def kernel(*refs):
        for layer in range(layers):
            refs[-1][layer] = product_of(refs[layer][0], refs[-2][layer])

    return pl.pallas_call(
        kernel,
        out_shape=jax.ShapeDtypeStruct((layers, grads[0].shape[2], cols), jnp.float32),
        in_specs=[vmem_spec] * (layers + 1),
        out_specs=vmem_spec,
        compiler_params=pltpu.CompilerParams(vmem_limit_bytes=16 * 1024 * 1024),
        cost_estimate=light,
    )(*grads, act)


def product_of(grad, act):
    return lax.dot_general(grad, act, (((0,), (0,)), ((), ())), preferred_element_type=jnp.float32)


def finish(grads, act, grams, factors):
    layers, tile, cols = grams.shape

    def kernel(*refs):
        grad_refs, (act_ref, gram_ref, factor_ref, out_hbm, out_ref, sems) = refs[:layers], refs[layers:]
        copies = []
        for layer in range(layers):
            gram = gram_ref[layer] + product_of(grad_refs[layer][1], act_ref[layer])
            out_ref[layer] = (gram * factor_ref[layer]).astype(jnp.bfloat16)
            copies.append(pltpu.make_async_copy(out_ref.at[layer], out_hbm.at[layer], sems.at[layer]))
            copies[-1].start()
        for copy in copies:
            copy.wait()

    return pl.pallas_call(
        kernel,
        out_shape=jax.ShapeDtypeStruct((layers, tile, cols), jnp.bfloat16),
        in_specs=[vmem_spec] * (layers + 3),
        out_specs=pl.BlockSpec(memory_space=pl.ANY),
        scratch_shapes=[pltpu.VMEM((layers, tile, cols), jnp.bfloat16), pltpu.SemaphoreType.DMA((layers,))],
        compiler_params=pltpu.CompilerParams(vmem_limit_bytes=24 * 1024 * 1024),
        cost_estimate=light,
    )(*grads, act, grams, factors)


def eigenvalues(scalars, states, packets, n_dp):
    n_own = len(packets)
    layers, tile = packets[0].shape[0] // 2, packets[0].shape[1]
    slot_count, width = states[0].shape[0] // 2, states[0].shape[1]

    def kernel(scalar_ref, *refs):
        state_refs, packet_refs, refs = refs[:n_own], refs[n_own : 2 * n_own], refs[2 * n_own :]
        out_ref, new_act_ref, new_grad_ref, act_full, grad_full = refs
        dp, own = scalar_ref[0], scalar_ref[1]
        total = scalar_ref[2]
        for index in range(1, n_dp):
            total += scalar_ref[2 + index]
        total = total.astype(jnp.float32)
        owners = [scalar_ref[2 + n_dp + layer] for layer in range(layers)]
        for mask in range(n_own):
            at = pl.ds(pl.multiple_of((own ^ mask) * tile, tile), tile)
            act_full[:, at] = packet_refs[mask][:layers] / total
            at = pl.ds(pl.multiple_of((n_own - (own ^ mask)) % n_own * tile, tile), tile)
            grad_full[:, at] = packet_refs[mask][layers:] / total
        new_acts = [state_refs[0][slot : slot + 1] for slot in range(slot_count)]
        new_grads = [state_refs[0][slot_count + slot : slot_count + slot + 1] for slot in range(slot_count)]
        for layer in range(layers):
            owner_now = owners[layer]
            rank = jnp.int32(0)
            for earlier in range(layer):
                rank += jnp.where(owners[earlier] == owner_now, 1, 0)
            old_act = jnp.zeros((1, width), jnp.float32)
            old_grad = jnp.zeros((1, width), jnp.float32)
            for mask in range(n_own):
                for slot in range(slot_count):
                    here = (owner_now == own ^ mask) & (rank == slot)
                    down = slot_count + slot
                    old_act = jnp.where(here, state_refs[mask][slot : slot + 1], old_act)
                    old_grad = jnp.where(here, state_refs[mask][down : down + 1], old_grad)
            eigen_act = decay_rate * old_act + (1.0 - decay_rate) * act_full[layer : layer + 1]
            eigen_grad = decay_rate * old_grad + (1.0 - decay_rate) * grad_full[layer : layer + 1]
            act_full[layer : layer + 1] = eigen_act
            grad_full[layer : layer + 1] = eigen_grad
            for slot in range(slot_count):
                here = (owner_now == own) & (rank == slot)
                new_acts[slot] = jnp.where(here, eigen_act, new_acts[slot])
                new_grads[slot] = jnp.where(here, eigen_grad, new_grads[slot])

            damping = damping_rate * (jnp.sum(eigen_grad) / width) * (jnp.sum(eigen_act) / width)
            rows = grad_full[layer : layer + 1, pl.ds(pl.multiple_of(dp * tile, tile), tile)]
            cols = act_full[layer : layer + 1, pl.ds(pl.multiple_of(own * tile, tile), tile)]
            rows = jnp.transpose(jnp.broadcast_to(rows, (128, tile)))
            rows = jnp.concatenate([rows] * (tile // 128), axis=1)
            out_ref[layer] = 1.0 / (total * (rows * cols + damping))
        for slot in range(slot_count):
            new_act_ref[slot : slot + 1] = new_acts[slot]
            new_grad_ref[slot : slot + 1] = new_grads[slot]

    out_shape = [
        jax.ShapeDtypeStruct((layers, tile, tile), jnp.float32),
        jax.ShapeDtypeStruct((slot_count, width), jnp.float32),
        jax.ShapeDtypeStruct((slot_count, width), jnp.float32),
    ]
    return pl.pallas_call(
        kernel,
        out_shape=out_shape,
        in_specs=[scalar_spec] + [vmem_spec] * (2 * n_own),
        out_specs=[vmem_spec] * len(out_shape),
        scratch_shapes=[pltpu.VMEM((layers, width), jnp.float32)] * 2,
        compiler_params=pltpu.CompilerParams(vmem_limit_bytes=16 * 1024 * 1024),
        cost_estimate=light,
    )(scalars, *states, *packets)


def line_plan(activations, out_grads, basis_act, basis_grad, owner_of, counts, state_act, state_grad):
    layers, tok_rows, width = activations.shape
    tile = basis_act.shape[1]
    n_dp = lax.axis_size("dp")
    n_own = lax.axis_size("owner")
    dp = lax.axis_index("dp")
    own = lax.axis_index("owner")
    scalars = jnp.concatenate([jnp.stack([dp, own]), counts, owner_of]).astype(jnp.int32)

    def after(array, *others):
        return lax.optimization_barrier((array, *others))[0]

    def step(arrays, *others):
        return lax.optimization_barrier((*arrays, *others))[: len(arrays)]

    owners = range(n_own)
    held = [-o % n_own for o in owners]
    cuts = cut_rows((out_grads, activations), tile, n_own, n_dp)
    cuts = [flip(cut, "dp", number % (n_dp - 1) + 1) for number, cut in enumerate(cuts)]
    got_grad, got_act = cuts[: n_dp - 1], cuts[n_dp - 1 :]
    own_grad, stay_grad = load((out_grads, basis_grad), 1)
    pieces = got_grad[:-1] + [after(got_grad[-1], got_act[0], own_grad)]
    pieces += [flip(piece, "owner", 2) for piece in pieces]
    pieces += [flip(piece, "owner", 1) for piece in pieces]
    keep, send = project_rows(scalars, own_grad, pieces, stay_grad, n_own, n_dp)

    near = flip(after(send, *got_act), "dp", 1)
    pieces = [join(got_act[:-1]), got_act[-1]]
    pieces += [flip(after(piece, keep), "owner", 2) for piece in pieces]
    own_act, stay_act = load((activations, basis_act), 1, keep)
    pieces += [flip(after(piece, own_act), "owner", 1) for piece in pieces]
    keep_act, send_act = project_rows(scalars, own_act, pieces, stay_act, n_own, n_dp)

    state = jnp.concatenate([state_act, state_grad], axis=0)
    keep, near, keep_act, send_act, state = step([keep, near, keep_act, send_act, state])
    states = [state] + [flip(state, "owner", mask) for mask in range(1, n_own)]
    parts = add_rows(keep, near, keep.shape[1] * 7 // 12)
    parts = [lax.ppermute(array, "owner", [*enumerate(held)]) for array in parts]
    to_pair = [((a, o), (a ^ 2, o)) for a in range(n_dp) for o in owners if (a ^ held[o]) & 2]
    crosses = [hop(array, to_pair) for array in parts]
    near_act = flip(send_act, "dp", 1)

    crosses[0] = after(crosses[0], *states)
    nears = [add(pair) for pair in zip(parts, crosses, strict=True)]
    aside = ((dp ^ (-own % n_own)) // 2).astype(jnp.int32)[None]
    square_grad = squares_of(aside, nears)
    square_far = flip(square_grad, "dp", 2)
    fars = [hop(array, [((held[o] ^ 1, o), (held[o], o)) for o in owners]) for array in nears]
    full = by_layer(nears, fars)
    chip = [hop(array, [((held[o], o), (held[o], o ^ 2)) for o in owners]) for array in full]

    part_act = add((keep_act, near_act))
    cross_act = flip(part_act, "dp", 2)

    done = step([part_act, cross_act, square_grad, square_far, *full, *chip])
    (part_act, cross_act, square_grad, square_far), full, chip = done[:4], done[4:][:layers], done[4 + layers :]
    full_act, half = settle(part_act, cross_act, square_grad, square_far)
    other = flip(half, "dp", 1)
    back_act = flip(after(full_act, other), "dp", 1)
    packet = total_of(half, other)
    packets = [packet] + [flip(packet, "owner", mask) for mask in range(1, n_own)]
    source = -dp % n_own
    home = jnp.where(own == source, 0, jnp.where(own == source ^ 2, 1, 2)).astype(jnp.int32)[None]
    full = pick(after(home, *packets), [*zip(full, chip, strict=True)])
    to_core = [((held[o], o ^ b), (held[o], o ^ b ^ 1)) for o in owners for b in (0, 2)]
    core = [hop(array, to_core) for array in full]
    factors, new_act, new_grad = eigenvalues(scalars, states, packets, n_dp)
    grads = pick(home // 2, [*zip(full, core, strict=True)])
    grams = gram_of(grads, full_act)

    grams, factors, back_act, *grads = step([grams, factors, back_act, *grads])
    return finish(grads, back_act, grams, factors), new_act, new_grad


def solution(mesh):
    placed = (
        P("groups", "dp", None),
        P("groups", "dp", None),
        P("groups", "dp", "owner"),
        P("groups", "dp", "owner"),
        P(),
        P("groups"),
        P("owner", "groups"),
        P("owner", "groups"),
    )
    square = mesh.shape["dp"] == 4 and mesh.shape["owner"] == 4
    return jax.shard_map(
        line_plan if square else gather_plan,
        mesh=mesh,
        in_specs=placed,
        out_specs=(P("groups", "dp", "owner"), P("owner", "groups"), P("owner", "groups")),
        check_vma=False,
    )
```
